128 devices in a mesh: ctx: 8 (over y, core), exp: 16 (over x, z).
Axes of the slice: x: 4, y: 4, z: 4, core: 2. Of those that a mesh axis runs over, the one named last changes fastest.
Arguments:
- residual: bfloat16 [2048, 7168], P(('ctx', 'exp')), may hold values from -1.5 to 1.5
- queries: bfloat16 [2048, 24576], P('ctx', 'exp'), may hold values from -66 to 66
- latent: bfloat16 [2048, 512], P(('ctx', 'exp')), may hold values from -6 to 6
- key_rope: bfloat16 [2048, 64], P(('ctx', 'exp')), may hold values from -6 to 6
- doc_ids: int32 [2048], replicated, may hold values from 0 to 3, as said below
- kv_weight: bfloat16 [512, 32768], P(None, 'exp'), may hold values from -0.25 to 0.25
- out_weight: bfloat16 [16384, 7168], P('exp', 'ctx'), may hold values from -0.046875 to 0.046875
- norm_gain: float32 [7168], replicated, may hold values from 0.5 to 1.5
- expert_ids: int32 [2048, 8], P(('ctx', 'exp')), may hold values from 0 to 255, as said below
- expert_gates: float32 [2048, 8], P(('ctx', 'exp')), may hold values from 0.1 to 1
- w_gate: bfloat16 [16, 7168, 2048], P('exp', None, 'ctx'), may hold values from -0.0625 to 0.0625
- w_up: bfloat16 [16, 7168, 2048], P('exp', None, 'ctx'), may hold values from -0.0625 to 0.0625
- w_down: bfloat16 [16, 2048, 7168], P('exp', 'ctx'), may hold values from -0.125 to 0.125
Outputs:
- layer_out: bfloat16 [2048, 7168], P(('ctx', 'exp'))
The draws below stay inside these ranges and needn't reach their ends.
Inputs may be any that keep to these rules, and one draw needn't show every extreme that they name: `doc_ids`: ids never fall along the positions, begin at 0, change only at multiples of 16 positions, and every id from 0 to 3 occurs. `expert_ids`: each row names 8 different experts; in each aligned block of 16 rows (the rows of one device) no expert is named by more than 3 rows, and in every block one expert below 16 is named by exactly 3 rows.
All inputs are finite; a program needn't handle non-finite values.
Results may differ from the reference program's by a relative error of at most 0.02.
Values may be sent and summed in bfloat16 or wider, within the bound.
No kernel may reach another device: no remote copies, remote signals or barrier semaphores. Data moves between devices by JAX's collectives and lax.ppermute only.
A program may use at most 128 MiB of HBM per device.

```python
import jax
import jax.numpy as jnp
from jax import lax

D = 7168
HEADS = 128
NOPE = 128
ROPE = 64
VDIM = 128
LATENT = 512
EXPERTS = 256
TOPK = 8
FF = 2048
CAP = 3
TOK_DEV = 16
TOKENS = 2048
WIN = 16
N_CTX = 8
N_EXP = 16


def draw_queries(key, part):
    key = jax.random.fold_in(key, 11)
    first_key = jax.random.fold_in(key, 0)
    values = jnp.clip(jax.random.normal(first_key, (TOKENS, HEADS, NOPE + ROPE), jnp.float32), -6.0, 6.0)
    return values.reshape(TOKENS, HEADS * (NOPE + ROPE)).astype(jnp.bfloat16)


def draw_key_rope(key, part):
    key = jax.random.fold_in(key, 12)
    values = jnp.clip(jax.random.normal(key, (TOKENS, ROPE), jnp.float32), -6.0, 6.0)
    return values.astype(jnp.bfloat16)


def draw_doc_ids(key, part):
    key = jax.random.fold_in(key, 13)
    tiles = TOKENS // 16
    order = jax.random.permutation(key, tiles - 1) + 1
    starts = order[:3]
    tile_range = jnp.arange(tiles, dtype=jnp.int32)
    marks = jnp.any(tile_range[:, None] == starts[None, :], axis=1)
    tile_ids = jnp.cumsum(marks.astype(jnp.int32))
    return jnp.repeat(tile_ids, 16).astype(jnp.int32)


def shuffled_rows(subkey):
    return jax.random.permutation(subkey, TOK_DEV)


def shuffled_others(subkey):
    return jax.random.permutation(subkey, EXPERTS - 1)


def draw_expert_ids(key, part):
    key = jax.random.fold_in(key, 14)
    key_list = jax.random.split(key, 6)
    blocks = TOKENS // TOK_DEV
    pick_count = TOK_DEV * TOPK
    pool_least = (pick_count + 2) // 3
    narrow_top = min(max(pool_least + 1, (pick_count + 1) // 2), EXPERTS)
    hot_expert = jax.random.randint(key_list[0], (blocks,), 0, WIN).astype(jnp.int32)
    hot_expert = hot_expert.at[0].set(0)
    narrow_flag = jax.random.randint(key_list[3], (blocks,), 0, 2)
    pool_narrow = jax.random.randint(key_list[4], (blocks,), pool_least, narrow_top)
    pool_wide = jax.random.randint(key_list[5], (blocks,), pool_least, EXPERTS)
    pool_size = jnp.where(narrow_flag == 1, pool_narrow, pool_wide).astype(jnp.int32)
    row_rank = jax.vmap(shuffled_rows)(jax.random.split(key_list[1], blocks))
    hot_row = row_rank < CAP
    orders = jax.vmap(shuffled_others)(jax.random.split(key_list[2], blocks)).astype(jnp.int32)
    slot_range = jnp.arange(EXPERTS - 1, dtype=jnp.int32)
    first_order = orders[0]
    top_place = jnp.sum(jnp.where(first_order == EXPERTS - 2, slot_range, 0))
    moved = jnp.where(slot_range == top_place, first_order[1], first_order)
    moved = jnp.where(slot_range == 1, EXPERTS - 2, moved)
    orders = orders.at[0].set(moved)
    local_rows = jnp.arange(TOK_DEV, dtype=jnp.int32)
    place = local_rows[:, None] * TOPK + jnp.arange(TOPK, dtype=jnp.int32)[None, :]
    place = place[None, :, :] % pool_size[:, None, None]
    chosen = jnp.take_along_axis(orders, place.reshape(blocks, pick_count), axis=1)
    chosen = chosen.reshape(blocks, TOK_DEV, TOPK)
    chosen = chosen + (chosen >= hot_expert[:, None, None]).astype(jnp.int32)
    first_slot = jnp.where(hot_row, hot_expert[:, None], chosen[:, :, 0])
    chosen = chosen.at[:, :, 0].set(first_slot)
    return chosen.reshape(TOKENS, TOPK).astype(jnp.int32)


def block_levels(key, shape, pieces, least, top_value):
    def one(dim, blocks):
        steps = jax.random.uniform(jax.random.fold_in(jax.random.fold_in(key, 6), dim), (blocks,), jnp.float32, least / len(pieces), top_value / len(pieces))
        return jnp.repeat(jnp.exp(steps), shape[dim] // blocks).reshape((-1,) + (1,) * (len(shape) - dim - 1))

    gain = one(*pieces[0])
    for cut in pieces[1:]:
        gain = gain * one(*cut)
    return gain


def bell_draw(rng, shape, scale, bound, shards=(), held_as=jnp.bfloat16):
    entries = scale * jax.random.normal(rng, shape, jnp.float32)
    if shards:
        entries = entries * block_levels(rng, shape, shards, -0.22, 0.18)
    return jnp.clip(entries, -bound, bound).astype(held_as)


def setup_inputs(seed: int = 0) -> dict:
    arg_keys = jax.random.split(jax.random.key(seed), 14)
    return {
        "residual": bell_draw(arg_keys[0], (TOKENS, D), 0.25, 1.5, ((0, 128),)),
        "queries": draw_queries(jax.random.fold_in(arg_keys[13], 71), 0),
        "latent": bell_draw(arg_keys[2], (TOKENS, LATENT), 1.0, 6.0, ((0, 128),)),
        "key_rope": draw_key_rope(jax.random.fold_in(arg_keys[13], 71), 0),
        "doc_ids": draw_doc_ids(jax.random.fold_in(arg_keys[13], 71), 0),
        "kv_weight": bell_draw(arg_keys[5], (LATENT, HEADS * (NOPE + VDIM)), LATENT ** -0.5, 0.25, ((1, 16),)),
        "out_weight": bell_draw(arg_keys[6], (HEADS * VDIM, D), (HEADS * VDIM) ** -0.5, 0.046875, ((0, 16), (1, 8))),
        "norm_gain": jnp.clip(1.0 + 0.1 * jax.random.normal(arg_keys[7], (D,), jnp.float32), 0.5, 1.5),
        "expert_ids": draw_expert_ids(jax.random.fold_in(arg_keys[13], 71), 0),
        "expert_gates": jnp.clip(0.1 + 0.9 * jax.random.uniform(arg_keys[9], (TOKENS, TOPK), jnp.float32) ** block_levels(arg_keys[9], (TOKENS, TOPK), ((0, 128),), -0.2, 0.2), 0.1, 1.0),
        "w_gate": bell_draw(arg_keys[10], (WIN, D, FF), D ** -0.5, 0.0625, ((0, 16), (2, 8))),
        "w_up": bell_draw(arg_keys[11], (WIN, D, FF), D ** -0.5, 0.0625, ((0, 16), (2, 8))),
        "w_down": bell_draw(arg_keys[12], (WIN, FF, D), FF ** -0.5, 0.125, ((0, 16), (1, 8))),
    }


NEG_FILL = -1e+30
EPSILON = 1e-06

def head_attention(head_query, head_weight, latent, key_rope, doc_ids):
    kv_pairs = jnp.dot(latent, head_weight, preferred_element_type=jnp.float32).astype(jnp.bfloat16)
    key_nope = kv_pairs[:, :NOPE]
    head_values = kv_pairs[:, NOPE:]
    scores = jnp.dot(head_query[:, :NOPE], key_nope.T, preferred_element_type=jnp.float32)
    scores = scores + jnp.dot(head_query[:, NOPE:], key_rope.T, preferred_element_type=jnp.float32)
    scores = scores * (NOPE + ROPE) ** (-0.5)
    positions = jnp.arange(TOKENS, dtype=jnp.int32)
    allowed = (doc_ids[:, None] == doc_ids[None, :]) & (positions[None, :] <= positions[:, None])
    scores = jnp.where(allowed, scores, NEG_FILL)
    row_peak = lax.optimization_barrier(jnp.max(scores, axis=1, keepdims=True))
    weights = jnp.exp(scores - row_peak)
    probs = (weights / lax.optimization_barrier(jnp.sum(weights, axis=1, keepdims=True))).astype(jnp.bfloat16)
    return jnp.dot(probs, head_values, preferred_element_type=jnp.float32).astype(jnp.bfloat16)

def expert_rows(normed, gate_w, up_w, down_w, row_index):
    picked = normed[row_index]
    gate_val = jnp.dot(picked, gate_w, preferred_element_type=jnp.float32)
    up_val = jnp.dot(picked, up_w, preferred_element_type=jnp.float32)
    hidden = (jax.nn.silu(gate_val) * up_val).astype(jnp.bfloat16)
    slice_width = FF // N_CTX
    total_sum = jnp.zeros((row_index.shape[0], D), jnp.float32)
    for part_index in range(N_CTX):
        lower = part_index * slice_width
        term = jnp.dot(hidden[:, lower:lower + slice_width], down_w[lower:lower + slice_width], preferred_element_type=jnp.float32).astype(jnp.bfloat16)
        term = lax.optimization_barrier(term)
        total_sum = total_sum + term.astype(jnp.float32)
    return total_sum.astype(jnp.bfloat16)

def reference(residual, queries, latent, key_rope, doc_ids, kv_weight, out_weight, norm_gain, expert_ids, expert_gates, w_gate, w_up, w_down):
    query_heads = queries.reshape(TOKENS, HEADS, NOPE + ROPE).transpose(1, 0, 2)
    weight_heads = kv_weight.reshape(LATENT, HEADS, NOPE + VDIM).transpose(1, 0, 2)

    def one_head(operands):
        return head_attention(operands[0], operands[1], latent, key_rope, doc_ids)
    head_out = lax.map(one_head, (query_heads, weight_heads))
    head_out = head_out.transpose(1, 0, 2).reshape(TOKENS, HEADS * VDIM)
    group_cols = HEADS // N_EXP * VDIM

    def add_group(group, total_sum):
        head_cols = lax.dynamic_slice_in_dim(head_out, group * group_cols, group_cols, 1)
        weight_rows = lax.dynamic_slice_in_dim(out_weight, group * group_cols, group_cols, 0)
        part_sum = jnp.dot(head_cols, weight_rows, preferred_element_type=jnp.float32).astype(jnp.bfloat16)
        part_sum = lax.optimization_barrier(part_sum)
        return total_sum + part_sum.astype(jnp.float32)
    attn_proj = lax.fori_loop(0, N_EXP, add_group, jnp.zeros((TOKENS, D), jnp.float32))
    stream = residual.astype(jnp.float32) + attn_proj
    mean_square = lax.optimization_barrier(jnp.mean(stream * stream, axis=1, keepdims=True))
    normed = (stream * lax.rsqrt(mean_square + EPSILON) * norm_gain).astype(jnp.bfloat16)
    row_limit = CAP * N_CTX * N_EXP

    def add_expert(expert, total_sum):
        hits = expert_ids == expert
        chosen = jnp.any(hits, axis=1)
        route_weight = lax.optimization_barrier(jnp.sum(jnp.where(hits, expert_gates, 0.0), axis=1))
        row_index = jnp.nonzero(chosen, size=row_limit, fill_value=0)[0].astype(jnp.int32)
        live_rows = jnp.arange(row_limit, dtype=jnp.int32) < jnp.sum(chosen.astype(jnp.int32))
        expert_out = expert_rows(normed, w_gate[expert], w_up[expert], w_down[expert], row_index).astype(jnp.float32)
        scaled = jnp.where(live_rows[:, None], route_weight[row_index][:, None] * expert_out, 0.0)
        return total_sum.at[row_index].add(scaled)
    routed = lax.fori_loop(0, WIN, add_expert, jnp.zeros((TOKENS, D), jnp.float32))
    return (stream + routed).astype(jnp.bfloat16)
```

```python
import functools
import math

import jax
import jax.numpy as jnp
from jax import lax
from jax.experimental import pallas as pl
from jax.experimental.pallas import tpu as pltpu
from jax.sharding import PartitionSpec as P

NOPE = 128
ROPE = 64
VDIM = 128
LATENT = 512
CAP = 3
D = 7168
EPSILON = 1e-06
HEADS_HERE = 8
ROWS = 256
KEYS = 2048
BLK = 16
SEG = 896
NEG_FILL = -1e30
F32 = jnp.float32
BF16 = jnp.bfloat16
MIB = 1024 * 1024


def params(mib):
    return pltpu.CompilerParams(vmem_limit_bytes=mib * MIB)


def whole(shape):
    zeros = (0,) * len(shape)
    return pl.BlockSpec(shape, lambda *_: zeros)


def swap_ctx(value, bits):
    return lax.ppermute(value, "ctx", [(i, i ^ bits) for i in range(8)])


def swap_exp(value, bits):
    return lax.ppermute(value, "exp", [(i, i ^ bits) for i in range(16)])


KEY_STEP = 512


def attention_kernel(q_ref, near_ref, far_ref, w_ref, kpos_ref, qpos_ref, qlo_ref, out_ref,
                     bias, keys, values, scores):
    half = KEYS // 2

    @pl.when(pl.program_id(0) == 0)
    def _():
        kpos = kpos_ref[...]
        allowed = (kpos <= qpos_ref[...]) & (kpos >= qlo_ref[...])
        bias[...] = jnp.where(allowed, 0.0, NEG_FILL)
        keys[:half, NOPE:] = near_ref[:, LATENT:]
        keys[half:, NOPE:] = far_ref[:, LATENT:]

    for step in range(KEYS // KEY_STEP):
        rows = slice(step * KEY_STEP, (step + 1) * KEY_STEP)
        if step * KEY_STEP < half:
            lat = near_ref[rows, :LATENT]
        else:
            lat = far_ref[step * KEY_STEP - half:(step + 1) * KEY_STEP - half, :LATENT]
        pair = jnp.dot(lat, w_ref[...], preferred_element_type=F32).astype(BF16)
        keys[rows, :NOPE] = pair[:, :NOPE]
        values[rows, :] = pair[:, NOPE:]
    log2e = 1.4426950408889634
    factor = (NOPE + ROPE) ** (-0.5) * log2e
    query = q_ref[0]
    peak = None
    for step in range(KEYS // KEY_STEP):
        rows = slice(step * KEY_STEP, (step + 1) * KEY_STEP)
        part = lax.dot_general(query, keys[rows, :], (((1,), (1,)), ((), ())),
                               preferred_element_type=F32)
        part = part * factor + bias[:, rows]
        scores[:, rows] = part
        top = jnp.max(part, axis=1, keepdims=True)
        peak = top if peak is None else jnp.maximum(peak, top)
    total = jnp.zeros((ROWS, 1), F32)
    out = jnp.zeros((ROWS, VDIM), F32)
    for step in range(KEYS // KEY_STEP):
        rows = slice(step * KEY_STEP, (step + 1) * KEY_STEP)
        weight = jnp.exp2(scores[:, rows] - peak)
        total = total + jnp.sum(weight, axis=1, keepdims=True)
        out = out + jnp.dot(weight.astype(BF16), values[rows, :], preferred_element_type=F32)
    out_ref[...] = (out / total).astype(BF16)


def attention(query, near, far, weight, kpos, qpos, qlo):
    return pl.pallas_call(
        attention_kernel,
        grid=(HEADS_HERE,),
        in_specs=[
            pl.BlockSpec((1, ROWS, NOPE + ROPE), lambda h: (h, 0, 0)),
            whole(near.shape),
            whole(far.shape),
            pl.BlockSpec((LATENT, NOPE + VDIM), lambda h: (0, h)),
            whole(kpos.shape),
            whole(qpos.shape),
            whole(qlo.shape),
        ],
        out_specs=pl.BlockSpec((ROWS, VDIM), lambda h: (0, h)),
        out_shape=jax.ShapeDtypeStruct((ROWS, HEADS_HERE * VDIM), BF16),
        scratch_shapes=[
            pltpu.VMEM((ROWS, KEYS), F32),
            pltpu.VMEM((KEYS, NOPE + ROPE), BF16),
            pltpu.VMEM((KEYS, VDIM), BF16),
            pltpu.VMEM((ROWS, KEYS), F32),
        ],
        compiler_params=params(32),
        cost_estimate=pl.CostEstimate(flops=7_000_000_000, bytes_accessed=8_000_000, transcendentals=4_200_000),
        name="attention",
    )(query, near, far, weight, kpos, qpos, qlo)


def project_kernel(index_ref, heads_ref, w0, w1, w2, w3, a0, a1, a2, a3, b0, b1, b2, b3,
                   rows_a, rows_b, weights, sems):
    sources = (w0, w1, w2, w3)
    copies = [pltpu.make_async_copy(sources[i], weights.at[i], sems.at[i]) for i in range(4)]
    for copy in copies:
        copy.start()
    x, z = index_ref[0], index_ref[1]
    for m in range(4):
        first = pl.multiple_of((x ^ m) * 64, 64)
        rows_a[m * 64:(m + 1) * 64, :] = heads_ref[pl.ds(first, 64), :]
        for n in range(4):
            first = pl.multiple_of(n * 64 + (z ^ m) * 16, 16)
            rows_b[m * 64 + n * 16:m * 64 + n * 16 + 16, :] = heads_ref[pl.ds(first, 16), :]
    for i in range(4):
        copies[i].wait()
        left = rows_a if i < 2 else rows_b
        outs = (a0, a1, a2, a3) if i < 2 else (b0, b1, b2, b3)
        cols = slice((i % 2) * SEG, (i % 2 + 1) * SEG)
        part = jnp.dot(left[...], weights[i], preferred_element_type=F32).astype(BF16)
        for m in range(4):
            outs[m][:, cols] = part[m * 64:(m + 1) * 64, :]


def project(index, heads, weights):
    piece = jax.ShapeDtypeStruct((64, 2 * SEG), BF16)
    return pl.pallas_call(
        project_kernel,
        grid_spec=pltpu.PrefetchScalarGridSpec(
            num_scalar_prefetch=1,
            grid=(1,),
            in_specs=[whole(heads.shape)] + [pl.BlockSpec(memory_space=pl.ANY)] * 4,
            out_specs=[whole(piece.shape)] * 8,
            scratch_shapes=[
                pltpu.VMEM(heads.shape, BF16),
                pltpu.VMEM(heads.shape, BF16),
                pltpu.VMEM((4, 1024, SEG), BF16),
                pltpu.SemaphoreType.DMA((4,)),
            ],
        ),
        out_shape=[piece] * 8,
        compiler_params=params(32),
        cost_estimate=pl.CostEstimate(flops=1_900_000_000, bytes_accessed=9_000_000, transcendentals=0),
        name="project",
    )(index, heads, *weights)


def first_sum_kernel(index_ref, *refs):
    ins, outs = refs[:16], refs[16:]
    for side in range(2):
        spot = index_ref[1 - side]
        for m in range(4):
            first = pl.multiple_of((spot ^ m) * 16, 16)
            for block in range(2):
                group = ins[side * 8 + block * 4:side * 8 + block * 4 + 4]
                total = group[0][pl.ds(first, 16), :].astype(F32)
                for ref in group[1:]:
                    total = total + ref[pl.ds(first, 16), :].astype(F32)
                outs[side * 4 + m][block * 16:(block + 1) * 16, :] = total.astype(BF16)


def first_sum(index, pieces):
    out = jax.ShapeDtypeStruct((32, 2 * SEG), BF16)
    return pl.pallas_call(
        first_sum_kernel,
        grid_spec=pltpu.PrefetchScalarGridSpec(
            num_scalar_prefetch=1,
            grid=(1,),
            in_specs=[whole((64, 2 * SEG))] * 16,
            out_specs=[whole(out.shape)] * 8,
        ),
        out_shape=[out] * 8,
        compiler_params=params(24),
        cost_estimate=pl.CostEstimate(flops=2_000_000, bytes_accessed=4_600_000, transcendentals=0),
        name="first_sum",
    )(index, *pieces)


def stream_kernel(index_ref, *refs):
    sums, (own_res, far_res, gain, place, stream_own, stream_far, send, stack) = refs[:8], refs[8:]
    spot = index_ref[2]
    for i in range(4):
        seg = spot ^ i
        cols = slice((i % 2) * SEG, (i % 2 + 1) * SEG)
        group = sums[(i // 2) * 4:(i // 2) * 4 + 4]
        total = group[0][:, cols].astype(F32)
        for ref in group[1:]:
            total = total + ref[:, cols].astype(F32)
        own = total[:16] + own_res[seg].astype(F32)
        far = total[16:] + far_res[seg].astype(F32)
        stream_own[seg] = own
        stream_far[seg] = far
        scaled = gain[seg]
        stack[pl.ds(pl.multiple_of(seg * 32, 32), 16), :] = (own * scaled).astype(BF16)
        stack[pl.ds(pl.multiple_of(seg * 32 + 16, 16), 16), :] = (far * scaled).astype(BF16)
    send[...] = jnp.dot(place[...], stack[...], preferred_element_type=F32).astype(BF16)


def make_stream(index, sums, own_res, far_res, gain, place):
    return pl.pallas_call(
        stream_kernel,
        grid_spec=pltpu.PrefetchScalarGridSpec(
            num_scalar_prefetch=1,
            grid=(1,),
            in_specs=[whole(v.shape) for v in (*sums, own_res, far_res, gain, place)],
            out_specs=[whole((4, 16, SEG))] * 2 + [whole((384, SEG))],
            scratch_shapes=[pltpu.VMEM((128, SEG), BF16)],
        ),
        out_shape=[jax.ShapeDtypeStruct((4, 16, SEG), F32)] * 2
        + [jax.ShapeDtypeStruct((384, SEG), BF16)],
        compiler_params=params(24),
        cost_estimate=pl.CostEstimate(flops=90_000_000, bytes_accessed=3_000_000, transcendentals=0),
        name="make_stream",
    )(index, *sums, own_res, far_res, gain, place)


def pick_rows(order):
    import numpy as np

    matrix = np.zeros((4, 96, 384), np.float32)
    for q in range(4):
        for block in range(2):
            for e in range(16):
                for s in range(CAP):
                    matrix[q, block * 48 + e * 3 + s, e * 24 + q * 6 + order[block] * 3 + s] = 1.0
    return jnp.asarray(matrix, BF16)


def up_step(pick_ref, x0, x1, gain_ref, weights, gate_up, squares):
    rows = [jnp.dot(pick_ref[0], x[...], preferred_element_type=F32) for x in (x0, x1)]
    rows = jnp.concatenate(rows, axis=0)
    plain = rows / gain_ref[0]
    squares[...] += jnp.sum(plain * plain, axis=1, keepdims=True)
    rows = rows.astype(BF16)
    for i, ref in enumerate(weights):
        cols = slice(i * 256, (i + 1) * 256)
        gate_up[:, cols] += jnp.dot(rows, ref[...], preferred_element_type=F32)


def expert_first_kernel(index_ref, x0, x1, pick_ref, gain_ref, g0, g1, u0, u1, gate_up, squares):
    @pl.when(pl.program_id(0) == 0)
    def _():
        gate_up[...] = jnp.zeros_like(gate_up)
        squares[...] = jnp.zeros_like(squares)

    up_step(pick_ref, x0, x1, gain_ref, (g0, g1, u0, u1), gate_up, squares)


def expert_first(index, x0, x1, pick, gain, weights):
    spec = pl.BlockSpec((SEG, 256), lambda q, index_ref: (index_ref[3] * 4 + q, 0))
    return pl.pallas_call(
        expert_first_kernel,
        grid_spec=pltpu.PrefetchScalarGridSpec(
            num_scalar_prefetch=1,
            grid=(4,),
            in_specs=[
                whole(x0.shape),
                whole(x1.shape),
                pl.BlockSpec((1, 96, 384), lambda q, index_ref: (q, 0, 0)),
                pl.BlockSpec((1, 1, SEG), lambda q, index_ref: (index_ref[3] * 4 + q, 0, 0)),
            ] + [spec] * 4,
            out_specs=[whole((192, 1024)), whole((192, 1))],
        ),
        out_shape=[jax.ShapeDtypeStruct((192, 1024), F32), jax.ShapeDtypeStruct((192, 1), F32)],
        compiler_params=params(24),
        cost_estimate=pl.CostEstimate(flops=1_700_000_000, bytes_accessed=9_500_000, transcendentals=0),
        name="expert_first",
    )(index, x0, x1, pick, gain, *weights)


def expert_last_kernel(index_ref, x0, x1, pick_ref, gain_ref, g0, g1, u0, u1, d0, d1, before, squares_before,
                       r0, r1, r2, r3, gate_up, squares, hidden):
    step = pl.program_id(0)

    @pl.when(step == 0)
    def _():
        gate_up[...] = before[...]
        squares[...] = squares_before[...]

    @pl.when(step < 4)
    def _():
        up_step(pick_ref, x0, x1, gain_ref, (g0, g1, u0, u1), gate_up, squares)

    @pl.when(step == 3)
    def _():
        scale = lax.rsqrt(squares[...] * (1.0 / D) + EPSILON)
        gate = gate_up[:, :512] * scale
        up = gate_up[:, 512:] * scale
        hidden[...] = (gate / (1.0 + jnp.exp(-gate)) * up).astype(BF16)

    @pl.when(step >= 4)
    def _():
        out = jnp.dot(hidden[:, :256], d0[...], preferred_element_type=F32)
        out = out + jnp.dot(hidden[:, 256:], d1[...], preferred_element_type=F32)
        out = out.astype(BF16)
        for i, ref in enumerate((r0, r1, r2, r3)):
            ref[...] = out[i * 48:(i + 1) * 48]


def expert_last(index, x0, x1, pick, gain, weights, downs, before, squares_before):
    up_spec = pl.BlockSpec(
        (SEG, 256), lambda q, index_ref: ((1 - index_ref[3]) * 4 + jnp.minimum(q, 3), 0)
    )
    down_spec = pl.BlockSpec((256, 2 * SEG), lambda q, index_ref: (0, jnp.maximum(q - 4, 0)))
    out_spec = pl.BlockSpec((48, 2 * SEG), lambda q, index_ref: (0, jnp.maximum(q - 4, 0)))
    return pl.pallas_call(
        expert_last_kernel,
        grid_spec=pltpu.PrefetchScalarGridSpec(
            num_scalar_prefetch=1,
            grid=(8,),
            in_specs=[
                whole(x0.shape),
                whole(x1.shape),
                pl.BlockSpec((1, 96, 384), lambda q, index_ref: (jnp.minimum(q, 3), 0, 0)),
                pl.BlockSpec(
                    (1, 1, SEG), lambda q, index_ref: ((1 - index_ref[3]) * 4 + jnp.minimum(q, 3), 0, 0)
                ),
            ] + [up_spec] * 4 + [down_spec] * 2 + [whole((192, 1024)), whole((192, 1))],
            out_specs=[out_spec] * 4,
            scratch_shapes=[
                pltpu.VMEM((192, 1024), F32),
                pltpu.VMEM((192, 1), F32),
                pltpu.VMEM((192, 512), BF16),
            ],
        ),
        out_shape=[jax.ShapeDtypeStruct((48, D), BF16)] * 4,
        compiler_params=params(32),
        cost_estimate=pl.CostEstimate(flops=3_200_000_000, bytes_accessed=21_000_000, transcendentals=100_000),
        name="expert_last",
    )(index, x0, x1, pick, gain, *weights, *downs, before, squares_before)


def spread_kernel(p0, p1, p2, p3, out):
    total = p0[...].astype(F32)
    for ref in (p1, p2, p3):
        total = total + ref[...].astype(F32)
    total = total.astype(BF16)
    stack = jnp.concatenate([total[:, q * SEG:(q + 1) * SEG] for q in range(8)], axis=0)
    row = lax.broadcasted_iota(jnp.int32, (384, 384), 0)
    col = lax.broadcasted_iota(jnp.int32, (384, 384), 1)
    move = (row == (col % 48) * 8 + col // 48).astype(BF16)
    out[...] = jnp.dot(move, stack, preferred_element_type=F32).astype(BF16)


def spread(parts):
    return pl.pallas_call(
        spread_kernel,
        out_shape=jax.ShapeDtypeStruct((384, SEG), BF16),
        compiler_params=params(24),
        cost_estimate=pl.CostEstimate(flops=260_000_000, bytes_accessed=3_500_000, transcendentals=0),
        name="spread",
    )(*parts)


def combine_kernel(index_ref, rows, weight, stream_own, stream_far, out, routed):
    total = jnp.dot(weight[0], rows[...], preferred_element_type=F32)
    for i in (1, 2):
        total = total + jnp.dot(weight[i], rows[...], preferred_element_type=F32)
    routed[...] = total
    pair = index_ref[3]
    for q in range(4):
        for side, stream in ((pair, stream_own), (1 - pair, stream_far)):
            seg = side * 4 + q
            picked = routed[pl.ds(pl.multiple_of(seg * 16, 16), 16), :]
            out[:, pl.ds(pl.multiple_of(seg * SEG, 128), SEG)] = (picked + stream[q]).astype(BF16)


def combine(index, rows, weight, stream_own, stream_far):
    return pl.pallas_call(
        combine_kernel,
        grid_spec=pltpu.PrefetchScalarGridSpec(
            num_scalar_prefetch=1,
            grid=(1,),
            in_specs=[whole(v.shape) for v in (rows, weight, stream_own, stream_far)],
            out_specs=whole((16, D)),
            scratch_shapes=[pltpu.VMEM((128, SEG), F32)],
        ),
        out_shape=jax.ShapeDtypeStruct((16, D), BF16),
        compiler_params=params(24),
        cost_estimate=pl.CostEstimate(flops=270_000_000, bytes_accessed=1_800_000, transcendentals=0),
        name="combine",
    )(index, rows, weight, stream_own, stream_far)


def three_parts(value):
    first = lax.reduce_precision(value, 8, 7)
    second = lax.reduce_precision(value - first, 8, 7)
    third = value - first - second
    return jnp.stack([first, second, third]).astype(BF16)


def slots_of(expert_ids):
    matches = expert_ids[:, :, None] == jnp.arange(16, dtype=jnp.int32)[None, None, :]
    named = jnp.any(matches, axis=1)
    slot = jnp.cumsum(named.astype(jnp.int32), axis=0) - 1
    placed = named[:, :, None] & (slot[:, :, None] == jnp.arange(CAP, dtype=jnp.int32))
    return matches, placed


def per_device(residual, queries, latent, key_rope, doc_ids, kv_weight, out_weight, norm_gain,
               expert_ids, expert_gates, w_gate, w_up, w_down):
    c = lax.axis_index("ctx")
    e = lax.axis_index("exp")
    y, k, x, z = c // 2, c % 2, e // 4, e % 4
    pair = y // 2
    index = jnp.stack([x, z, c % 4, pair]).astype(jnp.int32)

    lat = jnp.concatenate([latent, key_rope], axis=1)
    lat = jnp.concatenate([lat] + [swap_ctx(lat, 2 * m) for m in (1, 2, 3)], axis=0)
    lat = jnp.concatenate([lat] + [swap_exp(lat, m) for m in (1, 2, 3)], axis=0)
    near = jnp.concatenate([lat] + [swap_exp(lat, 4 * m) for m in (1, 2, 3)], axis=0)
    far = swap_ctx(near, 1)

    out_own = out_weight
    out_core = swap_ctx(out_own, 1)
    out_next = swap_ctx(out_own, 2)
    out_both = swap_ctx(out_next, 1)
    out_weights = (out_own, out_core, out_next, out_both)

    spot = jnp.arange(KEYS, dtype=jnp.int32)
    my, mz, mx, mk = (spot // 16) % 4, (spot // 64) % 4, (spot // 256) % 4, spot // 1024
    key_block = ((y ^ my) * 2 + (k ^ mk)) * 16 + (x ^ mx) * 4 + (z ^ mz)
    kpos = (key_block * 16 + spot % 16).reshape(1, KEYS).astype(jnp.int32)
    qpos = (c * ROWS + jnp.arange(ROWS, dtype=jnp.int32)).reshape(ROWS, 1)
    own_docs = lax.dynamic_slice_in_dim(doc_ids, c * ROWS, ROWS, 0)
    qlo = jnp.sum((doc_ids[None, :] < own_docs[:, None]).astype(jnp.int32), axis=1, keepdims=True)
    query = queries.reshape(ROWS, HEADS_HERE, NOPE + ROPE).transpose(1, 0, 2)

    res = residual.reshape(BLK, 8, SEG).transpose(1, 0, 2)
    own_res = lax.dynamic_slice_in_dim(res, pair * 4, 4, 0)
    far_res = swap_ctx(lax.dynamic_slice_in_dim(res, (1 - pair) * 4, 4, 0), 6)
    gain_rows = norm_gain.reshape(8, 1, SEG)
    own_gain = lax.dynamic_slice_in_dim(gain_rows, pair * 4, 4, 0)

    far_ids = swap_ctx(expert_ids, 6)
    matches, placed = slots_of(expert_ids)
    _, far_placed = slots_of(far_ids)
    both = jnp.stack([placed, far_placed]).astype(BF16)
    place = jnp.einsum(
        "btjs,qr,bd->jqbsrdt", both, jnp.eye(4, dtype=BF16), jnp.eye(2, dtype=BF16)
    ).reshape(384, 128)
    route = jnp.sum(jnp.where(matches, expert_gates[:, :, None], 0.0), axis=1)
    slot_weight = jnp.where(placed, route[:, :, None], 0.0)
    weight = slot_weight.reshape(1, BLK, 48, 1) * jnp.eye(8, dtype=F32)[:, None, None, :]
    weight = three_parts(weight.reshape(128, 384))

    heads = attention(query, near, far, kv_weight, kpos, qpos, qlo)

    gate, up, down = w_gate[0], w_up[0], w_down[0]
    gate_in, up_in, down_in, _ = lax.optimization_barrier((gate, up, down, far))
    gate_far = swap_ctx(gate_in, 1)
    up_far = swap_ctx(up_in, 1)
    down_far = swap_ctx(down_in, 1)

    heads_far = swap_ctx(heads, 6)
    own_pieces = project(index, heads, out_weights)
    far_pieces = project(index, heads_far, out_weights)
    own_a = [own_pieces[0]] + [swap_exp(own_pieces[m], 4 * m) for m in (1, 2, 3)]
    own_b = [own_pieces[4]] + [swap_exp(own_pieces[4 + m], m) for m in (1, 2, 3)]
    far_a = [far_pieces[0]] + [swap_exp(far_pieces[m], 4 * m) for m in (1, 2, 3)]
    far_b = [far_pieces[4]] + [swap_exp(far_pieces[4 + m], m) for m in (1, 2, 3)]
    sums = first_sum(index, own_a + far_a + own_b + far_b)
    sum_a = [sums[0]] + [swap_exp(sums[m], m) for m in (1, 2, 3)]
    sum_b = [sums[4]] + [swap_exp(sums[4 + m], 4 * m) for m in (1, 2, 3)]
    stream_own, stream_far, send = make_stream(index, sum_a + sum_b, own_res, far_res, own_gain, place)

    got = lax.all_to_all(send.reshape(16, 24, SEG), "exp", split_axis=0, concat_axis=0, tiled=True)
    got = got.reshape(384, SEG)
    stream_far = swap_ctx(stream_far, 6)
    got_1, got_3, got_2 = swap_ctx(got, 2), swap_ctx(got, 6), swap_ctx(got, 4)
    ups = (gate, gate_far, up, up_far)
    gate_up, squares = expert_first(index, got, got_1, pick_rows((0, 1)), gain_rows, ups)
    r0, r3, r1, r2 = expert_last(
        index, got_3, got_2, pick_rows((1, 0)), gain_rows, ups, (down, down_far), gate_up, squares
    )
    back = spread([r0, swap_ctx(r1, 2), swap_ctx(r3, 6), swap_ctx(r2, 4)])
    rows = lax.all_to_all(back.reshape(16, 24, SEG), "exp", split_axis=0, concat_axis=0, tiled=True)
    return combine(index, rows.reshape(384, SEG), weight, stream_own, stream_far)


def solution(mesh):
    placed = (
        P(("ctx", "exp"), None),
        P("ctx", "exp"),
        P(("ctx", "exp"), None),
        P(("ctx", "exp"), None),
        P(),
        P(None, "exp"),
        P("exp", "ctx"),
        P(),
        P(("ctx", "exp"), None),
        P(("ctx", "exp"), None),
        P("exp", None, "ctx"),
        P("exp", None, "ctx"),
        P("exp", "ctx", None),
    )
    return jax.shard_map(
        per_device, mesh=mesh, in_specs=placed, out_specs=P(("ctx", "exp"), None), check_vma=False
    )
```

```python
import functools

import jax
import jax.numpy as jnp
import numpy as np
from jax import lax
from jax.experimental import pallas as pl
from jax.experimental.pallas import tpu as pltpu
from jax.sharding import PartitionSpec as P

NOPE = 128
ROPE = 64
VDIM = 128
LATENT = 512
CAP = 3
D = 7168
EPSILON = 1e-06
HEADS_HERE = 8
ROWS = 256
KEYS = 2048
BLK = 16
SEG = 896
NEG_FILL = -1e30
F32 = jnp.float32
BF16 = jnp.bfloat16
MIB = 1024 * 1024


def params(mib):
    return pltpu.CompilerParams(vmem_limit_bytes=mib * MIB)


def whole(shape):
    zeros = (0,) * len(shape)
    return pl.BlockSpec(shape, lambda *_: zeros)


def swap_ctx(value, bits):
    return lax.ppermute(value, "ctx", [(i, i ^ bits) for i in range(8)])


def swap_exp(value, bits):
    return lax.ppermute(value, "exp", [(i, i ^ bits) for i in range(16)])


KEY_STEP = 512
LAT_WIDTH = LATENT + 128


def attention_kernel(q_ref, near_ref, far_ref, w_ref, kpos_ref, qpos_ref, qlo_ref, out_ref,
                     bias, keys, values, scores):
    half = KEYS // 2

    @pl.when(pl.program_id(0) == 0)
    def _():
        kpos = kpos_ref[...]
        allowed = (kpos <= qpos_ref[...]) & (kpos >= qlo_ref[...])
        bias[...] = jnp.where(allowed, 0.0, NEG_FILL)
        for head in range(2):
            keys[head, :half, NOPE:] = near_ref[:, LATENT:LATENT + ROPE]
            keys[head, half:, NOPE:] = far_ref[:, LATENT:LATENT + ROPE]

    log2e = 1.4426950408889634
    factor = (NOPE + ROPE) ** (-0.5) * log2e
    steps = range(KEYS // KEY_STEP)
    for head in range(2):
        cols = slice(head * (NOPE + VDIM), (head + 1) * (NOPE + VDIM))
        for step in steps:
            rows = slice(step * KEY_STEP, (step + 1) * KEY_STEP)
            if step * KEY_STEP < half:
                lat = near_ref[rows, :LATENT]
            else:
                lat = far_ref[step * KEY_STEP - half:(step + 1) * KEY_STEP - half, :LATENT]
            pair = jnp.dot(lat, w_ref[:, cols], preferred_element_type=F32).astype(BF16)
            keys[head, rows, :NOPE] = pair[:, :NOPE]
            values[head, rows, :] = pair[:, NOPE:]
    for head in range(2):
        query = q_ref[:, head * (NOPE + ROPE):(head + 1) * (NOPE + ROPE)]
        peak = None
        for step in steps:
            rows = slice(step * KEY_STEP, (step + 1) * KEY_STEP)
            part = lax.dot_general(query, keys[head, rows, :], (((1,), (1,)), ((), ())),
                                   preferred_element_type=F32)
            part = part * factor + bias[:, rows]
            scores[head, :, rows] = part
            top = jnp.max(part, axis=1, keepdims=True)
            peak = top if peak is None else jnp.maximum(peak, top)
        total = jnp.zeros((ROWS, 1), F32)
        out = jnp.zeros((ROWS, VDIM), F32)
        for step in steps:
            rows = slice(step * KEY_STEP, (step + 1) * KEY_STEP)
            weight = jnp.exp2(scores[head, :, rows] - peak)
            total = total + jnp.sum(weight, axis=1, keepdims=True)
            out = out + jnp.dot(weight.astype(BF16), values[head, rows, :], preferred_element_type=F32)
        out_ref[:, head * VDIM:(head + 1) * VDIM] = (out / total).astype(BF16)


def attention(part, query, near, far, weight, kpos, qpos, qlo):
    pairs = HEADS_HERE // 4
    first = part * pairs
    return pl.pallas_call(
        attention_kernel,
        grid=(pairs,),
        in_specs=[
            pl.BlockSpec((ROWS, 2 * (NOPE + ROPE)), lambda h: (0, first + h)),
            whole(near.shape),
            whole(far.shape),
            pl.BlockSpec((LATENT, 2 * (NOPE + VDIM)), lambda h: (0, first + h)),
            whole(kpos.shape),
            whole(qpos.shape),
            whole(qlo.shape),
        ],
        out_specs=pl.BlockSpec((ROWS, 2 * VDIM), lambda h: (0, h)),
        out_shape=jax.ShapeDtypeStruct((ROWS, pairs * 2 * VDIM), BF16),
        scratch_shapes=[
            pltpu.VMEM((ROWS, KEYS), F32),
            pltpu.VMEM((2, KEYS, NOPE + ROPE), BF16),
            pltpu.VMEM((2, KEYS, VDIM), BF16),
            pltpu.VMEM((2, ROWS, KEYS), F32),
        ],
        compiler_params=params(40),
        cost_estimate=pl.CostEstimate(flops=3_500_000_000, bytes_accessed=8_000_000, transcendentals=2_100_000),
        name="attention",
    )(query, near, far, weight, kpos, qpos, qlo)


HALF = HEADS_HERE * VDIM // 2


def project_kernel(by_x, index_ref, heads_0, heads_1, w0, w1, w2, w3, p0, p1, p2, p3,
                   left, weights, sems):
    sources = (w0, w1, w2, w3)
    copies = [pltpu.make_async_copy(sources[i], weights.at[i], sems.at[i]) for i in range(4)]
    for copy in copies:
        copy.start()
    for m in range(4):
        for n in range(4):
            if by_x:
                first = (index_ref[0] ^ m) * 64 + n * 16
            else:
                first = n * 64 + (index_ref[1] ^ m) * 16
            first = pl.multiple_of(first, 16)
            rows = slice(m * 64 + n * 16, m * 64 + n * 16 + 16)
            left[rows, :HALF] = heads_0[pl.ds(first, 16), :]
            left[rows, HALF:] = heads_1[pl.ds(first, 16), :]
    for i in range(4):
        copies[i].wait()
        part = jnp.dot(left[...], weights[i], preferred_element_type=F32).astype(BF16)
        for m, ref in enumerate((p0, p1, p2, p3)):
            ref[:, i * SEG:(i + 1) * SEG] = part[m * 64:(m + 1) * 64, :]


def project(by_x, index, heads, weights):
    piece = jax.ShapeDtypeStruct((64, 4 * SEG), BF16)
    return pl.pallas_call(
        functools.partial(project_kernel, by_x),
        grid_spec=pltpu.PrefetchScalarGridSpec(
            num_scalar_prefetch=1,
            grid=(1,),
            in_specs=[whole(heads[0].shape)] * 2 + [pl.BlockSpec(memory_space=pl.ANY)] * 4,
            out_specs=[whole(piece.shape)] * 4,
            scratch_shapes=[
                pltpu.VMEM((ROWS, 2 * HALF), BF16),
                pltpu.VMEM((4, 2 * HALF, SEG), BF16),
                pltpu.SemaphoreType.DMA((4,)),
            ],
        ),
        out_shape=[piece] * 4,
        compiler_params=params(24),
        cost_estimate=pl.CostEstimate(flops=3_800_000_000, bytes_accessed=9_000_000, transcendentals=0),
        name="project",
    )(index, *heads, *weights)


def first_sum_kernel(by_x, index_ref, i0, i1, i2, i3, o0, o1, o2, o3):
    spot = index_ref[1] if by_x else index_ref[0]
    for m, out in enumerate((o0, o1, o2, o3)):
        rows = pl.ds(pl.multiple_of((spot ^ m) * 16, 16), 16)
        total = i0[rows, :].astype(F32)
        for ref in (i1, i2, i3):
            total = total + ref[rows, :].astype(F32)
        out[...] = total.astype(BF16)


def first_sum(by_x, index, pieces):
    out = jax.ShapeDtypeStruct((16, 4 * SEG), BF16)
    return pl.pallas_call(
        functools.partial(first_sum_kernel, by_x),
        grid_spec=pltpu.PrefetchScalarGridSpec(
            num_scalar_prefetch=1,
            grid=(1,),
            in_specs=[whole((64, 4 * SEG))] * 4,
            out_specs=[whole(out.shape)] * 4,
        ),
        out_shape=[out] * 4,
        compiler_params=params(12),
        cost_estimate=pl.CostEstimate(flops=1_000_000, bytes_accessed=2_300_000, transcendentals=0),
        name="first_sum",
    )(index, *pieces)


def stream_kernel(index_ref, *refs):
    sums, (own_res, far_res, gain, place, stream_own, stream_far, send, stack) = refs[:8], refs[8:]
    spot = index_ref[2]
    for i in range(4):
        seg = spot ^ i
        cols = slice(i * SEG, (i + 1) * SEG)
        scaled = gain[seg]
        for block, res, stream in ((0, own_res, stream_own), (1, far_res, stream_far)):
            total = res[seg].astype(F32)
            for ref in sums[block * 4:block * 4 + 4]:
                total = total + ref[:, cols].astype(F32)
            stream[seg] = total
            first = pl.multiple_of(seg * 32 + block * 16, 16)
            stack[pl.ds(first, 16), :] = (total * scaled).astype(BF16)
    send[...] = jnp.dot(place[...], stack[...], preferred_element_type=F32).astype(BF16)


def make_stream(index, sums, own_res, far_res, gain, place):
    return pl.pallas_call(
        stream_kernel,
        grid_spec=pltpu.PrefetchScalarGridSpec(
            num_scalar_prefetch=1,
            grid=(1,),
            in_specs=[whole(v.shape) for v in (*sums, own_res, far_res, gain, place)],
            out_specs=[whole((4, 16, SEG))] * 2 + [whole((384, SEG))],
            scratch_shapes=[pltpu.VMEM((128, SEG), BF16)],
        ),
        out_shape=[jax.ShapeDtypeStruct((4, 16, SEG), F32)] * 2
        + [jax.ShapeDtypeStruct((384, SEG), BF16)],
        compiler_params=params(12),
        cost_estimate=pl.CostEstimate(flops=90_000_000, bytes_accessed=3_000_000, transcendentals=0),
        name="make_stream",
    )(index, *sums, own_res, far_res, gain, place)


def pick_rows(order):
    matrix = np.zeros((4, 96, 384), np.float32)
    for q in range(4):
        for block in range(2):
            for e in range(16):
                for s in range(CAP):
                    matrix[q, block * 48 + e * 3 + s, e * 24 + q * 6 + order[block] * 3 + s] = 1.0
    return jnp.asarray(matrix.reshape(384, 384), BF16)


def up_step(pick_ref, x0, x1, gain_ref, weights, gate_up, squares):
    rows = [jnp.dot(pick_ref[...], x[...], preferred_element_type=F32) for x in (x0, x1)]
    rows = jnp.concatenate(rows, axis=0)
    squares[...] += jnp.sum(rows * rows * gain_ref[0], axis=1, keepdims=True)
    rows = rows.astype(BF16)
    for i, ref in enumerate(weights):
        cols = slice(i * 256, (i + 1) * 256)
        gate_up[:, cols] += jnp.dot(rows, ref[...], preferred_element_type=F32)


def expert_first_kernel(index_ref, x0, x1, pick_ref, gain_ref, g0, g1, u0, u1, gate_up, squares):
    @pl.when(pl.program_id(0) == 0)
    def _():
        gate_up[...] = jnp.zeros_like(gate_up)
        squares[...] = jnp.zeros_like(squares)

    up_step(pick_ref, x0, x1, gain_ref, (g0, g1, u0, u1), gate_up, squares)


def expert_first(index, x0, x1, pick, gain, weights):
    spec = pl.BlockSpec((SEG, 256), lambda q, index_ref: (index_ref[3] * 4 + q, 0))
    return pl.pallas_call(
        expert_first_kernel,
        grid_spec=pltpu.PrefetchScalarGridSpec(
            num_scalar_prefetch=1,
            grid=(4,),
            in_specs=[
                whole(x0.shape),
                whole(x1.shape),
                pl.BlockSpec((96, 384), lambda q, index_ref: (q, 0)),
                pl.BlockSpec((1, 1, SEG), lambda q, index_ref: (index_ref[3] * 4 + q, 0, 0)),
            ] + [spec] * 4,
            out_specs=[whole((192, 1024)), whole((192, 1))],
        ),
        out_shape=[jax.ShapeDtypeStruct((192, 1024), F32), jax.ShapeDtypeStruct((192, 1), F32)],
        compiler_params=params(24),
        cost_estimate=pl.CostEstimate(flops=1_700_000_000, bytes_accessed=9_500_000, transcendentals=0),
        name="expert_first",
    )(index, x0, x1, pick, gain, *weights)


def expert_last_kernel(index_ref, x0, x1, pick_ref, gain_ref, g0, g1, u0, u1, d0, d1, before, squares_before,
                       r0, r1, r2, r3, gate_up, squares, hidden):
    step = pl.program_id(0)

    @pl.when(step == 0)
    def _():
        gate_up[...] = before[...]
        squares[...] = squares_before[...]

    @pl.when(step < 4)
    def _():
        up_step(pick_ref, x0, x1, gain_ref, (g0, g1, u0, u1), gate_up, squares)

    @pl.when(step == 3)
    def _():
        scale = lax.rsqrt(squares[...] * (1.0 / D) + EPSILON)
        gate = gate_up[:, :512] * scale
        up = gate_up[:, 512:] * scale
        hidden[...] = (gate / (1.0 + jnp.exp(-gate)) * up).astype(BF16)

    @pl.when(step >= 4)
    def _():
        out = jnp.dot(hidden[:, :256], d0[...], preferred_element_type=F32)
        out = out + jnp.dot(hidden[:, 256:], d1[...], preferred_element_type=F32)
        out = out.astype(BF16)
        for i, ref in enumerate((r0, r1, r2, r3)):
            ref[...] = out[i * 48:(i + 1) * 48]


def expert_last(index, x0, x1, pick, gain, weights, downs, before, squares_before):
    up_spec = pl.BlockSpec(
        (SEG, 256), lambda q, index_ref: ((1 - index_ref[3]) * 4 + jnp.minimum(q, 3), 0)
    )
    down_spec = pl.BlockSpec((256, 2 * SEG), lambda q, index_ref: (0, jnp.maximum(q - 4, 0)))
    out_spec = pl.BlockSpec((48, 2 * SEG), lambda q, index_ref: (0, jnp.maximum(q - 4, 0)))
    return pl.pallas_call(
        expert_last_kernel,
        grid_spec=pltpu.PrefetchScalarGridSpec(
            num_scalar_prefetch=1,
            grid=(8,),
            in_specs=[
                whole(x0.shape),
                whole(x1.shape),
                pl.BlockSpec((96, 384), lambda q, index_ref: (jnp.minimum(q, 3), 0)),
                pl.BlockSpec(
                    (1, 1, SEG), lambda q, index_ref: ((1 - index_ref[3]) * 4 + jnp.minimum(q, 3), 0, 0)
                ),
            ] + [up_spec] * 4 + [down_spec] * 2 + [whole((192, 1024)), whole((192, 1))],
            out_specs=[out_spec] * 4,
            scratch_shapes=[
                pltpu.VMEM((192, 1024), F32),
                pltpu.VMEM((192, 1), F32),
                pltpu.VMEM((192, 512), BF16),
            ],
        ),
        out_shape=[jax.ShapeDtypeStruct((48, D), BF16)] * 4,
        compiler_params=params(32),
        cost_estimate=pl.CostEstimate(flops=3_200_000_000, bytes_accessed=21_000_000, transcendentals=100_000),
        name="expert_last",
    )(index, x0, x1, pick, gain, *weights, *downs, before, squares_before)


def spread_kernel(p0, p1, p2, p3, out):
    total = p0[...].astype(F32)
    for ref in (p1, p2, p3):
        total = total + ref[...].astype(F32)
    total = total.astype(BF16)
    stack = jnp.concatenate([total[:, q * SEG:(q + 1) * SEG] for q in range(8)], axis=0)
    row = lax.broadcasted_iota(jnp.int32, (384, 384), 0)
    col = lax.broadcasted_iota(jnp.int32, (384, 384), 1)
    move = (row == (col % 48) * 8 + col // 48).astype(BF16)
    out[...] = jnp.dot(move, stack, preferred_element_type=F32).astype(BF16)


def spread(parts):
    return pl.pallas_call(
        spread_kernel,
        out_shape=jax.ShapeDtypeStruct((384, SEG), BF16),
        compiler_params=params(24),
        cost_estimate=pl.CostEstimate(flops=260_000_000, bytes_accessed=3_500_000, transcendentals=0),
        name="spread",
    )(*parts)


def combine_kernel(index_ref, rows, weight, stream_own, stream_far, out, routed):
    total = jnp.dot(weight[0], rows[...], preferred_element_type=F32)
    for i in (1, 2):
        total = total + jnp.dot(weight[i], rows[...], preferred_element_type=F32)
    routed[...] = total
    pair = index_ref[3]
    for q in range(4):
        for side, stream in ((pair, stream_own), (1 - pair, stream_far)):
            seg = side * 4 + q
            picked = routed[pl.ds(pl.multiple_of(seg * 16, 16), 16), :]
            out[:, pl.ds(pl.multiple_of(seg * SEG, 128), SEG)] = (picked + stream[q]).astype(BF16)


def combine(index, rows, weight, stream_own, stream_far):
    return pl.pallas_call(
        combine_kernel,
        grid_spec=pltpu.PrefetchScalarGridSpec(
            num_scalar_prefetch=1,
            grid=(1,),
            in_specs=[whole(v.shape) for v in (rows, weight, stream_own, stream_far)],
            out_specs=whole((16, D)),
            scratch_shapes=[pltpu.VMEM((128, SEG), F32)],
        ),
        out_shape=jax.ShapeDtypeStruct((16, D), BF16),
        compiler_params=params(24),
        cost_estimate=pl.CostEstimate(flops=270_000_000, bytes_accessed=1_800_000, transcendentals=0),
        name="combine",
    )(index, rows, weight, stream_own, stream_far)


def three_parts(value):
    first = lax.reduce_precision(value, 8, 7)
    second = lax.reduce_precision(value - first, 8, 7)
    third = value - first - second
    return jnp.stack([first, second, third]).astype(BF16)


def slots_of(expert_ids):
    matches = expert_ids[:, :, None] == jnp.arange(16, dtype=jnp.int32)[None, None, :]
    named = jnp.any(matches, axis=1)
    slot = jnp.cumsum(named.astype(jnp.int32), axis=0) - 1
    placed = named[:, :, None] & (slot[:, :, None] == jnp.arange(CAP, dtype=jnp.int32))
    return matches, placed


def per_device(residual, queries, latent, key_rope, doc_ids, kv_weight, out_weight, norm_gain,
               expert_ids, expert_gates, w_gate, w_up, w_down):
    c = lax.axis_index("ctx")
    e = lax.axis_index("exp")
    y, k, x, z = c >> 1, c & 1, e >> 2, e & 3
    pair = y >> 1
    index = jnp.stack([x, z, c & 3, pair]).astype(jnp.int32)

    lat = jnp.concatenate(
        [latent, key_rope, jnp.zeros((BLK, LAT_WIDTH - LATENT - ROPE), BF16)], axis=1
    )
    lat = jnp.concatenate([lat] + [swap_ctx(lat, 2 * m) for m in (1, 2, 3)], axis=0)

    out_core = swap_ctx(out_weight, 1)
    out_next = swap_ctx(out_weight, 2)

    spot = jnp.arange(KEYS, dtype=jnp.int32)
    my, mz, mx, mk = (spot >> 4) & 3, (spot >> 6) & 3, (spot >> 8) & 3, spot >> 10
    key_block = ((y ^ my) * 2 + (k ^ mk)) * 16 + (x ^ mx) * 4 + (z ^ mz)
    kpos = (key_block * 16 + (spot & 15)).reshape(1, KEYS).astype(jnp.int32)
    qpos = (c * ROWS + jnp.arange(ROWS, dtype=jnp.int32)).reshape(ROWS, 1)
    own_docs = lax.dynamic_slice_in_dim(doc_ids, c * ROWS, ROWS, 0)
    qlo = jnp.sum((doc_ids[None, :] < own_docs[:, None]).astype(jnp.int32), axis=1, keepdims=True)

    res = residual.reshape(BLK, 8, SEG).transpose(1, 0, 2)
    own_res = lax.dynamic_slice_in_dim(res, pair * 4, 4, 0)
    far_res = swap_ctx(lax.dynamic_slice_in_dim(res, (1 - pair) * 4, 4, 0), 6)
    gain_rows = norm_gain.reshape(8, 1, SEG)
    own_gain = lax.dynamic_slice_in_dim(gain_rows, pair * 4, 4, 0)
    inverse_gain = 1.0 / (gain_rows * gain_rows)
    far_ids = swap_ctx(expert_ids, 6)
    lat, kpos, qpos, qlo, own_res, far_res, own_gain, inverse_gain, far_ids = lax.optimization_barrier(
        (lat, kpos, qpos, qlo, own_res, far_res, own_gain, inverse_gain, far_ids)
    )
    lat = jnp.concatenate([lat] + [swap_exp(lat, m) for m in (1, 2, 3)], axis=0)

    matches, placed = slots_of(expert_ids)
    _, far_placed = slots_of(far_ids)
    both = jnp.stack([placed, far_placed]).astype(BF16)
    place = jnp.einsum(
        "btjs,qr,bd->jqbsrdt", both, jnp.eye(4, dtype=BF16), jnp.eye(2, dtype=BF16)
    ).reshape(384, 128)
    lat, place = lax.optimization_barrier((lat, place))
    near = jnp.concatenate([lat] + [swap_exp(lat, 4 * m) for m in (1, 2, 3)], axis=0)
    route = jnp.sum(jnp.where(matches, expert_gates[:, :, None], 0.0), axis=1)
    slot_weight = jnp.where(placed, route[:, :, None], 0.0)
    weight = slot_weight.reshape(1, BLK, 48, 1) * jnp.eye(8, dtype=F32)[:, None, None, :]
    weight = three_parts(weight.reshape(128, 384))
    near, weight = lax.optimization_barrier((near, weight))
    far = swap_ctx(near, 1)

    heads_0 = attention(0, queries, near, far, kv_weight, kpos, qpos, qlo)
    heads_0, out_next = lax.optimization_barrier((heads_0, out_next))
    out_both = swap_ctx(out_next, 1)
    far_heads_0 = swap_ctx(heads_0, 6)
    near, far, heads_0 = lax.optimization_barrier((near, far, heads_0))
    heads_1 = attention(1, queries, near, far, kv_weight, kpos, qpos, qlo)
    far_heads_1 = swap_ctx(heads_1, 6)

    gate, up, down = w_gate[0], w_up[0], w_down[0]
    gate_in, up_in, down_in, heads_1 = lax.optimization_barrier((gate, up, down, heads_1))
    gate_far = swap_ctx(gate_in, 1)
    up_far = swap_ctx(up_in, 1)
    down_far = swap_ctx(down_in, 1)

    out_weights = (out_weight, out_core, out_next, out_both)
    own = project(True, index, (heads_0, heads_1), out_weights)
    far_heads_0, far_heads_1, *own = lax.optimization_barrier((far_heads_0, far_heads_1, *own))
    other = project(False, index, (far_heads_0, far_heads_1), out_weights)
    own = [own[0]] + [swap_exp(own[m], 4 * m) for m in (1, 2, 3)]
    other = [other[0]] + [swap_exp(other[m], m) for m in (1, 2, 3)]
    own = first_sum(True, index, own)
    own = [own[0]] + [swap_exp(own[m], m) for m in (1, 2, 3)]
    other = first_sum(False, index, other)
    other = [other[0]] + [swap_exp(other[m], 4 * m) for m in (1, 2, 3)]
    stream_own, stream_far, send = make_stream(index, own + other, own_res, far_res, own_gain, place)

    got = lax.all_to_all(send.reshape(16, 24, SEG), "exp", split_axis=0, concat_axis=0, tiled=True)
    stream_far = swap_ctx(stream_far, 6)
    got, stream_far = lax.optimization_barrier((got.reshape(384, SEG), stream_far))
    got_1, got_3, got_2 = swap_ctx(got, 2), swap_ctx(got, 6), swap_ctx(got, 4)
    ups = (gate, gate_far, up, up_far)
    gate_up, squares = expert_first(index, got, got_1, pick_rows((0, 1)), inverse_gain, ups)
    r0, r3, r1, r2 = expert_last(
        index, got_3, got_2, pick_rows((1, 0)), inverse_gain, ups, (down, down_far), gate_up, squares
    )
    back = spread([r0, swap_ctx(r1, 2), swap_ctx(r3, 6), swap_ctx(r2, 4)])
    rows = lax.all_to_all(back.reshape(16, 24, SEG), "exp", split_axis=0, concat_axis=0, tiled=True)
    return combine(index, rows.reshape(384, SEG), weight, stream_own, stream_far)


def solution(mesh):
    placed = (
        P(("ctx", "exp"), None),
        P("ctx", "exp"),
        P(("ctx", "exp"), None),
        P(("ctx", "exp"), None),
        P(),
        P(None, "exp"),
        P("exp", "ctx"),
        P(),
        P(("ctx", "exp"), None),
        P(("ctx", "exp"), None),
        P("exp", None, "ctx"),
        P("exp", None, "ctx"),
        P("exp", "ctx", None),
    )
    return jax.shard_map(
        per_device, mesh=mesh, in_specs=placed, out_specs=P(("ctx", "exp"), None), check_vma=False
    )
```

```python
import functools

import jax
import jax.numpy as jnp
import numpy as np
from jax import lax
from jax.experimental import pallas as pl
from jax.experimental.pallas import tpu as pltpu
from jax.sharding import PartitionSpec as P

NOPE = 128
ROPE = 64
VDIM = 128
LATENT = 512
CAP = 3
D = 7168
EPSILON = 1e-06
HEADS_HERE = 8
ROWS = 256
KEYS = 2048
BLK = 16
SEG = 896
NEG_FILL = -1e30
F32 = jnp.float32
BF16 = jnp.bfloat16
MIB = 1024 * 1024
SMEM = pl.BlockSpec(memory_space=pltpu.SMEM)
VMEM = pl.BlockSpec(memory_space=pltpu.VMEM)


def params(mib):
    return pltpu.CompilerParams(vmem_limit_bytes=mib * MIB)


def whole(shape):
    zeros = (0,) * len(shape)
    return pl.BlockSpec(shape, lambda *_: zeros)


def swap_ctx(value, bits):
    return lax.ppermute(value, "ctx", [(i, i ^ bits) for i in range(8)])


def swap_exp(value, bits):
    return lax.ppermute(value, "exp", [(i, i ^ bits) for i in range(16)])


KEY_STEP = 512
LAT_WIDTH = LATENT + 128


def mask_kernel(index_ref, docs_ref, bias):
    y, k = index_ref[4], index_ref[5]
    spot = lax.broadcasted_iota(jnp.int32, (1, KEYS), 1)
    my, e, mk = (spot >> 4) & 3, (spot >> 6) & 15, spot >> 10
    kpos = (((my ^ y) * 2 + (mk ^ k)) * 16 + e) * 16 + (spot & 15)
    first = (y * 2 + k) * ROWS
    row = lax.broadcasted_iota(jnp.int32, (ROWS, ROWS), 0)
    col = lax.broadcasted_iota(jnp.int32, (ROWS, ROWS), 1)
    own = docs_ref[:, pl.ds(pl.multiple_of(first, ROWS), ROWS)]
    own = jnp.sum(jnp.where(row == col, own, 0), axis=1, keepdims=True)
    qlo = jnp.sum((docs_ref[...] < own).astype(jnp.int32), axis=1, keepdims=True)
    qpos = first + lax.broadcasted_iota(jnp.int32, (ROWS, 1), 0)
    allowed = (kpos <= qpos) & (kpos >= qlo)
    bias[...] = jnp.where(allowed, 0.0, NEG_FILL)


def make_mask(index, docs):
    return pl.pallas_call(
        mask_kernel,
        in_specs=[SMEM, VMEM],
        out_specs=VMEM,
        out_shape=jax.ShapeDtypeStruct((ROWS, KEYS), F32),
        compiler_params=params(8),
        cost_estimate=pl.CostEstimate(flops=2_000_000, bytes_accessed=2_100_000, transcendentals=0),
        name="make_mask",
    )(index, docs)


def attention_kernel(q_ref, near_ref, far_ref, w_ref, bias, out_ref, keys, values, scores):
    half = KEYS // 2

    @pl.when(pl.program_id(0) == 0)
    def _():
        for head in range(2):
            keys[head, :half, NOPE:] = near_ref[:, LATENT:LATENT + ROPE]
            keys[head, half:, NOPE:] = far_ref[:, LATENT:LATENT + ROPE]

    log2e = 1.4426950408889634
    factor = (NOPE + ROPE) ** (-0.5) * log2e
    steps = range(KEYS // KEY_STEP)
    for head in range(2):
        cols = slice(head * (NOPE + VDIM), (head + 1) * (NOPE + VDIM))
        for step in steps:
            rows = slice(step * KEY_STEP, (step + 1) * KEY_STEP)
            if step * KEY_STEP < half:
                lat = near_ref[rows, :LATENT]
            else:
                lat = far_ref[step * KEY_STEP - half:(step + 1) * KEY_STEP - half, :LATENT]
            pair = jnp.dot(lat, w_ref[:, cols], preferred_element_type=F32).astype(BF16)
            keys[head, rows, :NOPE] = pair[:, :NOPE]
            values[head, rows, :] = pair[:, NOPE:]
    for head in range(2):
        query = q_ref[:, head * (NOPE + ROPE):(head + 1) * (NOPE + ROPE)]
        peak = None
        for step in steps:
            rows = slice(step * KEY_STEP, (step + 1) * KEY_STEP)
            part = lax.dot_general(query, keys[head, rows, :], (((1,), (1,)), ((), ())),
                                   preferred_element_type=F32)
            part = part * factor + bias[:, rows]
            scores[head, :, rows] = part
            top = jnp.max(part, axis=1, keepdims=True)
            peak = top if peak is None else jnp.maximum(peak, top)
        total = jnp.zeros((ROWS, 1), F32)
        out = jnp.zeros((ROWS, VDIM), F32)
        for step in steps:
            rows = slice(step * KEY_STEP, (step + 1) * KEY_STEP)
            weight = jnp.exp2(scores[head, :, rows] - peak)
            total = total + jnp.sum(weight, axis=1, keepdims=True)
            out = out + jnp.dot(weight.astype(BF16), values[head, rows, :], preferred_element_type=F32)
        out_ref[:, head * VDIM:(head + 1) * VDIM] = (out / total).astype(BF16)


def attention(part, query, near, far, weight, bias):
    pairs = HEADS_HERE // 4
    first = part * pairs
    return pl.pallas_call(
        attention_kernel,
        grid=(pairs,),
        in_specs=[
            pl.BlockSpec((ROWS, 2 * (NOPE + ROPE)), lambda h: (0, first + h)),
            VMEM,
            VMEM,
            pl.BlockSpec((LATENT, 2 * (NOPE + VDIM)), lambda h: (0, first + h)),
            VMEM,
        ],
        out_specs=pl.BlockSpec((ROWS, 2 * VDIM), lambda h: (0, h)),
        scratch_shapes=[
            pltpu.VMEM((2, KEYS, NOPE + ROPE), BF16),
            pltpu.VMEM((2, KEYS, VDIM), BF16),
            pltpu.VMEM((2, ROWS, KEYS), F32),
        ],
        out_shape=jax.ShapeDtypeStruct((ROWS, pairs * 2 * VDIM), BF16),
        compiler_params=params(24),
        cost_estimate=pl.CostEstimate(flops=1000, bytes_accessed=1000, transcendentals=0),
        name="attention",
    )(query, near, far, weight, bias)


HALF = HEADS_HERE * VDIM // 2


def pick_heads(by_x, index_ref, heads_0, heads_1, left):
    for m in range(4):
        for n in range(4):
            if by_x:
                first = (index_ref[0] ^ m) * 64 + n * 16
            else:
                first = n * 64 + (index_ref[1] ^ m) * 16
            first = pl.multiple_of(first, 16)
            rows = slice(m * 64 + n * 16, m * 64 + n * 16 + 16)
            left[rows, :HALF] = heads_0[pl.ds(first, 16), :]
            left[rows, HALF:] = heads_1[pl.ds(first, 16), :]


def project_segment(i, left, weight, outs):
    part = jnp.dot(left[...], weight, preferred_element_type=F32).astype(BF16)
    for m, ref in enumerate(outs):
        ref[:, i * SEG:(i + 1) * SEG] = part[m * 64:(m + 1) * 64, :]


def project_first_kernel(index_ref, heads_0, heads_1, w0, w1, w2, w3, p0, p1, p2, p3, kept, left, sems):
    copies = [pltpu.make_async_copy(w, kept.at[i], sems.at[i]) for i, w in enumerate((w0, w1, w2, w3))]
    for copy in copies:
        copy.start()
    pick_heads(True, index_ref, heads_0, heads_1, left)
    for i in range(4):
        copies[i].wait()
        project_segment(i, left, kept[i], (p0, p1, p2, p3))


def project_first(index, heads, weights):
    piece = jax.ShapeDtypeStruct((64, 4 * SEG), BF16)
    return pl.pallas_call(
        project_first_kernel,
        in_specs=[SMEM, VMEM, VMEM] + [pl.BlockSpec(memory_space=pl.ANY)] * 4,
        out_specs=[VMEM] * 5,
        scratch_shapes=[pltpu.VMEM((ROWS, 2 * HALF), BF16), pltpu.SemaphoreType.DMA((4,))],
        out_shape=[piece] * 4 + [jax.ShapeDtypeStruct((4, 2 * HALF, SEG), BF16)],
        compiler_params=params(16),
        cost_estimate=pl.CostEstimate(flops=3_800_000_000, bytes_accessed=9_000_000, transcendentals=0),
        name="project_first",
    )(index, *heads, *weights)


def project_kernel(index_ref, heads_0, heads_1, kept, p0, p1, p2, p3, left):
    pick_heads(False, index_ref, heads_0, heads_1, left)
    for i in range(4):
        project_segment(i, left, kept[i], (p0, p1, p2, p3))


def project(index, heads, kept):
    piece = jax.ShapeDtypeStruct((64, 4 * SEG), BF16)
    return pl.pallas_call(
        project_kernel,
        in_specs=[SMEM] + [VMEM] * 3,
        out_specs=[VMEM] * 4,
        scratch_shapes=[pltpu.VMEM((ROWS, 2 * HALF), BF16)],
        out_shape=[piece] * 4,
        compiler_params=params(16),
        cost_estimate=pl.CostEstimate(flops=3_800_000_000, bytes_accessed=9_000_000, transcendentals=0),
        name="project",
    )(index, *heads, kept)


def first_sum_kernel(by_x, index_ref, i0, i1, i2, i3, o0, o1, o2, o3):
    spot = index_ref[1] if by_x else index_ref[0]
    for m, out in enumerate((o0, o1, o2, o3)):
        rows = pl.ds(pl.multiple_of((spot ^ m) * 16, 16), 16)
        total = i0[rows, :].astype(F32)
        for ref in (i1, i2, i3):
            total = total + ref[rows, :].astype(F32)
        out[...] = total.astype(BF16)


def first_sum(by_x, index, pieces):
    out = jax.ShapeDtypeStruct((16, 4 * SEG), BF16)
    return pl.pallas_call(
        functools.partial(first_sum_kernel, by_x),
        in_specs=[SMEM] + [VMEM] * 4,
        out_specs=[VMEM] * 4,
        out_shape=[out] * 4,
        compiler_params=params(12),
        cost_estimate=pl.CostEstimate(flops=1_000_000, bytes_accessed=2_300_000, transcendentals=0),
        name="first_sum",
    )(index, *pieces)


def stream_kernel(index_ref, *refs):
    sums, (res, far_res, gain, place, stream_own, stream_far, send, stack) = refs[:8], refs[8:]
    spot, base = index_ref[2], index_ref[3] * 4
    for i in range(4):
        seg = spot ^ i
        cols = slice(i * SEG, (i + 1) * SEG)
        wide = pl.ds(pl.multiple_of((base + seg) * SEG, 128), SEG)
        near = pl.ds(pl.multiple_of(seg * SEG, 128), SEG)
        for block, start, stream in ((0, res[:, wide], stream_own), (1, far_res[:, near], stream_far)):
            total = start.astype(F32)
            for ref in sums[block * 4:block * 4 + 4]:
                total = total + ref[:, cols].astype(F32)
            stream[seg] = total
            first = pl.multiple_of(seg * 32 + block * 16, 16)
            stack[pl.ds(first, 16), :] = (total * gain[:, wide]).astype(BF16)
    send[...] = jnp.dot(place[...], stack[...], preferred_element_type=F32).astype(BF16)


def make_stream(index, sums, res, far_res, gain, place):
    return pl.pallas_call(
        stream_kernel,
        in_specs=[SMEM] + [VMEM] * 12,
        out_specs=[VMEM] * 3,
        scratch_shapes=[pltpu.VMEM((128, SEG), BF16)],
        out_shape=[jax.ShapeDtypeStruct((4, 16, SEG), F32)] * 2
        + [jax.ShapeDtypeStruct((384, SEG), BF16)],
        compiler_params=params(12),
        cost_estimate=pl.CostEstimate(flops=90_000_000, bytes_accessed=3_000_000, transcendentals=0),
        name="make_stream",
    )(index, *sums, res, far_res, gain, place)


def one_hot(values, count):
    return (np.asarray(values)[:, None] == np.arange(count)[None, :]).astype(np.float32)


def routing_tables():
    row, col = np.arange(384), np.arange(128)
    to_expert = one_hot(row // 24, 16)
    to_token = one_hot(col % 16, 16).T
    segment = (row // 6 % 4)[:, None] == (col // 32)[None, :]
    block = (row // 3 % 2)[:, None] == (col // 16 % 2)[None, :]
    kept = np.stack([segment & block & (col // 16 % 2 == b)[None, :] for b in range(2)])
    slot = (row % 3).astype(np.float32)[:, None]
    return_kept = (col // 16)[:, None] == (row % 8)[None, :]
    return_slot = (row // 8 % 3).astype(np.float32)[None, :]
    return [
        jnp.asarray(to_expert, BF16), jnp.asarray(to_token, BF16), jnp.asarray(kept, F32),
        jnp.asarray(slot, F32), jnp.asarray(return_kept, F32), jnp.asarray(return_slot, F32),
    ]


def routing_kernel(ids_ref, far_ref, gates_ref, to_expert, to_token, kept, slot, return_kept, return_slot,
                   place, weight):
    expert = lax.broadcasted_iota(jnp.int32, (16, 16), 0)
    token = lax.broadcasted_iota(jnp.int32, (16, 16), 1)
    earlier = (expert < token).astype(BF16)

    def spots(ref):
        named = jnp.zeros((16, 16), F32)
        for j in range(8):
            named = jnp.maximum(named, (ref[j:j + 1, :] == expert).astype(F32))
        rank = jnp.dot(named.astype(BF16), earlier, preferred_element_type=F32)
        return jnp.where(named > 0.0, rank, -1.0).astype(BF16)

    by_block = [spots(ids_ref), spots(far_ref)]
    total = jnp.zeros((384, 128), F32)
    for block in range(2):
        wide = jnp.dot(to_expert[...], by_block[block], preferred_element_type=F32)
        wide = jnp.dot(wide.astype(BF16), to_token[...], preferred_element_type=F32)
        total = total + jnp.where(wide == slot[...], kept[block], 0.0)
    place[...] = total.astype(BF16)

    def spread_out(value):
        tall = lax.dot_general(to_token[...], value, (((0,), (1,)), ((), ())), preferred_element_type=F32)
        return lax.dot_general(tall.astype(BF16), to_expert[...], (((1,), (1,)), ((), ())),
                               preferred_element_type=F32)

    live = jnp.where(spread_out(by_block[0]) == return_slot[...], return_kept[...], 0.0)
    route = jnp.zeros((16, 16), F32)
    for j in range(8):
        route = route + jnp.where(ids_ref[j:j + 1, :] == expert, gates_ref[j:j + 1, :], 0.0)
    for i in range(3):
        part = route.astype(BF16)
        weight[i] = (spread_out(part) * live).astype(BF16)
        route = route - part.astype(F32)


def routing(ids, far_ids, gates):
    tables = routing_tables()
    return pl.pallas_call(
        routing_kernel,
        in_specs=[VMEM] * 9,
        out_specs=[VMEM] * 2,
        out_shape=[jax.ShapeDtypeStruct((384, 128), BF16), jax.ShapeDtypeStruct((3, 128, 384), BF16)],
        compiler_params=params(8),
        cost_estimate=pl.CostEstimate(flops=20_000_000, bytes_accessed=1_000_000, transcendentals=0),
        name="routing",
    )(ids, far_ids, gates, *tables)


def pick_rows(order):
    matrix = np.zeros((4, 96, 384), np.float32)
    for q in range(4):
        for block in range(2):
            for e in range(16):
                for s in range(CAP):
                    matrix[q, block * 48 + e * 3 + s, e * 24 + q * 6 + order[block] * 3 + s] = 1.0
    return jnp.asarray(matrix.reshape(384, 384), BF16)


def up_part(base, pick_ref, inputs, gain_ref, gate_ref, up_ref, rows):
    squares = jnp.zeros((192, 1), F32)
    for i, ref in enumerate(inputs):
        moved = jnp.dot(pick_ref[...], ref[...], preferred_element_type=F32)
        for q in range(4):
            part = moved[q * 96:(q + 1) * 96]
            rows[i * 96:(i + 1) * 96, q * SEG:(q + 1) * SEG] = part.astype(BF16)
    for q in range(4):
        part = rows[:, q * SEG:(q + 1) * SEG].astype(F32)
        gain = gain_ref[:, pl.ds(pl.multiple_of((base * 4 + q) * SEG, 128), SEG)]
        squares = squares + jnp.sum(part * part * (1.0 / (gain * gain)), axis=1, keepdims=True)
    parts = [
        jnp.dot(rows[...], ref[core], preferred_element_type=F32)
        for ref in (gate_ref, up_ref) for core in range(2)
    ]
    return parts, squares


def load_kernel(index_ref, g0, g1, u0, u1, d0, d1, gate_near, up_near, gate_far, up_far, down, sems):
    base = index_ref[3]
    depth = 4 * SEG
    copies = []
    for outs, half in (((gate_near, up_near), base), ((gate_far, up_far), 1 - base)):
        rows = pl.ds(pl.multiple_of(half * depth, depth), depth)
        for out, refs in zip(outs, ((g0, g1), (u0, u1))):
            for core in range(2):
                copies.append((refs[core].at[rows], out.at[core]))
    copies += [(d0, down.at[0]), (d1, down.at[1])]
    copies = [pltpu.make_async_copy(a, b, sems.at[i]) for i, (a, b) in enumerate(copies)]
    for copy in copies:
        copy.start()
    for copy in copies:
        copy.wait()


def load_weights(index, gate, up, down):
    half = jax.ShapeDtypeStruct((2, 4 * SEG, 256), BF16)
    return pl.pallas_call(
        load_kernel,
        in_specs=[SMEM] + [pl.BlockSpec(memory_space=pl.ANY)] * 6,
        out_specs=[VMEM] * 5,
        scratch_shapes=[pltpu.SemaphoreType.DMA((10,))],
        out_shape=[half] * 4 + [jax.ShapeDtypeStruct((2, 256, D), BF16)],
        compiler_params=params(30),
        cost_estimate=pl.CostEstimate(flops=0, bytes_accessed=44_000_000, transcendentals=0),
        name="load_weights",
    )(index, *gate, *up, *down)


def expert_first_kernel(index_ref, x0, x1, pick_ref, gain_ref, gate_ref, up_ref, gate_up, squares, rows):
    parts, total = up_part(index_ref[3], pick_ref, (x0, x1), gain_ref, gate_ref, up_ref, rows)
    for i, part in enumerate(parts):
        gate_up[:, i * 256:(i + 1) * 256] = part
    squares[...] = total


def expert_first(index, x0, x1, pick, gain, gate, up):
    return pl.pallas_call(
        expert_first_kernel,
        in_specs=[SMEM] + [VMEM] * 6,
        out_specs=[VMEM] * 2,
        scratch_shapes=[pltpu.VMEM((192, 4 * SEG), BF16)],
        out_shape=[jax.ShapeDtypeStruct((192, 1024), F32), jax.ShapeDtypeStruct((192, 1), F32)],
        compiler_params=params(16),
        cost_estimate=pl.CostEstimate(flops=1_700_000_000, bytes_accessed=9_500_000, transcendentals=0),
        name="expert_first",
    )(index, x0, x1, pick, gain, gate, up)


def expert_last_kernel(index_ref, x0, x1, pick_ref, gain_ref, gate_ref, up_ref, down_ref, before, squares_before,
                       r0, r1, r2, r3, rows, hidden):
    parts, total = up_part(1 - index_ref[3], pick_ref, (x0, x1), gain_ref, gate_ref, up_ref, rows)
    scale = lax.rsqrt((total + squares_before[...]) * (1.0 / D) + EPSILON)
    for core in range(2):
        gate = (parts[core] + before[:, core * 256:(core + 1) * 256]) * scale
        up = (parts[2 + core] + before[:, 512 + core * 256:512 + (core + 1) * 256]) * scale
        hidden[:, core * 256:(core + 1) * 256] = (gate / (1.0 + jnp.exp(-gate)) * up).astype(BF16)
    for q in range(4):
        cols = slice(q * 2 * SEG, (q + 1) * 2 * SEG)
        out = jnp.dot(hidden[:, :256], down_ref[0, :, cols], preferred_element_type=F32)
        out = out + jnp.dot(hidden[:, 256:], down_ref[1, :, cols], preferred_element_type=F32)
        out = out.astype(BF16)
        for i, ref in enumerate((r0, r1, r2, r3)):
            ref[:, cols] = out[i * 48:(i + 1) * 48]


def expert_last(index, x0, x1, pick, gain, gate, up, down, before, squares_before):
    return pl.pallas_call(
        expert_last_kernel,
        in_specs=[SMEM] + [VMEM] * 9,
        out_specs=[VMEM] * 4,
        scratch_shapes=[pltpu.VMEM((192, 4 * SEG), BF16), pltpu.VMEM((192, 512), BF16)],
        out_shape=[jax.ShapeDtypeStruct((48, D), BF16)] * 4,
        compiler_params=params(16),
        cost_estimate=pl.CostEstimate(flops=3_200_000_000, bytes_accessed=21_000_000, transcendentals=100_000),
        name="expert_last",
    )(index, x0, x1, pick, gain, gate, up, down, before, squares_before)


def spread_kernel(p0, p1, p2, p3, out):
    total = p0[...].astype(F32)
    for ref in (p1, p2, p3):
        total = total + ref[...].astype(F32)
    total = total.astype(BF16)
    stack = jnp.concatenate([total[:, q * SEG:(q + 1) * SEG] for q in range(8)], axis=0)
    row = lax.broadcasted_iota(jnp.int32, (384, 384), 0)
    col = lax.broadcasted_iota(jnp.int32, (384, 384), 1)
    move = (row == (col % 48) * 8 + col // 48).astype(BF16)
    out[...] = jnp.dot(move, stack, preferred_element_type=F32).astype(BF16)


def spread(parts):
    return pl.pallas_call(
        spread_kernel,
        out_shape=jax.ShapeDtypeStruct((384, SEG), BF16),
        compiler_params=params(24),
        cost_estimate=pl.CostEstimate(flops=260_000_000, bytes_accessed=3_500_000, transcendentals=0),
        name="spread",
    )(*parts)


def combine_kernel(index_ref, rows, weight, stream_own, stream_far, out, routed):
    total = jnp.dot(weight[0], rows[...], preferred_element_type=F32)
    for i in (1, 2):
        total = total + jnp.dot(weight[i], rows[...], preferred_element_type=F32)
    routed[...] = total
    pair = index_ref[3]
    for q in range(4):
        for side, stream in ((pair, stream_own), (1 - pair, stream_far)):
            seg = side * 4 + q
            picked = routed[pl.ds(pl.multiple_of(seg * 16, 16), 16), :]
            out[:, pl.ds(pl.multiple_of(seg * SEG, 128), SEG)] = (picked + stream[q]).astype(BF16)


def combine(index, rows, weight, stream_own, stream_far):
    return pl.pallas_call(
        combine_kernel,
        in_specs=[SMEM] + [VMEM] * 4,
        out_specs=VMEM,
        scratch_shapes=[pltpu.VMEM((128, SEG), F32)],
        out_shape=jax.ShapeDtypeStruct((16, D), BF16),
        compiler_params=params(12),
        cost_estimate=pl.CostEstimate(flops=270_000_000, bytes_accessed=1_800_000, transcendentals=0),
        name="combine",
    )(index, rows, weight, stream_own, stream_far)


def per_device(residual, queries, latent, key_rope, doc_ids, kv_weight, out_weight, norm_gain,
               expert_ids, expert_gates, w_gate, w_up, w_down):
    c = lax.axis_index("ctx")
    e = lax.axis_index("exp")
    y, k, x, z = c >> 1, c & 1, e >> 2, e & 3
    pair = y >> 1
    index = jnp.stack([x, z, c & 3, pair, y, k]).astype(jnp.int32)

    lat = jnp.concatenate(
        [latent, key_rope, jnp.zeros((BLK, LAT_WIDTH - LATENT - ROPE), BF16)], axis=1
    )
    lat = jnp.concatenate([lat] + [swap_ctx(lat, 2 * m) for m in (1, 2, 3)], axis=0)
    lat, out_weight, residual, expert_ids, doc_ids = lax.optimization_barrier(
        (lat, out_weight, residual, expert_ids, doc_ids)
    )
    out_next = swap_ctx(out_weight, 2)
    near = lax.all_to_all(
        jnp.broadcast_to(lat[None], (16,) + lat.shape), "exp", split_axis=0, concat_axis=0, tiled=True
    ).reshape(16 * lat.shape[0], LAT_WIDTH)
    near, out_weight, doc_ids = lax.optimization_barrier((near, out_weight, doc_ids))
    far = swap_ctx(near, 1)
    bias = make_mask(index, doc_ids.reshape(1, KEYS))
    out_core = swap_ctx(out_weight, 1)
    near, far, bias = lax.optimization_barrier((near, far, bias))

    heads_0 = attention(0, queries, near, far, kv_weight, bias)
    near, far, heads_0, out_next, out_core, w_gate, w_up, w_down, residual, expert_ids = (
        lax.optimization_barrier(
            (near, far, heads_0, out_next, out_core, w_gate[0], w_up[0], w_down[0], residual, expert_ids)
        )
    )
    far_heads_0 = swap_ctx(heads_0, 6)
    out_both = swap_ctx(out_next, 1)
    gate, up, down = ((v, swap_ctx(v, 1)) for v in (w_gate, w_up, w_down))
    far_res = swap_ctx(lax.dynamic_slice_in_dim(residual, (1 - pair) * 4 * SEG, 4 * SEG, 1), 6)
    ids = expert_ids.T
    far_ids = swap_ctx(ids, 6)
    heads_1 = attention(1, queries, near, far, kv_weight, bias)
    heads_1, gate, up, down, far_res, far_ids, out_both = lax.optimization_barrier(
        (heads_1, gate, up, down, far_res, far_ids, out_both)
    )
    far_heads_1 = swap_ctx(heads_1, 6)

    *own, out_weights = project_first(index, (heads_0, heads_1), (out_weight, out_core, out_next, out_both))
    far_ids, _ = lax.optimization_barrier((far_ids, own[0]))
    place, weight = routing(ids, far_ids, expert_gates.T)
    far_heads_0, far_heads_1, place, weight = lax.optimization_barrier(
        (far_heads_0, far_heads_1, place, weight)
    )
    other = project(index, (far_heads_0, far_heads_1), out_weights)
    own = [own[0]] + [swap_exp(own[m], 4 * m) for m in (1, 2, 3)]
    other = [other[0]] + [swap_exp(other[m], m) for m in (1, 2, 3)]
    own = first_sum(True, index, own)
    own = [own[0]] + [swap_exp(own[m], m) for m in (1, 2, 3)]
    other = first_sum(False, index, other)
    other = [other[0]] + [swap_exp(other[m], 4 * m) for m in (1, 2, 3)]
    gain = norm_gain.reshape(1, D)
    stream_own, stream_far, send = make_stream(index, own + other, residual, far_res, gain, place)

    got = lax.all_to_all(send.reshape(16, 24, SEG), "exp", split_axis=0, concat_axis=0, tiled=True)
    got, stream_far, gate, up, down = lax.optimization_barrier(
        (got.reshape(384, SEG), stream_far, gate, up, down)
    )
    got_1, got_3, got_2 = swap_ctx(got, 2), swap_ctx(got, 6), swap_ctx(got, 4)
    stream_far = swap_ctx(stream_far, 6)
    gate_near, up_near, gate_far, up_far, down = load_weights(index, gate, up, down)
    gate_up, squares = expert_first(index, got, got_1, pick_rows((0, 1)), gain, gate_near, up_near)
    r0, r3, r1, r2 = expert_last(
        index, got_3, got_2, pick_rows((1, 0)), gain, gate_far, up_far, down, gate_up, squares
    )
    back = spread([r0, swap_ctx(r1, 2), swap_ctx(r3, 6), swap_ctx(r2, 4)])
    back, stream_far = lax.optimization_barrier((back, stream_far))
    rows = lax.all_to_all(back.reshape(16, 24, SEG), "exp", split_axis=0, concat_axis=0, tiled=True)
    return combine(index, rows.reshape(384, SEG), weight, stream_own, stream_far)


def solution(mesh):
    placed = (
        P(("ctx", "exp"), None),
        P("ctx", "exp"),
        P(("ctx", "exp"), None),
        P(("ctx", "exp"), None),
        P(),
        P(None, "exp"),
        P("exp", "ctx"),
        P(),
        P(("ctx", "exp"), None),
        P(("ctx", "exp"), None),
        P("exp", None, "ctx"),
        P("exp", None, "ctx"),
        P("exp", "ctx", None),
    )
    return jax.shard_map(
        per_device, mesh=mesh, in_specs=placed, out_specs=P(("ctx", "exp"), None), check_vma=False
    )
```

```python
import functools

import jax
import jax.numpy as jnp
import numpy as np
from jax import lax
from jax.experimental import pallas as pl
from jax.experimental.pallas import tpu as pltpu
from jax.sharding import PartitionSpec as P

NOPE = 128
ROPE = 64
VDIM = 128
LATENT = 512
CAP = 3
D = 7168
EPSILON = 1e-06
HEADS_HERE = 8
ROWS = 256
KEYS = 2048
BLK = 16
SEG = 896
NEG_FILL = -1e30
F32 = jnp.float32
BF16 = jnp.bfloat16
MIB = 1024 * 1024
SMEM = pl.BlockSpec(memory_space=pltpu.SMEM)
VMEM = pl.BlockSpec(memory_space=pltpu.VMEM)


def params(mib):
    return pltpu.CompilerParams(vmem_limit_bytes=mib * MIB)


def whole(shape):
    zeros = (0,) * len(shape)
    return pl.BlockSpec(shape, lambda *_: zeros)


def swap_ctx(value, bits):
    return lax.ppermute(value, "ctx", [(i, i ^ bits) for i in range(8)])


def swap_exp(value, bits):
    return lax.ppermute(value, "exp", [(i, i ^ bits) for i in range(16)])


def swap_plane(value, m, first):
    pairs = []
    for i in range(128):
        along_x = (i // 16 % 2 == 0) == first
        pairs.append((i, i ^ (4 * m if along_x else m)))
    return lax.ppermute(value, ("ctx", "exp"), pairs)


KEY_STEP = 512
LAT_WIDTH = LATENT + 128


def mask_kernel(index_ref, docs_ref, bias):
    y, k = index_ref[4], index_ref[5]
    spot = lax.broadcasted_iota(jnp.int32, (1, KEYS), 1)
    my, e, mk = (spot >> 4) & 3, (spot >> 6) & 15, spot >> 10
    kpos = (((my ^ y) * 2 + (mk ^ k)) * 16 + e) * 16 + (spot & 15)
    first = (y * 2 + k) * ROWS
    row = lax.broadcasted_iota(jnp.int32, (ROWS, ROWS), 0)
    col = lax.broadcasted_iota(jnp.int32, (ROWS, ROWS), 1)
    own = docs_ref[:, pl.ds(pl.multiple_of(first, ROWS), ROWS)]
    own = jnp.sum(jnp.where(row == col, own, 0), axis=1, keepdims=True)
    qlo = jnp.sum((docs_ref[...] < own).astype(jnp.int32), axis=1, keepdims=True)
    qpos = first + lax.broadcasted_iota(jnp.int32, (ROWS, 1), 0)
    allowed = (kpos <= qpos) & (kpos >= qlo)
    bias[...] = jnp.where(allowed, 0.0, NEG_FILL)


def make_mask(index, docs):
    return pl.pallas_call(
        mask_kernel,
        in_specs=[SMEM, VMEM],
        out_specs=VMEM,
        out_shape=jax.ShapeDtypeStruct((ROWS, KEYS), F32),
        compiler_params=params(8),
        cost_estimate=pl.CostEstimate(flops=1000, bytes_accessed=1000, transcendentals=0),
        name="make_mask",
    )(index, docs)


def attention_kernel(q_ref, near_ref, far_ref, w_ref, bias, out_ref, keys, values, scores):
    half = KEYS // 2

    @pl.when(pl.program_id(0) == 0)
    def _():
        for head in range(2):
            keys[head, :half, NOPE:] = near_ref[:, LATENT:LATENT + ROPE]
            keys[head, half:, NOPE:] = far_ref[:, LATENT:LATENT + ROPE]

    log2e = 1.4426950408889634
    factor = (NOPE + ROPE) ** (-0.5) * log2e
    steps = range(KEYS // KEY_STEP)
    for head in range(2):
        cols = slice(head * (NOPE + VDIM), (head + 1) * (NOPE + VDIM))
        for step in steps:
            rows = slice(step * KEY_STEP, (step + 1) * KEY_STEP)
            if step * KEY_STEP < half:
                lat = near_ref[rows, :LATENT]
            else:
                lat = far_ref[step * KEY_STEP - half:(step + 1) * KEY_STEP - half, :LATENT]
            pair = jnp.dot(lat, w_ref[:, cols], preferred_element_type=F32).astype(BF16)
            keys[head, rows, :NOPE] = pair[:, :NOPE]
            values[head, rows, :] = pair[:, NOPE:]
    for head in range(2):
        query = q_ref[:, head * (NOPE + ROPE):(head + 1) * (NOPE + ROPE)]
        peak = None
        for step in steps:
            rows = slice(step * KEY_STEP, (step + 1) * KEY_STEP)
            part = lax.dot_general(query, keys[head, rows, :], (((1,), (1,)), ((), ())),
                                   preferred_element_type=F32)
            part = part * factor + bias[:, rows]
            scores[head, :, rows] = part
            top = jnp.max(part, axis=1, keepdims=True)
            peak = top if peak is None else jnp.maximum(peak, top)
        total = jnp.zeros((ROWS, 1), F32)
        out = jnp.zeros((ROWS, VDIM), F32)
        for step in steps:
            rows = slice(step * KEY_STEP, (step + 1) * KEY_STEP)
            weight = jnp.exp2(scores[head, :, rows] - peak)
            total = total + jnp.sum(weight, axis=1, keepdims=True)
            out = out + jnp.dot(weight.astype(BF16), values[head, rows, :], preferred_element_type=F32)
        out_ref[:, head * VDIM:(head + 1) * VDIM] = (out / total).astype(BF16)


def attention(part, query, near, far, weight, bias):
    pairs = HEADS_HERE // 4
    first = part * pairs
    return pl.pallas_call(
        attention_kernel,
        grid=(pairs,),
        in_specs=[
            pl.BlockSpec((ROWS, 2 * (NOPE + ROPE)), lambda h: (0, first + h)),
            VMEM,
            VMEM,
            pl.BlockSpec((LATENT, 2 * (NOPE + VDIM)), lambda h: (0, first + h)),
            VMEM,
        ],
        out_specs=pl.BlockSpec((ROWS, 2 * VDIM), lambda h: (0, h)),
        scratch_shapes=[
            pltpu.VMEM((2, KEYS, NOPE + ROPE), BF16),
            pltpu.VMEM((2, KEYS, VDIM), BF16),
            pltpu.VMEM((2, ROWS, KEYS), F32),
        ],
        out_shape=jax.ShapeDtypeStruct((ROWS, pairs * 2 * VDIM), BF16),
        compiler_params=params(24),
        cost_estimate=pl.CostEstimate(flops=1000, bytes_accessed=1000, transcendentals=0),
        name="attention",
    )(query, near, far, weight, bias)


HALF = HEADS_HERE * VDIM // 2


def load_out_kernel(w0, w1, w2, w3, w4, w5, kept, sems):
    top, low = pl.ds(0, HALF), pl.ds(HALF, HALF)
    targets = (kept.at[0], kept.at[1], kept.at[2, top], kept.at[2, low], kept.at[3, top], kept.at[3, low])
    copies = [
        pltpu.make_async_copy(w, target, sems.at[i])
        for i, (w, target) in enumerate(zip((w0, w1, w2, w3, w4, w5), targets))
    ]
    for copy in copies:
        copy.start()
    for copy in copies:
        copy.wait()


def load_out(weights):
    return pl.pallas_call(
        load_out_kernel,
        in_specs=[pl.BlockSpec(memory_space=pl.ANY)] * 6,
        out_specs=VMEM,
        scratch_shapes=[pltpu.SemaphoreType.DMA((6,))],
        out_shape=jax.ShapeDtypeStruct((4, 2 * HALF, SEG), BF16),
        compiler_params=params(8),
        cost_estimate=pl.CostEstimate(flops=1000, bytes_accessed=1000, transcendentals=0),
        name="load_out",
    )(*weights)


def project_kernel(steps, widths, index_ref, h0, h1, h2, h3, kept, *refs):
    outs, left = refs[:-1], refs[-1]
    x, z, k = index_ref[0], index_ref[1], index_ref[5]
    heads = (h0, h1, h2, h3)
    for i, m in enumerate(steps):
        for n in range(4):
            first = (1 - k) * ((x ^ m) * 64 + n * 16) + k * (n * 64 + (z ^ m) * 16)
            first = pl.multiple_of(first, 16)
            for block in range(2):
                start = i * 128 + block * 64 + n * 16
                for half in range(2):
                    cols = slice(half * HALF, (half + 1) * HALF)
                    left[start:start + 16, cols] = heads[block * 2 + half][pl.ds(first, 16), :]
    count = 4 // widths
    for seg in range(4):
        part = jnp.dot(left[...], kept[seg], preferred_element_type=F32).astype(BF16)
        for i in range(len(steps)):
            out = outs[i * count + seg // widths]
            cols = slice(seg % widths * SEG, (seg % widths + 1) * SEG)
            out[:, cols] = part[i * 128:(i + 1) * 128, :]


def project(steps, widths, index, heads, kept):
    piece = jax.ShapeDtypeStruct((128, widths * SEG), BF16)
    count = len(steps) * (4 // widths)
    return pl.pallas_call(
        functools.partial(project_kernel, steps, widths),
        in_specs=[SMEM] + [VMEM] * 5,
        out_specs=[VMEM] * count,
        scratch_shapes=[pltpu.VMEM((128 * len(steps), 2 * HALF), BF16)],
        out_shape=[piece] * count,
        compiler_params=params(16),
        cost_estimate=pl.CostEstimate(flops=1000, bytes_accessed=1000, transcendentals=0),
        name="project",
    )(index, *heads, kept)


def add_halves_kernel(p1, p3, from_1, from_3, o1, o3):
    half = 2 * SEG
    o1[:, :half] = p1[:, :half]
    o1[:, half:] = (p1[:, half:].astype(F32) + from_3[...].astype(F32)).astype(BF16)
    o3[:, :half] = (p3[:, :half].astype(F32) + from_1[...].astype(F32)).astype(BF16)
    o3[:, half:] = p3[:, half:]


def add_halves(p1, p3, from_1, from_3):
    return pl.pallas_call(
        add_halves_kernel,
        in_specs=[VMEM] * 4,
        out_specs=[VMEM] * 2,
        out_shape=[jax.ShapeDtypeStruct(p1.shape, BF16)] * 2,
        compiler_params=params(8),
        cost_estimate=pl.CostEstimate(flops=1000, bytes_accessed=1000, transcendentals=0),
        name="add_halves",
    )(p1, p3, from_1, from_3)


def first_sum_kernel(index_ref, i0, i1, i3, *outs):
    k = index_ref[5]
    spot = (1 - k) * index_ref[1] + k * index_ref[0]
    for m, out in enumerate(outs):
        for block in range(2):
            rows = pl.ds(pl.multiple_of(block * 64 + (spot ^ m) * 16, 16), 16)
            total = i0[rows, :].astype(F32)
            for ref in (i1, i3):
                total = total + ref[rows, :].astype(F32)
            out[block * 16:(block + 1) * 16, :] = total.astype(BF16)


def first_sum(index, pieces):
    out = jax.ShapeDtypeStruct((32, 4 * SEG), BF16)
    return pl.pallas_call(
        first_sum_kernel,
        in_specs=[SMEM] + [VMEM] * 3,
        out_specs=[VMEM] * 4,
        out_shape=[out] * 4,
        compiler_params=params(12),
        cost_estimate=pl.CostEstimate(flops=1000, bytes_accessed=1000, transcendentals=0),
        name="first_sum",
    )(index, *pieces)


def stream_kernel(index_ref, *refs):
    sums, (res, far_res, gain, place, stream_own, stream_far, send, stack) = refs[:4], refs[4:]
    spot, base = index_ref[2], index_ref[3] * 4
    for i in range(4):
        seg = spot ^ i
        cols = slice(i * SEG, (i + 1) * SEG)
        wide = pl.ds(pl.multiple_of((base + seg) * SEG, 128), SEG)
        near = pl.ds(pl.multiple_of(seg * SEG, 128), SEG)
        for block, start, stream in ((0, res[:, wide], stream_own), (1, far_res[:, near], stream_far)):
            total = start.astype(F32)
            for ref in sums:
                total = total + ref[block * 16:(block + 1) * 16, cols].astype(F32)
            stream[seg] = total.astype(stream.dtype)
            first = pl.multiple_of(seg * 32 + block * 16, 16)
            stack[pl.ds(first, 16), :] = (total * gain[:, wide]).astype(BF16)
    send[...] = jnp.dot(place[...], stack[...], preferred_element_type=F32).astype(BF16)


def make_stream(index, sums, res, far_res, gain, place):
    return pl.pallas_call(
        stream_kernel,
        in_specs=[SMEM] + [VMEM] * 8,
        out_specs=[VMEM] * 3,
        scratch_shapes=[pltpu.VMEM((128, SEG), BF16)],
        out_shape=[
            jax.ShapeDtypeStruct((4, 16, SEG), F32),
            jax.ShapeDtypeStruct((4, 16, SEG), BF16),
            jax.ShapeDtypeStruct((384, SEG), BF16),
        ],
        compiler_params=params(12),
        cost_estimate=pl.CostEstimate(flops=1000, bytes_accessed=1000, transcendentals=0),
        name="make_stream",
    )(index, *sums, res, far_res, gain, place)


def one_hot(values, count):
    return (np.asarray(values)[:, None] == np.arange(count)[None, :]).astype(np.float32)


def routing_tables():
    row, col = np.arange(384), np.arange(128)
    to_expert = one_hot(row // 24, 16)
    to_token = one_hot(col % 16, 16).T
    segment = (row // 6 % 4)[:, None] == (col // 32)[None, :]
    block = (row // 3 % 2)[:, None] == (col // 16 % 2)[None, :]
    kept = np.stack([segment & block & (col // 16 % 2 == b)[None, :] for b in range(2)])
    slot = (row % 3).astype(np.float32)[:, None]
    return_kept = (col // 16)[:, None] == (row % 8)[None, :]
    return_slot = (row // 8 % 3).astype(np.float32)[None, :]
    return [
        jnp.asarray(to_expert, BF16), jnp.asarray(to_token, BF16), jnp.asarray(kept, F32),
        jnp.asarray(slot, F32), jnp.asarray(return_kept, F32), jnp.asarray(return_slot, F32),
    ]


def routing_kernel(ids_ref, far_ref, gates_ref, to_expert, to_token, kept, slot, return_kept, return_slot,
                   place, weight):
    expert = lax.broadcasted_iota(jnp.int32, (16, 16), 0)
    token = lax.broadcasted_iota(jnp.int32, (16, 16), 1)
    earlier = (expert < token).astype(BF16)

    def spots(ids):
        named = jnp.zeros((16, 16), F32)
        for j in range(8):
            named = jnp.maximum(named, (ids[j:j + 1, :] == expert).astype(F32))
        rank = jnp.dot(named.astype(BF16), earlier, preferred_element_type=F32)
        return jnp.where(named > 0.0, rank, -1.0).astype(BF16)

    same = (expert == token).astype(BF16)
    far_ids = lax.dot_general(
        far_ref[:, 4 * SEG:4 * SEG + 128], same, (((0,), (0,)), ((), ())), preferred_element_type=F32
    )
    by_block = [spots(ids_ref[...]), spots(far_ids[:8].astype(jnp.int32))]
    total = jnp.zeros((384, 128), F32)
    for block in range(2):
        wide = jnp.dot(to_expert[...], by_block[block], preferred_element_type=F32)
        wide = jnp.dot(wide.astype(BF16), to_token[...], preferred_element_type=F32)
        total = total + jnp.where(wide == slot[...], kept[block], 0.0)
    place[...] = total.astype(BF16)

    def spread_out(value):
        tall = lax.dot_general(to_token[...], value, (((0,), (1,)), ((), ())), preferred_element_type=F32)
        return lax.dot_general(tall.astype(BF16), to_expert[...], (((1,), (1,)), ((), ())),
                               preferred_element_type=F32)

    live = jnp.where(spread_out(by_block[0]) == return_slot[...], return_kept[...], 0.0)
    route = jnp.zeros((16, 16), F32)
    for j in range(8):
        route = route + jnp.where(ids_ref[j:j + 1, :] == expert, gates_ref[j:j + 1, :], 0.0)
    for i in range(3):
        part = route.astype(BF16)
        weight[i] = (spread_out(part) * live).astype(BF16)
        route = route - part.astype(F32)


def routing(ids, letter, gates):
    tables = routing_tables()
    return pl.pallas_call(
        routing_kernel,
        in_specs=[VMEM] * 9,
        out_specs=[VMEM] * 2,
        out_shape=[jax.ShapeDtypeStruct((384, 128), BF16), jax.ShapeDtypeStruct((3, 128, 384), BF16)],
        compiler_params=params(8),
        cost_estimate=pl.CostEstimate(flops=1000, bytes_accessed=1000, transcendentals=0),
        name="routing",
    )(ids, letter, gates, *tables)


def pick_rows(order):
    matrix = np.zeros((4, 96, 384), np.float32)
    for q in range(4):
        for block in range(2):
            for e in range(16):
                for s in range(CAP):
                    matrix[q, block * 48 + e * 3 + s, e * 24 + q * 6 + order[block] * 3 + s] = 1.0
    return jnp.asarray(matrix.reshape(384, 384), BF16)


def up_part(base, pick_ref, inputs, gain_ref, gate_ref, up_ref, rows):
    squares = jnp.zeros((192, 1), F32)
    for i, ref in enumerate(inputs):
        moved = jnp.dot(pick_ref[...], ref[...], preferred_element_type=F32)
        for q in range(4):
            part = moved[q * 96:(q + 1) * 96]
            rows[i * 96:(i + 1) * 96, q * SEG:(q + 1) * SEG] = part.astype(BF16)
    for q in range(4):
        part = rows[:, q * SEG:(q + 1) * SEG].astype(F32)
        gain = gain_ref[:, pl.ds(pl.multiple_of((base * 4 + q) * SEG, 128), SEG)]
        squares = squares + jnp.sum(part * part * (1.0 / (gain * gain)), axis=1, keepdims=True)
    parts = [
        jnp.dot(rows[...], ref[core], preferred_element_type=F32)
        for ref in (gate_ref, up_ref) for core in range(2)
    ]
    return parts, squares


def load_kernel(index_ref, g0, g1, u0, u1, d0, d1, gate_near, up_near, gate_far, up_far, down, sems):
    base = index_ref[3]
    depth = 4 * SEG
    copies = []
    for outs, half in (((gate_near, up_near), base), ((gate_far, up_far), 1 - base)):
        rows = pl.ds(pl.multiple_of(half * depth, depth), depth)
        for out, refs in zip(outs, ((g0, g1), (u0, u1))):
            for core in range(2):
                copies.append((refs[core].at[rows], out.at[core]))
    copies += [(d0, down.at[0]), (d1, down.at[1])]
    copies = [pltpu.make_async_copy(a, b, sems.at[i]) for i, (a, b) in enumerate(copies)]
    for copy in copies:
        copy.start()
    for copy in copies:
        copy.wait()


def load_weights(index, gate, up, down):
    half = jax.ShapeDtypeStruct((2, 4 * SEG, 256), BF16)
    return pl.pallas_call(
        load_kernel,
        in_specs=[SMEM] + [pl.BlockSpec(memory_space=pl.ANY)] * 6,
        out_specs=[VMEM] * 5,
        scratch_shapes=[pltpu.SemaphoreType.DMA((10,))],
        out_shape=[half] * 4 + [jax.ShapeDtypeStruct((2, 256, D), BF16)],
        compiler_params=params(30),
        cost_estimate=pl.CostEstimate(flops=1000, bytes_accessed=1000, transcendentals=0),
        name="load_weights",
    )(index, *gate, *up, *down)


def expert_first_kernel(index_ref, x0, x1, pick_ref, gain_ref, gate_ref, up_ref, gate_up, squares, rows):
    parts, total = up_part(index_ref[3], pick_ref, (x0, x1), gain_ref, gate_ref, up_ref, rows)
    for i, part in enumerate(parts):
        gate_up[:, i * 256:(i + 1) * 256] = part
    squares[...] = total


def expert_first(index, x0, x1, pick, gain, gate, up):
    return pl.pallas_call(
        expert_first_kernel,
        in_specs=[SMEM] + [VMEM] * 6,
        out_specs=[VMEM] * 2,
        scratch_shapes=[pltpu.VMEM((192, 4 * SEG), BF16)],
        out_shape=[jax.ShapeDtypeStruct((192, 1024), F32), jax.ShapeDtypeStruct((192, 1), F32)],
        compiler_params=params(16),
        cost_estimate=pl.CostEstimate(flops=1000, bytes_accessed=1000, transcendentals=0),
        name="expert_first",
    )(index, x0, x1, pick, gain, gate, up)


def expert_last_kernel(index_ref, x0, x1, pick_ref, gain_ref, gate_ref, up_ref, down_ref, before, squares_before,
                       r0, r1, r2, r3, rows, hidden):
    parts, total = up_part(1 - index_ref[3], pick_ref, (x0, x1), gain_ref, gate_ref, up_ref, rows)
    scale = lax.rsqrt((total + squares_before[...]) * (1.0 / D) + EPSILON)
    for core in range(2):
        gate = (parts[core] + before[:, core * 256:(core + 1) * 256]) * scale
        up = (parts[2 + core] + before[:, 512 + core * 256:512 + (core + 1) * 256]) * scale
        hidden[:, core * 256:(core + 1) * 256] = (gate / (1.0 + jnp.exp(-gate)) * up).astype(BF16)
    for q in range(4):
        cols = slice(q * 2 * SEG, (q + 1) * 2 * SEG)
        out = jnp.dot(hidden[:, :256], down_ref[0, :, cols], preferred_element_type=F32)
        out = out + jnp.dot(hidden[:, 256:], down_ref[1, :, cols], preferred_element_type=F32)
        out = out.astype(BF16)
        for i, ref in enumerate((r0, r1, r2, r3)):
            ref[:, cols] = out[i * 48:(i + 1) * 48]


def expert_last(index, x0, x1, pick, gain, gate, up, down, before, squares_before):
    return pl.pallas_call(
        expert_last_kernel,
        in_specs=[SMEM] + [VMEM] * 9,
        out_specs=[VMEM] * 4,
        scratch_shapes=[pltpu.VMEM((192, 4 * SEG), BF16), pltpu.VMEM((192, 512), BF16)],
        out_shape=[jax.ShapeDtypeStruct((48, D), BF16)] * 4,
        compiler_params=params(16),
        cost_estimate=pl.CostEstimate(flops=1000, bytes_accessed=1000, transcendentals=0),
        name="expert_last",
    )(index, x0, x1, pick, gain, gate, up, down, before, squares_before)


def spread_kernel(p0, p1, p2, p3, out):
    total = p0[...].astype(F32)
    for ref in (p1, p2, p3):
        total = total + ref[...].astype(F32)
    total = total.astype(BF16)
    stack = jnp.concatenate([total[:, q * SEG:(q + 1) * SEG] for q in range(8)], axis=0)
    row = lax.broadcasted_iota(jnp.int32, (384, 384), 0)
    col = lax.broadcasted_iota(jnp.int32, (384, 384), 1)
    move = (row == (col % 48) * 8 + col // 48).astype(BF16)
    out[...] = jnp.dot(move, stack, preferred_element_type=F32).astype(BF16)


def spread(parts):
    return pl.pallas_call(
        spread_kernel,
        out_shape=jax.ShapeDtypeStruct((384, SEG), BF16),
        compiler_params=params(24),
        cost_estimate=pl.CostEstimate(flops=1000, bytes_accessed=1000, transcendentals=0),
        name="spread",
    )(*parts)


def combine_kernel(index_ref, rows, weight, stream_own, stream_far, out, routed):
    total = jnp.dot(weight[0], rows[...], preferred_element_type=F32)
    for i in (1, 2):
        total = total + jnp.dot(weight[i], rows[...], preferred_element_type=F32)
    routed[...] = total
    pair = index_ref[3]
    for q in range(4):
        for side, stream in ((pair, stream_own), (1 - pair, stream_far)):
            seg = side * 4 + q
            picked = routed[pl.ds(pl.multiple_of(seg * 16, 16), 16), :]
            out[:, pl.ds(pl.multiple_of(seg * SEG, 128), SEG)] = (picked + stream[q].astype(F32)).astype(BF16)


def combine(index, rows, weight, stream_own, stream_far):
    return pl.pallas_call(
        combine_kernel,
        in_specs=[SMEM] + [VMEM] * 4,
        out_specs=VMEM,
        scratch_shapes=[pltpu.VMEM((128, SEG), F32)],
        out_shape=jax.ShapeDtypeStruct((16, D), BF16),
        compiler_params=params(12),
        cost_estimate=pl.CostEstimate(flops=1000, bytes_accessed=1000, transcendentals=0),
        name="combine",
    )(index, rows, weight, stream_own, stream_far)


def per_device(residual, queries, latent, key_rope, doc_ids, kv_weight, out_weight, norm_gain,
               expert_ids, expert_gates, w_gate, w_up, w_down):
    c = lax.axis_index("ctx")
    e = lax.axis_index("exp")
    y, k, x, z = c >> 1, c & 1, e >> 2, e & 3
    pair = y >> 1
    index = jnp.stack([x, z, c & 3, pair, y, k]).astype(jnp.int32)

    far_start = (1 - pair) * (4 * SEG)

    lat = jnp.concatenate(
        [latent, key_rope, jnp.zeros((BLK, LAT_WIDTH - LATENT - ROPE), BF16)], axis=1
    )
    lat = jnp.concatenate([lat] + [swap_ctx(lat, 2 * m) for m in (1, 2, 3)], axis=0)
    out_top, out_low = out_weight[:HALF], out_weight[HALF:]
    lat, out_top, out_low, out_weight, doc_ids, w_gate, w_up, w_down, index = lax.optimization_barrier(
        (lat, out_top, out_low, out_weight, doc_ids, w_gate[0], w_up[0], w_down[0], index)
    )
    next_top = swap_ctx(out_top, 2)
    gate, up, down = ((v, swap_ctx(v, 1)) for v in (w_gate, w_up, w_down))
    near = lax.all_to_all(
        jnp.broadcast_to(lat[None], (16,) + lat.shape), "exp", split_axis=0, concat_axis=0, tiled=True
    ).reshape(16 * lat.shape[0], LAT_WIDTH)
    near, next_top, out_weight, doc_ids, gate, up, down = lax.optimization_barrier(
        (near, next_top, out_weight, doc_ids, gate, up, down)
    )
    far = swap_ctx(near, 1)
    bias = make_mask(index, doc_ids.reshape(1, KEYS))
    next_low = swap_ctx(out_low, 2)
    out_core = swap_ctx(out_weight, 1)
    near, far, bias = lax.optimization_barrier((near, far, bias))

    heads_0 = attention(0, queries, near, far, kv_weight, bias)
    near, far, heads_0, out_core = lax.optimization_barrier((near, far, heads_0, out_core))
    far_heads_0 = swap_ctx(heads_0, 6)
    both_top = swap_ctx(next_top, 1)
    heads_1 = attention(1, queries, near, far, kv_weight, bias)
    far_heads_1 = swap_ctx(heads_1, 6)
    both_top, next_low, far_heads_0, residual, expert_ids, _ = lax.optimization_barrier(
        (both_top, next_low, far_heads_0, residual, expert_ids, heads_1)
    )
    both_low = swap_ctx(next_low, 1)

    ids = jnp.concatenate([expert_ids.astype(BF16), jnp.zeros((BLK, 120), BF16)], axis=1)
    part = lax.dynamic_slice_in_dim(residual, far_start, 4 * SEG, 1)
    letter = swap_ctx(jnp.concatenate([part, ids], axis=1), 6)

    kept = load_out((out_weight, out_core, next_top, next_low, both_top, both_low))
    far_heads_0, far_heads_1, kept = lax.optimization_barrier((far_heads_0, far_heads_1, kept))
    heads = (heads_0, heads_1, far_heads_0, far_heads_1)
    left, right = project((2,), 2, index, heads, kept)
    from_1, from_3 = swap_plane(left, 1, True), swap_plane(right, 3, True)
    kept, _ = lax.optimization_barrier((kept, left))
    p0, p1, p3 = project((0, 1, 3), 4, index, heads, kept)
    p1, p3 = add_halves(p1, p3, from_1, from_3)
    letter, _ = lax.optimization_barrier((letter, p1))
    place, weight = routing(expert_ids.T, letter, expert_gates.T)
    pieces = [p0, swap_plane(p1, 1, True), swap_plane(p3, 3, True)]
    pieces, place, weight = lax.optimization_barrier((pieces, place, weight))
    sums = first_sum(index, pieces)
    sums = [sums[0]] + [swap_plane(sums[m], m, False) for m in (1, 2, 3)]
    gain = norm_gain.reshape(1, D)
    stream_own, stream_far, send = make_stream(index, sums, residual, letter, gain, place)

    got = lax.all_to_all(send.reshape(16, 24, SEG), "exp", split_axis=0, concat_axis=0, tiled=True)
    got, stream_far, gate, up, down = lax.optimization_barrier(
        (got.reshape(384, SEG), stream_far, gate, up, down)
    )
    got_1, got_3, got_2 = swap_ctx(got, 2), swap_ctx(got, 6), swap_ctx(got, 4)
    stream_far = swap_ctx(stream_far, 6)
    gate_near, up_near, gate_far, up_far, down = load_weights(index, gate, up, down)
    gate_up, squares = expert_first(index, got, got_1, pick_rows((0, 1)), gain, gate_near, up_near)
    r0, r3, r1, r2 = expert_last(
        index, got_3, got_2, pick_rows((1, 0)), gain, gate_far, up_far, down, gate_up, squares
    )
    back = spread([r0, swap_ctx(r1, 2), swap_ctx(r3, 6), swap_ctx(r2, 4)])
    back, stream_far = lax.optimization_barrier((back, stream_far))
    rows = lax.all_to_all(back.reshape(16, 24, SEG), "exp", split_axis=0, concat_axis=0, tiled=True)
    return combine(index, rows.reshape(384, SEG), weight, stream_own, stream_far)


def solution(mesh):
    placed = (
        P(("ctx", "exp"), None),
        P("ctx", "exp"),
        P(("ctx", "exp"), None),
        P(("ctx", "exp"), None),
        P(),
        P(None, "exp"),
        P("exp", "ctx"),
        P(),
        P(("ctx", "exp"), None),
        P(("ctx", "exp"), None),
        P("exp", None, "ctx"),
        P("exp", None, "ctx"),
        P("exp", "ctx", None),
    )
    return jax.shard_map(
        per_device, mesh=mesh, in_specs=placed, out_specs=P(("ctx", "exp"), None), check_vma=False
    )
```

```python
import functools

import jax
import jax.numpy as jnp
import numpy as np
from jax import lax
from jax.experimental import pallas as pl
from jax.experimental.pallas import tpu as pltpu
from jax.sharding import PartitionSpec as P

NOPE = 128
ROPE = 64
VDIM = 128
LATENT = 512
CAP = 3
D = 7168
EPSILON = 1e-06
HEADS_HERE = 8
ROWS = 256
KEYS = 2048
BLK = 16
SEG = 896
NEG_FILL = -1e30
F32 = jnp.float32
BF16 = jnp.bfloat16
MIB = 1024 * 1024
SMEM = pl.BlockSpec(memory_space=pltpu.SMEM)
VMEM = pl.BlockSpec(memory_space=pltpu.VMEM)


def params(mib):
    return pltpu.CompilerParams(vmem_limit_bytes=mib * MIB)


def whole(shape):
    zeros = (0,) * len(shape)
    return pl.BlockSpec(shape, lambda *_: zeros)


def swap_ctx(value, bits):
    return lax.ppermute(value, "ctx", [(i, i ^ bits) for i in range(8)])


def swap_exp(value, bits):
    return lax.ppermute(value, "exp", [(i, i ^ bits) for i in range(16)])


def swap_plane(value, m, first):
    pairs = []
    for i in range(128):
        along_x = (i // 16 % 2 == 0) == first
        pairs.append((i, i ^ (4 * m if along_x else m)))
    return lax.ppermute(value, ("ctx", "exp"), pairs)


KEY_STEP = 512
LAT_WIDTH = LATENT + 128


def mask_kernel(index_ref, docs_ref, bias):
    y, k = index_ref[4], index_ref[5]
    spot = lax.broadcasted_iota(jnp.int32, (1, KEYS), 1)
    my, e, mk = (spot >> 4) & 3, (spot >> 6) & 15, spot >> 10
    kpos = (((my ^ y) * 2 + (mk ^ k)) * 16 + e) * 16 + (spot & 15)
    first = (y * 2 + k) * ROWS
    row = lax.broadcasted_iota(jnp.int32, (ROWS, ROWS), 0)
    col = lax.broadcasted_iota(jnp.int32, (ROWS, ROWS), 1)
    own = docs_ref[:, pl.ds(pl.multiple_of(first, ROWS), ROWS)]
    own = jnp.sum(jnp.where(row == col, own, 0), axis=1, keepdims=True)
    qlo = jnp.sum((docs_ref[...] < own).astype(jnp.int32), axis=1, keepdims=True)
    qpos = first + lax.broadcasted_iota(jnp.int32, (ROWS, 1), 0)
    allowed = (kpos <= qpos) & (kpos >= qlo)
    bias[...] = jnp.where(allowed, 0.0, NEG_FILL)


def make_mask(index, docs):
    return pl.pallas_call(
        mask_kernel,
        in_specs=[SMEM, VMEM],
        out_specs=VMEM,
        out_shape=jax.ShapeDtypeStruct((ROWS, KEYS), F32),
        compiler_params=params(8),
        cost_estimate=pl.CostEstimate(flops=1000, bytes_accessed=1000, transcendentals=0),
        name="make_mask",
    )(index, docs)


def attention_kernel(q_ref, near_ref, far_ref, w_ref, bias, out_ref, keys, values, scores):
    half = KEYS // 2

    @pl.when(pl.program_id(0) == 0)
    def _():
        for head in range(2):
            keys[head, :half, NOPE:] = near_ref[:, LATENT:LATENT + ROPE]
            keys[head, half:, NOPE:] = far_ref[:, LATENT:LATENT + ROPE]

    log2e = 1.4426950408889634
    factor = (NOPE + ROPE) ** (-0.5) * log2e
    steps = range(KEYS // KEY_STEP)
    for head in range(2):
        cols = slice(head * (NOPE + VDIM), (head + 1) * (NOPE + VDIM))
        for step in steps:
            rows = slice(step * KEY_STEP, (step + 1) * KEY_STEP)
            if step * KEY_STEP < half:
                lat = near_ref[rows, :LATENT]
            else:
                lat = far_ref[step * KEY_STEP - half:(step + 1) * KEY_STEP - half, :LATENT]
            pair = jnp.dot(lat, w_ref[:, cols], preferred_element_type=F32).astype(BF16)
            keys[head, rows, :NOPE] = pair[:, :NOPE]
            values[head, rows, :] = pair[:, NOPE:]
    for head in range(2):
        query = q_ref[:, head * (NOPE + ROPE):(head + 1) * (NOPE + ROPE)]
        peak = None
        for step in steps:
            rows = slice(step * KEY_STEP, (step + 1) * KEY_STEP)
            part = lax.dot_general(query, keys[head, rows, :], (((1,), (1,)), ((), ())),
                                   preferred_element_type=F32)
            part = part * factor + bias[:, rows]
            scores[head, :, rows] = part
            top = jnp.max(part, axis=1, keepdims=True)
            peak = top if peak is None else jnp.maximum(peak, top)
        total = jnp.zeros((ROWS, 1), F32)
        out = jnp.zeros((ROWS, VDIM), F32)
        for step in steps:
            rows = slice(step * KEY_STEP, (step + 1) * KEY_STEP)
            weight = jnp.exp2(scores[head, :, rows] - peak)
            total = total + jnp.sum(weight, axis=1, keepdims=True)
            out = out + jnp.dot(weight.astype(BF16), values[head, rows, :], preferred_element_type=F32)
        out_ref[:, head * VDIM:(head + 1) * VDIM] = (out / total).astype(BF16)


def attention(part, query, near, far, weight, bias):
    pairs = HEADS_HERE // 4
    first = part * pairs
    return pl.pallas_call(
        attention_kernel,
        grid=(pairs,),
        in_specs=[
            pl.BlockSpec((ROWS, 2 * (NOPE + ROPE)), lambda h: (0, first + h)),
            VMEM,
            VMEM,
            pl.BlockSpec((LATENT, 2 * (NOPE + VDIM)), lambda h: (0, first + h)),
            VMEM,
        ],
        out_specs=pl.BlockSpec((ROWS, 2 * VDIM), lambda h: (0, h)),
        scratch_shapes=[
            pltpu.VMEM((2, KEYS, NOPE + ROPE), BF16),
            pltpu.VMEM((2, KEYS, VDIM), BF16),
            pltpu.VMEM((2, ROWS, KEYS), F32),
        ],
        out_shape=jax.ShapeDtypeStruct((ROWS, pairs * 2 * VDIM), BF16),
        compiler_params=params(24),
        cost_estimate=pl.CostEstimate(flops=1000, bytes_accessed=1000, transcendentals=0),
        name="attention",
    )(query, near, far, weight, bias)


HALF = HEADS_HERE * VDIM // 2


def load_out_kernel(w0, w1, w2, w3, w4, w5, kept, sems):
    top, low = pl.ds(0, HALF), pl.ds(HALF, HALF)
    targets = (kept.at[0], kept.at[1], kept.at[2, top], kept.at[2, low], kept.at[3, top], kept.at[3, low])
    copies = [
        pltpu.make_async_copy(w, target, sems.at[i])
        for i, (w, target) in enumerate(zip((w0, w1, w2, w3, w4, w5), targets))
    ]
    for copy in copies:
        copy.start()
    for copy in copies:
        copy.wait()


def load_out(weights):
    return pl.pallas_call(
        load_out_kernel,
        in_specs=[pl.BlockSpec(memory_space=pl.ANY)] * 6,
        out_specs=VMEM,
        scratch_shapes=[pltpu.SemaphoreType.DMA((6,))],
        out_shape=jax.ShapeDtypeStruct((4, 2 * HALF, SEG), BF16),
        compiler_params=params(8),
        cost_estimate=pl.CostEstimate(flops=1000, bytes_accessed=1000, transcendentals=0),
        name="load_out",
    )(*weights)


def project_kernel(steps, widths, index_ref, h0, h1, h2, h3, kept, *refs):
    outs, left = refs[:-1], refs[-1]
    x, z, k = index_ref[0], index_ref[1], index_ref[5]
    heads = (h0, h1, h2, h3)
    for i, m in enumerate(steps):
        for n in range(4):
            first = (1 - k) * ((x ^ m) * 64 + n * 16) + k * (n * 64 + (z ^ m) * 16)
            first = pl.multiple_of(first, 16)
            for block in range(2):
                start = i * 128 + block * 64 + n * 16
                for half in range(2):
                    cols = slice(half * HALF, (half + 1) * HALF)
                    left[start:start + 16, cols] = heads[block * 2 + half][pl.ds(first, 16), :]
    count = 4 // widths
    for seg in range(4):
        part = jnp.dot(left[...], kept[seg], preferred_element_type=F32).astype(BF16)
        for i in range(len(steps)):
            out = outs[i * count + seg // widths]
            cols = slice(seg % widths * SEG, (seg % widths + 1) * SEG)
            out[:, cols] = part[i * 128:(i + 1) * 128, :]


def project(steps, widths, index, heads, kept):
    piece = jax.ShapeDtypeStruct((128, widths * SEG), BF16)
    count = len(steps) * (4 // widths)
    return pl.pallas_call(
        functools.partial(project_kernel, steps, widths),
        in_specs=[SMEM] + [VMEM] * 5,
        out_specs=[VMEM] * count,
        scratch_shapes=[pltpu.VMEM((128 * len(steps), 2 * HALF), BF16)],
        out_shape=[piece] * count,
        compiler_params=params(16),
        cost_estimate=pl.CostEstimate(flops=1000, bytes_accessed=1000, transcendentals=0),
        name="project",
    )(index, *heads, kept)


def add_halves_kernel(p1, p3, from_1, from_3, o1, o3):
    half = p1.shape[1] // 2
    o1[:, :half] = p1[:, :half]
    o1[:, half:] = (p1[:, half:].astype(F32) + from_3[...].astype(F32)).astype(BF16)
    o3[:, :half] = (p3[:, :half].astype(F32) + from_1[...].astype(F32)).astype(BF16)
    o3[:, half:] = p3[:, half:]


def add_halves(p1, p3, from_1, from_3):
    return pl.pallas_call(
        add_halves_kernel,
        in_specs=[VMEM] * 4,
        out_specs=[VMEM] * 2,
        out_shape=[jax.ShapeDtypeStruct(p1.shape, BF16)] * 2,
        compiler_params=params(8),
        cost_estimate=pl.CostEstimate(flops=1000, bytes_accessed=1000, transcendentals=0),
        name="add_halves",
    )(p1, p3, from_1, from_3)


def first_sum_kernel(index_ref, i0, i1, i3, *outs):
    k = index_ref[5]
    spot = (1 - k) * index_ref[1] + k * index_ref[0]
    for m, out in enumerate(outs):
        for block in range(2):
            rows = pl.ds(pl.multiple_of(block * 64 + (spot ^ m) * 16, 16), 16)
            total = i0[rows, :].astype(F32)
            for ref in (i1, i3):
                total = total + ref[rows, :].astype(F32)
            out[block * 16:(block + 1) * 16, :] = total.astype(BF16)


def first_sum(index, pieces):
    out = jax.ShapeDtypeStruct((32, 4 * SEG), BF16)
    return pl.pallas_call(
        first_sum_kernel,
        in_specs=[SMEM] + [VMEM] * 3,
        out_specs=[VMEM] * 4,
        out_shape=[out] * 4,
        compiler_params=params(12),
        cost_estimate=pl.CostEstimate(flops=1000, bytes_accessed=1000, transcendentals=0),
        name="first_sum",
    )(index, *pieces)


def stream_kernel(index_ref, *refs):
    sums, (res, far_res, gain, place, stream_own, stream_far, send, stack) = refs[:4], refs[4:]
    spot, base = index_ref[2], index_ref[3] * 4
    for i in range(4):
        seg = spot ^ i
        cols = slice(i * SEG, (i + 1) * SEG)
        wide = pl.ds(pl.multiple_of((base + seg) * SEG, 128), SEG)
        near = pl.ds(pl.multiple_of(seg * SEG, 128), SEG)
        for block, start, stream in ((0, res[:, wide], stream_own), (1, far_res[:, near], stream_far)):
            total = start.astype(F32)
            for ref in sums:
                total = total + ref[block * 16:(block + 1) * 16, cols].astype(F32)
            stream[seg] = total.astype(stream.dtype)
            first = pl.multiple_of(seg * 32 + block * 16, 16)
            stack[pl.ds(first, 16), :] = (total * gain[:, wide]).astype(BF16)
    send[...] = jnp.dot(place[...], stack[...], preferred_element_type=F32).astype(BF16)


def make_stream(index, sums, res, far_res, gain, place):
    return pl.pallas_call(
        stream_kernel,
        in_specs=[SMEM] + [VMEM] * 8,
        out_specs=[VMEM] * 3,
        scratch_shapes=[pltpu.VMEM((128, SEG), BF16)],
        out_shape=[
            jax.ShapeDtypeStruct((4, 16, SEG), F32),
            jax.ShapeDtypeStruct((4, 16, SEG), BF16),
            jax.ShapeDtypeStruct((384, SEG), BF16),
        ],
        compiler_params=params(12),
        cost_estimate=pl.CostEstimate(flops=1000, bytes_accessed=1000, transcendentals=0),
        name="make_stream",
    )(index, *sums, res, far_res, gain, place)


def one_hot(values, count):
    return (np.asarray(values)[:, None] == np.arange(count)[None, :]).astype(np.float32)


def routing_tables():
    row, col = np.arange(384), np.arange(128)
    to_expert = one_hot(row // 24, 16)
    to_token = one_hot(col % 16, 16).T
    segment = (row // 6 % 4)[:, None] == (col // 32)[None, :]
    block = (row // 3 % 2)[:, None] == (col // 16 % 2)[None, :]
    kept = np.stack([segment & block & (col // 16 % 2 == b)[None, :] for b in range(2)])
    slot = (row % 3).astype(np.float32)[:, None]
    return_kept = (col // 16)[:, None] == (row % 8)[None, :]
    return_slot = (row // 8 % 3).astype(np.float32)[None, :]
    return [
        jnp.asarray(to_expert, BF16), jnp.asarray(to_token, BF16), jnp.asarray(kept, F32),
        jnp.asarray(slot, F32), jnp.asarray(return_kept, F32), jnp.asarray(return_slot, F32),
    ]


def routing_kernel(ids_ref, far_ref, gates_ref, to_expert, to_token, kept, slot, return_kept, return_slot,
                   place, weight):
    expert = lax.broadcasted_iota(jnp.int32, (16, 16), 0)
    token = lax.broadcasted_iota(jnp.int32, (16, 16), 1)
    earlier = (expert < token).astype(BF16)

    def spots(ids):
        named = jnp.zeros((16, 16), F32)
        for j in range(8):
            named = jnp.maximum(named, (ids[j:j + 1, :] == expert).astype(F32))
        rank = jnp.dot(named.astype(BF16), earlier, preferred_element_type=F32)
        return jnp.where(named > 0.0, rank, -1.0).astype(BF16)

    same = (expert == token).astype(BF16)
    far_ids = lax.dot_general(
        far_ref[:, 4 * SEG:4 * SEG + 128], same, (((0,), (0,)), ((), ())), preferred_element_type=F32
    )
    by_block = [spots(ids_ref[...]), spots(far_ids[:8].astype(jnp.int32))]
    total = jnp.zeros((384, 128), F32)
    for block in range(2):
        wide = jnp.dot(to_expert[...], by_block[block], preferred_element_type=F32)
        wide = jnp.dot(wide.astype(BF16), to_token[...], preferred_element_type=F32)
        total = total + jnp.where(wide == slot[...], kept[block], 0.0)
    place[...] = total.astype(BF16)

    def spread_out(value):
        tall = lax.dot_general(to_token[...], value, (((0,), (1,)), ((), ())), preferred_element_type=F32)
        return lax.dot_general(tall.astype(BF16), to_expert[...], (((1,), (1,)), ((), ())),
                               preferred_element_type=F32)

    live = jnp.where(spread_out(by_block[0]) == return_slot[...], return_kept[...], 0.0)
    route = jnp.zeros((16, 16), F32)
    for j in range(8):
        route = route + jnp.where(ids_ref[j:j + 1, :] == expert, gates_ref[j:j + 1, :], 0.0)
    for i in range(3):
        part = route.astype(BF16)
        weight[i] = (spread_out(part) * live).astype(BF16)
        route = route - part.astype(F32)


def routing(ids, letter, gates):
    tables = routing_tables()
    return pl.pallas_call(
        routing_kernel,
        in_specs=[VMEM] * 9,
        out_specs=[VMEM] * 2,
        out_shape=[jax.ShapeDtypeStruct((384, 128), BF16), jax.ShapeDtypeStruct((3, 128, 384), BF16)],
        compiler_params=params(8),
        cost_estimate=pl.CostEstimate(flops=1000, bytes_accessed=1000, transcendentals=0),
        name="routing",
    )(ids, letter, gates, *tables)


def pick_rows(order):
    matrix = np.zeros((4, 96, 384), np.float32)
    for q in range(4):
        for block in range(2):
            for e in range(16):
                for s in range(CAP):
                    matrix[q, block * 48 + e * 3 + s, e * 24 + q * 6 + order[block] * 3 + s] = 1.0
    return jnp.asarray(matrix.reshape(384, 384), BF16)


def up_part(base, pick_ref, inputs, gain_ref, gate_ref, up_ref, rows):
    squares = jnp.zeros((192, 1), F32)
    for i, refs in enumerate(inputs):
        if len(refs) == 1:
            moved = jnp.dot(pick_ref[...], refs[0][...], preferred_element_type=F32)
        else:
            moved = jnp.dot(pick_ref[:, :192], refs[0][...], preferred_element_type=F32)
            moved = moved + jnp.dot(pick_ref[:, 192:], refs[1][...], preferred_element_type=F32)
        for q in range(4):
            part = moved[q * 96:(q + 1) * 96]
            rows[i * 96:(i + 1) * 96, q * SEG:(q + 1) * SEG] = part.astype(BF16)
    for q in range(4):
        part = rows[:, q * SEG:(q + 1) * SEG].astype(F32)
        gain = gain_ref[:, pl.ds(pl.multiple_of((base * 4 + q) * SEG, 128), SEG)]
        squares = squares + jnp.sum(part * part * (1.0 / (gain * gain)), axis=1, keepdims=True)
    parts = [
        jnp.dot(rows[...], ref[core], preferred_element_type=F32)
        for ref in (gate_ref, up_ref) for core in range(2)
    ]
    return parts, squares


def load_kernel(index_ref, g0, g1, u0, u1, d0, d1, gate_near, up_near, gate_far, up_far, down, sems):
    base = index_ref[3]
    depth = 4 * SEG
    copies = []
    for outs, half in (((gate_near, up_near), base), ((gate_far, up_far), 1 - base)):
        rows = pl.ds(pl.multiple_of(half * depth, depth), depth)
        for out, refs in zip(outs, ((g0, g1), (u0, u1))):
            for core in range(2):
                copies.append((refs[core].at[rows], out.at[core]))
    copies += [(d0, down.at[0]), (d1, down.at[1])]
    copies = [pltpu.make_async_copy(a, b, sems.at[i]) for i, (a, b) in enumerate(copies)]
    for copy in copies:
        copy.start()
    for copy in copies:
        copy.wait()


def load_weights(index, gate, up, down):
    half = jax.ShapeDtypeStruct((2, 4 * SEG, 256), BF16)
    return pl.pallas_call(
        load_kernel,
        in_specs=[SMEM] + [pl.BlockSpec(memory_space=pl.ANY)] * 6,
        out_specs=[VMEM] * 5,
        scratch_shapes=[pltpu.SemaphoreType.DMA((10,))],
        out_shape=[half] * 4 + [jax.ShapeDtypeStruct((2, 256, D), BF16)],
        compiler_params=params(30),
        cost_estimate=pl.CostEstimate(flops=1000, bytes_accessed=1000, transcendentals=0),
        name="load_weights",
    )(index, *gate, *up, *down)


def expert_first_kernel(index_ref, x0, x1, pick_ref, gain_ref, gate_ref, up_ref, gate_up, squares, rows):
    parts, total = up_part(index_ref[3], pick_ref, ((x0,), (x1,)), gain_ref, gate_ref, up_ref, rows)
    for i, part in enumerate(parts):
        gate_up[:, i * 256:(i + 1) * 256] = part
    squares[...] = total


def expert_first(index, x0, x1, pick, gain, gate, up):
    return pl.pallas_call(
        expert_first_kernel,
        in_specs=[SMEM] + [VMEM] * 6,
        out_specs=[VMEM] * 2,
        scratch_shapes=[pltpu.VMEM((192, 4 * SEG), BF16)],
        out_shape=[jax.ShapeDtypeStruct((192, 1024), F32), jax.ShapeDtypeStruct((192, 1), F32)],
        compiler_params=params(16),
        cost_estimate=pl.CostEstimate(flops=1000, bytes_accessed=1000, transcendentals=0),
        name="expert_first",
    )(index, x0, x1, pick, gain, gate, up)


def expert_last_kernel(index_ref, x0, x1, x2, pick_ref, gain_ref, gate_ref, up_ref, down_ref, before, squares_before,
                       r0, r3, r1, r2_left, r2_right, rows, hidden):
    parts, total = up_part(1 - index_ref[3], pick_ref, ((x0,), (x1, x2)), gain_ref, gate_ref, up_ref, rows)
    scale = lax.rsqrt((total + squares_before[...]) * (1.0 / D) + EPSILON)
    for core in range(2):
        gate = (parts[core] + before[:, core * 256:(core + 1) * 256]) * scale
        up = (parts[2 + core] + before[:, 512 + core * 256:512 + (core + 1) * 256]) * scale
        hidden[:, core * 256:(core + 1) * 256] = (gate / (1.0 + jnp.exp(-gate)) * up).astype(BF16)
    for q in range(4):
        cols = slice(q * 2 * SEG, (q + 1) * 2 * SEG)
        out = jnp.dot(hidden[:, :256], down_ref[0, :, cols], preferred_element_type=F32)
        out = out + jnp.dot(hidden[:, 256:], down_ref[1, :, cols], preferred_element_type=F32)
        out = out.astype(BF16)
        for i, ref in enumerate((r0, r3, r1)):
            ref[:, cols] = out[i * 48:(i + 1) * 48]
        near = slice(q % 2 * 2 * SEG, (q % 2 + 1) * 2 * SEG)
        (r2_left, r2_right)[q // 2][:, near] = out[144:]


def expert_last(index, x0, x1, x2, pick, gain, gate, up, down, before, squares_before):
    return pl.pallas_call(
        expert_last_kernel,
        in_specs=[SMEM] + [VMEM] * 10,
        out_specs=[VMEM] * 5,
        scratch_shapes=[pltpu.VMEM((192, 4 * SEG), BF16), pltpu.VMEM((192, 512), BF16)],
        out_shape=[jax.ShapeDtypeStruct((48, D), BF16)] * 3
        + [jax.ShapeDtypeStruct((48, D // 2), BF16)] * 2,
        compiler_params=params(16),
        cost_estimate=pl.CostEstimate(flops=1000, bytes_accessed=1000, transcendentals=0),
        name="expert_last",
    )(index, x0, x1, x2, pick, gain, gate, up, down, before, squares_before)


def spread_kernel(p0, p1, p3, out):
    total = p0[...].astype(F32)
    for ref in (p1, p3):
        total = total + ref[...].astype(F32)
    total = total.astype(BF16)
    stack = jnp.concatenate([total[:, q * SEG:(q + 1) * SEG] for q in range(8)], axis=0)
    row = lax.broadcasted_iota(jnp.int32, (384, 384), 0)
    col = lax.broadcasted_iota(jnp.int32, (384, 384), 1)
    move = (row == (col % 48) * 8 + col // 48).astype(BF16)
    out[...] = jnp.dot(move, stack, preferred_element_type=F32).astype(BF16)


def spread(parts):
    return pl.pallas_call(
        spread_kernel,
        out_shape=jax.ShapeDtypeStruct((384, SEG), BF16),
        compiler_params=params(24),
        cost_estimate=pl.CostEstimate(flops=1000, bytes_accessed=1000, transcendentals=0),
        name="spread",
    )(*parts)


def combine_kernel(index_ref, rows, weight, stream_own, stream_far, out, routed):
    total = jnp.dot(weight[0], rows[...], preferred_element_type=F32)
    for i in (1, 2):
        total = total + jnp.dot(weight[i], rows[...], preferred_element_type=F32)
    routed[...] = total
    pair = index_ref[3]
    for q in range(4):
        for side, stream in ((pair, stream_own), (1 - pair, stream_far)):
            seg = side * 4 + q
            picked = routed[pl.ds(pl.multiple_of(seg * 16, 16), 16), :]
            out[:, pl.ds(pl.multiple_of(seg * SEG, 128), SEG)] = (picked + stream[q].astype(F32)).astype(BF16)


def combine(index, rows, weight, stream_own, stream_far):
    return pl.pallas_call(
        combine_kernel,
        in_specs=[SMEM] + [VMEM] * 4,
        out_specs=VMEM,
        scratch_shapes=[pltpu.VMEM((128, SEG), F32)],
        out_shape=jax.ShapeDtypeStruct((16, D), BF16),
        compiler_params=params(12),
        cost_estimate=pl.CostEstimate(flops=1000, bytes_accessed=1000, transcendentals=0),
        name="combine",
    )(index, rows, weight, stream_own, stream_far)


def per_device(residual, queries, latent, key_rope, doc_ids, kv_weight, out_weight, norm_gain,
               expert_ids, expert_gates, w_gate, w_up, w_down):
    c = lax.axis_index("ctx")
    e = lax.axis_index("exp")
    y, k, x, z = c >> 1, c & 1, e >> 2, e & 3
    pair = y >> 1
    index = jnp.stack([x, z, c & 3, pair, y, k]).astype(jnp.int32)

    far_start = (1 - pair) * (4 * SEG)

    lat = jnp.concatenate(
        [latent, key_rope, jnp.zeros((BLK, LAT_WIDTH - LATENT - ROPE), BF16)], axis=1
    )
    lat = jnp.concatenate([lat] + [swap_ctx(lat, 2 * m) for m in (1, 2, 3)], axis=0)
    out_top, out_low = out_weight[:HALF], out_weight[HALF:]
    lat, out_top, out_low, out_weight, doc_ids, w_gate, w_up, w_down, index = lax.optimization_barrier(
        (lat, out_top, out_low, out_weight, doc_ids, w_gate[0], w_up[0], w_down[0], index)
    )
    next_top = swap_ctx(out_top, 2)
    gate, up, down = ((v, swap_ctx(v, 1)) for v in (w_gate, w_up, w_down))
    near = lax.all_to_all(
        jnp.broadcast_to(lat[None], (16,) + lat.shape), "exp", split_axis=0, concat_axis=0, tiled=True
    ).reshape(16 * lat.shape[0], LAT_WIDTH)
    near, next_top, out_weight, doc_ids, gate, up, down = lax.optimization_barrier(
        (near, next_top, out_weight, doc_ids, gate, up, down)
    )
    far = swap_ctx(near, 1)
    bias = make_mask(index, doc_ids.reshape(1, KEYS))
    next_low = swap_ctx(out_low, 2)
    out_core = swap_ctx(out_weight, 1)
    near, far, bias = lax.optimization_barrier((near, far, bias))

    heads_0 = attention(0, queries, near, far, kv_weight, bias)
    near, far, heads_0, out_core = lax.optimization_barrier((near, far, heads_0, out_core))
    far_heads_0 = swap_ctx(heads_0, 6)
    both_top = swap_ctx(next_top, 1)
    heads_1 = attention(1, queries, near, far, kv_weight, bias)
    far_heads_1 = swap_ctx(heads_1, 6)
    both_top, next_low, far_heads_0, residual, expert_ids, _ = lax.optimization_barrier(
        (both_top, next_low, far_heads_0, residual, expert_ids, heads_1)
    )
    both_low = swap_ctx(next_low, 1)

    ids = jnp.concatenate([expert_ids.astype(BF16), jnp.zeros((BLK, 120), BF16)], axis=1)
    part = lax.dynamic_slice_in_dim(residual, far_start, 4 * SEG, 1)
    letter = swap_ctx(jnp.concatenate([part, ids], axis=1), 6)

    kept = load_out((out_weight, out_core, next_top, next_low, both_top, both_low))
    far_heads_0, far_heads_1, kept = lax.optimization_barrier((far_heads_0, far_heads_1, kept))
    heads = (heads_0, heads_1, far_heads_0, far_heads_1)
    left, right = project((2,), 2, index, heads, kept)
    from_1, from_3 = swap_plane(left, 1, True), swap_plane(right, 3, True)
    kept, _ = lax.optimization_barrier((kept, left))
    p0, p1, p3 = project((0, 1, 3), 4, index, heads, kept)
    p1, p3 = add_halves(p1, p3, from_1, from_3)
    letter, _ = lax.optimization_barrier((letter, p1))
    place, weight = routing(expert_ids.T, letter, expert_gates.T)
    pieces = [p0, swap_plane(p1, 1, True), swap_plane(p3, 3, True)]
    pieces, place, weight = lax.optimization_barrier((pieces, place, weight))
    sums = first_sum(index, pieces)
    sums = [sums[0]] + [swap_plane(sums[m], m, False) for m in (1, 2, 3)]
    gain = norm_gain.reshape(1, D)
    stream_own, stream_far, send = make_stream(index, sums, residual, letter, gain, place)

    got = lax.all_to_all(send.reshape(16, 24, SEG), "exp", split_axis=0, concat_axis=0, tiled=True)
    got, stream_far, gate, up, down = lax.optimization_barrier(
        (got.reshape(384, SEG), stream_far, gate, up, down)
    )
    got_1, got_3 = swap_ctx(got, 2), swap_ctx(got, 6)
    loaded = load_weights(index, gate, up, down)
    got_1, got_3, stream_far, loaded = lax.optimization_barrier((got_1, got_3, stream_far, loaded))
    got_2_top, got_2_low = swap_ctx(got_1[:192], 6), swap_ctx(got_3[192:], 2)
    stream_far = swap_ctx(stream_far, 6)
    gate_near, up_near, gate_far, up_far, down = loaded
    gate_up, squares = expert_first(index, got, got_1, pick_rows((0, 1)), gain, gate_near, up_near)
    r0, r3, r1, r2_left, r2_right = expert_last(
        index, got_3, got_2_top, got_2_low, pick_rows((1, 0)), gain, gate_far, up_far, down, gate_up, squares
    )
    r1, r3 = add_halves(r1, r3, swap_ctx(r2_left, 2), swap_ctx(r2_right, 6))
    back = spread([r0, swap_ctx(r1, 2), swap_ctx(r3, 6)])
    back, stream_far = lax.optimization_barrier((back, stream_far))
    rows = lax.all_to_all(back.reshape(16, 24, SEG), "exp", split_axis=0, concat_axis=0, tiled=True)
    return combine(index, rows.reshape(384, SEG), weight, stream_own, stream_far)


def solution(mesh):
    placed = (
        P(("ctx", "exp"), None),
        P("ctx", "exp"),
        P(("ctx", "exp"), None),
        P(("ctx", "exp"), None),
        P(),
        P(None, "exp"),
        P("exp", "ctx"),
        P(),
        P(("ctx", "exp"), None),
        P(("ctx", "exp"), None),
        P("exp", None, "ctx"),
        P("exp", None, "ctx"),
        P("exp", "ctx", None),
    )
    return jax.shard_map(
        per_device, mesh=mesh, in_specs=placed, out_specs=P(("ctx", "exp"), None), check_vma=False
    )
```

```python
import functools

import jax
import jax.numpy as jnp
import numpy as np
from jax import lax
from jax.experimental import pallas as pl
from jax.experimental.pallas import tpu as pltpu
from jax.sharding import PartitionSpec as P

NOPE = 128
ROPE = 64
VDIM = 128
LATENT = 512
CAP = 3
D = 7168
EPSILON = 1e-06
HEADS_HERE = 8
ROWS = 256
KEYS = 2048
BLK = 16
SEG = 896
NEG_FILL = -1e30
F32 = jnp.float32
BF16 = jnp.bfloat16
MIB = 1024 * 1024
SMEM = pl.BlockSpec(memory_space=pltpu.SMEM)
VMEM = pl.BlockSpec(memory_space=pltpu.VMEM)


def params(mib):
    return pltpu.CompilerParams(vmem_limit_bytes=mib * MIB)


def whole(shape):
    zeros = (0,) * len(shape)
    return pl.BlockSpec(shape, lambda *_: zeros)


def swap_ctx(value, bits):
    return lax.ppermute(value, "ctx", [(i, i ^ bits) for i in range(8)])


def swap_exp(value, bits):
    return lax.ppermute(value, "exp", [(i, i ^ bits) for i in range(16)])


def swap_plane(value, m, first):
    pairs = []
    for i in range(128):
        along_x = (i // 16 % 2 == 0) == first
        pairs.append((i, i ^ (4 * m if along_x else m)))
    return lax.ppermute(value, ("ctx", "exp"), pairs)


KEY_STEP = 512
LAT_WIDTH = LATENT + 128


def mask_kernel(index_ref, docs_ref, bias):
    y, k = index_ref[4], index_ref[5]
    spot = lax.broadcasted_iota(jnp.int32, (1, KEYS), 1)
    my, e, mk = (spot >> 4) & 3, (spot >> 6) & 15, spot >> 10
    kpos = (((my ^ y) * 2 + (mk ^ k)) * 16 + e) * 16 + (spot & 15)
    first = (y * 2 + k) * ROWS
    row = lax.broadcasted_iota(jnp.int32, (ROWS, ROWS), 0)
    col = lax.broadcasted_iota(jnp.int32, (ROWS, ROWS), 1)
    own = docs_ref[:, pl.ds(pl.multiple_of(first, ROWS), ROWS)]
    own = jnp.sum(jnp.where(row == col, own, 0), axis=1, keepdims=True)
    qlo = jnp.sum((docs_ref[...] < own).astype(jnp.int32), axis=1, keepdims=True)
    qpos = first + lax.broadcasted_iota(jnp.int32, (ROWS, 1), 0)
    allowed = (kpos <= qpos) & (kpos >= qlo)
    bias[...] = jnp.where(allowed, 0.0, NEG_FILL)


def make_mask(index, docs):
    return pl.pallas_call(
        mask_kernel,
        in_specs=[SMEM, VMEM],
        out_specs=VMEM,
        out_shape=jax.ShapeDtypeStruct((ROWS, KEYS), F32),
        compiler_params=params(8),
        cost_estimate=pl.CostEstimate(flops=1000, bytes_accessed=1000, transcendentals=0),
        name="make_mask",
    )(index, docs)


def attention_kernel(q_ref, near_ref, far_ref, w_ref, bias, out_ref, keys, values, scores):
    half = KEYS // 2

    @pl.when(pl.program_id(0) == 0)
    def _():
        for head in range(2):
            keys[head, :half, NOPE:] = near_ref[:, LATENT:LATENT + ROPE]
            keys[head, half:, NOPE:] = far_ref[:, LATENT:LATENT + ROPE]

    log2e = 1.4426950408889634
    factor = (NOPE + ROPE) ** (-0.5) * log2e
    steps = range(KEYS // KEY_STEP)
    for head in range(2):
        cols = slice(head * (NOPE + VDIM), (head + 1) * (NOPE + VDIM))
        for step in steps:
            rows = slice(step * KEY_STEP, (step + 1) * KEY_STEP)
            if step * KEY_STEP < half:
                lat = near_ref[rows, :LATENT]
            else:
                lat = far_ref[step * KEY_STEP - half:(step + 1) * KEY_STEP - half, :LATENT]
            pair = jnp.dot(lat, w_ref[:, cols], preferred_element_type=F32).astype(BF16)
            keys[head, rows, :NOPE] = pair[:, :NOPE]
            values[head, rows, :] = pair[:, NOPE:]
    for head in range(2):
        query = q_ref[:, head * (NOPE + ROPE):(head + 1) * (NOPE + ROPE)]
        peak = None
        for step in steps:
            rows = slice(step * KEY_STEP, (step + 1) * KEY_STEP)
            part = lax.dot_general(query, keys[head, rows, :], (((1,), (1,)), ((), ())),
                                   preferred_element_type=F32)
            part = part * factor + bias[:, rows]
            scores[head, :, rows] = part
            top = jnp.max(part, axis=1, keepdims=True)
            peak = top if peak is None else jnp.maximum(peak, top)
        total = jnp.zeros((ROWS, 1), F32)
        out = jnp.zeros((ROWS, VDIM), F32)
        for step in steps:
            rows = slice(step * KEY_STEP, (step + 1) * KEY_STEP)
            weight = jnp.exp2(scores[head, :, rows] - peak)
            total = total + jnp.sum(weight, axis=1, keepdims=True)
            out = out + jnp.dot(weight.astype(BF16), values[head, rows, :], preferred_element_type=F32)
        out_ref[:, head * VDIM:(head + 1) * VDIM] = (out / total).astype(BF16)


def attention(part, query, near, far, weight, bias):
    pairs = HEADS_HERE // 4
    first = part * pairs
    return pl.pallas_call(
        attention_kernel,
        grid=(pairs,),
        in_specs=[
            pl.BlockSpec((ROWS, 2 * (NOPE + ROPE)), lambda h: (0, first + h)),
            VMEM,
            VMEM,
            pl.BlockSpec((LATENT, 2 * (NOPE + VDIM)), lambda h: (0, first + h)),
            VMEM,
        ],
        out_specs=pl.BlockSpec((ROWS, 2 * VDIM), lambda h: (0, h)),
        scratch_shapes=[
            pltpu.VMEM((2, KEYS, NOPE + ROPE), BF16),
            pltpu.VMEM((2, KEYS, VDIM), BF16),
            pltpu.VMEM((2, ROWS, KEYS), F32),
        ],
        out_shape=jax.ShapeDtypeStruct((ROWS, pairs * 2 * VDIM), BF16),
        compiler_params=params(24),
        cost_estimate=pl.CostEstimate(flops=1000, bytes_accessed=1000, transcendentals=0),
        name="attention",
    )(query, near, far, weight, bias)


HALF = HEADS_HERE * VDIM // 2


def load_out_kernel(w0, w1, w2, w3, w4, w5, kept, sems):
    top, low = pl.ds(0, HALF), pl.ds(HALF, HALF)
    targets = (kept.at[0], kept.at[1], kept.at[2, top], kept.at[2, low], kept.at[3, top], kept.at[3, low])
    copies = [
        pltpu.make_async_copy(w, target, sems.at[i])
        for i, (w, target) in enumerate(zip((w0, w1, w2, w3, w4, w5), targets))
    ]
    for copy in copies:
        copy.start()
    for copy in copies:
        copy.wait()


def load_out(weights):
    return pl.pallas_call(
        load_out_kernel,
        in_specs=[pl.BlockSpec(memory_space=pl.ANY)] * 6,
        out_specs=VMEM,
        scratch_shapes=[pltpu.SemaphoreType.DMA((6,))],
        out_shape=jax.ShapeDtypeStruct((4, 2 * HALF, SEG), BF16),
        compiler_params=params(8),
        cost_estimate=pl.CostEstimate(flops=1000, bytes_accessed=1000, transcendentals=0),
        name="load_out",
    )(*weights)


def project_kernel(steps, widths, index_ref, h0, h1, h2, h3, kept, *refs):
    outs, left = refs[:-1], refs[-1]
    x, z, k = index_ref[0], index_ref[1], index_ref[5]
    heads = (h0, h1, h2, h3)
    for i, m in enumerate(steps):
        for n in range(4):
            first = (1 - k) * ((x ^ m) * 64 + n * 16) + k * (n * 64 + (z ^ m) * 16)
            first = pl.multiple_of(first, 16)
            for block in range(2):
                start = i * 128 + block * 64 + n * 16
                for half in range(2):
                    cols = slice(half * HALF, (half + 1) * HALF)
                    left[start:start + 16, cols] = heads[block * 2 + half][pl.ds(first, 16), :]
    count = 4 // widths
    for seg in range(4):
        part = jnp.dot(left[...], kept[seg], preferred_element_type=F32).astype(BF16)
        for i in range(len(steps)):
            out = outs[i * count + seg // widths]
            cols = slice(seg % widths * SEG, (seg % widths + 1) * SEG)
            out[:, cols] = part[i * 128:(i + 1) * 128, :]


def project(steps, widths, index, heads, kept):
    piece = jax.ShapeDtypeStruct((128, widths * SEG), BF16)
    count = len(steps) * (4 // widths)
    return pl.pallas_call(
        functools.partial(project_kernel, steps, widths),
        in_specs=[SMEM] + [VMEM] * 5,
        out_specs=[VMEM] * count,
        scratch_shapes=[pltpu.VMEM((128 * len(steps), 2 * HALF), BF16)],
        out_shape=[piece] * count,
        compiler_params=params(16),
        cost_estimate=pl.CostEstimate(flops=1000, bytes_accessed=1000, transcendentals=0),
        name="project",
    )(index, *heads, kept)


def add_half_kernel(on_left, piece, part, out):
    half = piece.shape[1] // 2
    with_part, without = slice(0, half), slice(half, 2 * half)
    if not on_left:
        with_part, without = without, with_part
    out[:, without] = piece[:, without]
    out[:, with_part] = (piece[:, with_part].astype(F32) + part[...].astype(F32)).astype(BF16)


def add_half(on_left, piece, part):
    return pl.pallas_call(
        functools.partial(add_half_kernel, on_left),
        in_specs=[VMEM] * 2,
        out_specs=VMEM,
        out_shape=jax.ShapeDtypeStruct(piece.shape, BF16),
        compiler_params=params(8),
        cost_estimate=pl.CostEstimate(flops=1000, bytes_accessed=1000, transcendentals=0),
        name="add_half",
    )(piece, part)


def first_sum_kernel(index_ref, i0, i1, i3, *outs):
    k = index_ref[5]
    spot = (1 - k) * index_ref[1] + k * index_ref[0]
    for m, out in enumerate(outs):
        for block in range(2):
            rows = pl.ds(pl.multiple_of(block * 64 + (spot ^ m) * 16, 16), 16)
            total = i0[rows, :].astype(F32)
            for ref in (i1, i3):
                total = total + ref[rows, :].astype(F32)
            out[block * 16:(block + 1) * 16, :] = total.astype(BF16)


def first_sum(index, pieces):
    out = jax.ShapeDtypeStruct((32, 4 * SEG), BF16)
    return pl.pallas_call(
        first_sum_kernel,
        in_specs=[SMEM] + [VMEM] * 3,
        out_specs=[VMEM] * 4,
        out_shape=[out] * 4,
        compiler_params=params(12),
        cost_estimate=pl.CostEstimate(flops=1000, bytes_accessed=1000, transcendentals=0),
        name="first_sum",
    )(index, *pieces)


def stream_kernel(index_ref, *refs):
    sums, (res, far_res, gain, place, stream_own, stream_far, send, stack) = refs[:4], refs[4:]
    spot, base = index_ref[2], index_ref[3] * 4
    for i in range(4):
        seg = spot ^ i
        cols = slice(i * SEG, (i + 1) * SEG)
        wide = pl.ds(pl.multiple_of((base + seg) * SEG, 128), SEG)
        near = pl.ds(pl.multiple_of(seg * SEG, 128), SEG)
        for block, start, stream in ((0, res[:, wide], stream_own), (1, far_res[:, near], stream_far)):
            total = start.astype(F32)
            for ref in sums:
                total = total + ref[block * 16:(block + 1) * 16, cols].astype(F32)
            stream[seg] = total.astype(stream.dtype)
            first = pl.multiple_of(seg * 32 + block * 16, 16)
            stack[pl.ds(first, 16), :] = (total * gain[:, wide]).astype(BF16)
    send[...] = jnp.dot(place[...], stack[...], preferred_element_type=F32).astype(BF16)


def make_stream(index, sums, res, far_res, gain, place):
    return pl.pallas_call(
        stream_kernel,
        in_specs=[SMEM] + [VMEM] * 8,
        out_specs=[VMEM] * 3,
        scratch_shapes=[pltpu.VMEM((128, SEG), BF16)],
        out_shape=[
            jax.ShapeDtypeStruct((4, 16, SEG), F32),
            jax.ShapeDtypeStruct((4, 16, SEG), BF16),
            jax.ShapeDtypeStruct((384, SEG), BF16),
        ],
        compiler_params=params(12),
        cost_estimate=pl.CostEstimate(flops=1000, bytes_accessed=1000, transcendentals=0),
        name="make_stream",
    )(index, *sums, res, far_res, gain, place)


def one_hot(values, count):
    return (np.asarray(values)[:, None] == np.arange(count)[None, :]).astype(np.float32)


def routing_tables():
    row, col = np.arange(384), np.arange(128)
    to_expert = one_hot(row // 24, 16)
    to_token = one_hot(col % 16, 16).T
    segment = (row // 6 % 4)[:, None] == (col // 32)[None, :]
    block = (row // 3 % 2)[:, None] == (col // 16 % 2)[None, :]
    kept = np.stack([segment & block & (col // 16 % 2 == b)[None, :] for b in range(2)])
    slot = (row % 3).astype(np.float32)[:, None]
    return_kept = (col // 16)[:, None] == (row % 8)[None, :]
    return_slot = (row // 8 % 3).astype(np.float32)[None, :]
    return [
        jnp.asarray(to_expert, BF16), jnp.asarray(to_token, BF16), jnp.asarray(kept, F32),
        jnp.asarray(slot, F32), jnp.asarray(return_kept, F32), jnp.asarray(return_slot, F32),
    ]


def routing_kernel(ids_ref, far_ref, gates_ref, to_expert, to_token, kept, slot, return_kept, return_slot,
                   place, weight):
    expert = lax.broadcasted_iota(jnp.int32, (16, 16), 0)
    token = lax.broadcasted_iota(jnp.int32, (16, 16), 1)
    earlier = (expert < token).astype(BF16)

    def spots(ids):
        named = jnp.zeros((16, 16), F32)
        for j in range(8):
            named = jnp.maximum(named, (ids[j:j + 1, :] == expert).astype(F32))
        rank = jnp.dot(named.astype(BF16), earlier, preferred_element_type=F32)
        return jnp.where(named > 0.0, rank, -1.0).astype(BF16)

    same = (expert == token).astype(BF16)
    far_ids = lax.dot_general(
        far_ref[:, 4 * SEG:4 * SEG + 128], same, (((0,), (0,)), ((), ())), preferred_element_type=F32
    )
    by_block = [spots(ids_ref[...]), spots(far_ids[:8].astype(jnp.int32))]
    total = jnp.zeros((384, 128), F32)
    for block in range(2):
        wide = jnp.dot(to_expert[...], by_block[block], preferred_element_type=F32)
        wide = jnp.dot(wide.astype(BF16), to_token[...], preferred_element_type=F32)
        total = total + jnp.where(wide == slot[...], kept[block], 0.0)
    place[...] = total.astype(BF16)

    def spread_out(value):
        tall = lax.dot_general(to_token[...], value, (((0,), (1,)), ((), ())), preferred_element_type=F32)
        return lax.dot_general(tall.astype(BF16), to_expert[...], (((1,), (1,)), ((), ())),
                               preferred_element_type=F32)

    live = jnp.where(spread_out(by_block[0]) == return_slot[...], return_kept[...], 0.0)
    route = jnp.zeros((16, 16), F32)
    for j in range(8):
        route = route + jnp.where(ids_ref[j:j + 1, :] == expert, gates_ref[j:j + 1, :], 0.0)
    for i in range(3):
        part = route.astype(BF16)
        weight[i] = (spread_out(part) * live).astype(BF16)
        route = route - part.astype(F32)


def routing(ids, letter, gates):
    tables = routing_tables()
    return pl.pallas_call(
        routing_kernel,
        in_specs=[VMEM] * 9,
        out_specs=[VMEM] * 2,
        out_shape=[jax.ShapeDtypeStruct((384, 128), BF16), jax.ShapeDtypeStruct((3, 128, 384), BF16)],
        compiler_params=params(8),
        cost_estimate=pl.CostEstimate(flops=1000, bytes_accessed=1000, transcendentals=0),
        name="routing",
    )(ids, letter, gates, *tables)


def pick_rows(order):
    matrix = np.zeros((4, 96, 384), np.float32)
    for q in range(4):
        for block in range(2):
            for e in range(16):
                for s in range(CAP):
                    matrix[q, block * 48 + e * 3 + s, e * 24 + q * 6 + order[block] * 3 + s] = 1.0
    return jnp.asarray(matrix.reshape(384, 384), BF16)


def up_part(base, pick_ref, inputs, gain_ref, gate_ref, up_ref, rows):
    squares = jnp.zeros((192, 1), F32)
    for i, refs in enumerate(inputs):
        if len(refs) == 1:
            moved = jnp.dot(pick_ref[...], refs[0][...], preferred_element_type=F32)
        else:
            moved = jnp.dot(pick_ref[:, :192], refs[0][...], preferred_element_type=F32)
            moved = moved + jnp.dot(pick_ref[:, 192:], refs[1][...], preferred_element_type=F32)
        for q in range(4):
            part = moved[q * 96:(q + 1) * 96]
            rows[i * 96:(i + 1) * 96, q * SEG:(q + 1) * SEG] = part.astype(BF16)
    for q in range(4):
        part = rows[:, q * SEG:(q + 1) * SEG].astype(F32)
        gain = gain_ref[:, pl.ds(pl.multiple_of((base * 4 + q) * SEG, 128), SEG)]
        squares = squares + jnp.sum(part * part * (1.0 / (gain * gain)), axis=1, keepdims=True)
    parts = [
        jnp.dot(rows[...], ref[core], preferred_element_type=F32)
        for ref in (gate_ref, up_ref) for core in range(2)
    ]
    return parts, squares


def load_kernel(index_ref, g0, g1, u0, u1, d0, d1, gate_near, up_near, gate_far, up_far, down, sems):
    base = index_ref[3]
    depth = 4 * SEG
    copies = []
    for outs, half in (((gate_near, up_near), base), ((gate_far, up_far), 1 - base)):
        rows = pl.ds(pl.multiple_of(half * depth, depth), depth)
        for out, refs in zip(outs, ((g0, g1), (u0, u1))):
            for core in range(2):
                copies.append((refs[core].at[rows], out.at[core]))
    copies += [(d0, down.at[0]), (d1, down.at[1])]
    copies = [pltpu.make_async_copy(a, b, sems.at[i]) for i, (a, b) in enumerate(copies)]
    for copy in copies:
        copy.start()
    for copy in copies:
        copy.wait()


def load_weights(index, gate, up, down):
    half = jax.ShapeDtypeStruct((2, 4 * SEG, 256), BF16)
    return pl.pallas_call(
        load_kernel,
        in_specs=[SMEM] + [pl.BlockSpec(memory_space=pl.ANY)] * 6,
        out_specs=[VMEM] * 5,
        scratch_shapes=[pltpu.SemaphoreType.DMA((10,))],
        out_shape=[half] * 4 + [jax.ShapeDtypeStruct((2, 256, D), BF16)],
        compiler_params=params(30),
        cost_estimate=pl.CostEstimate(flops=1000, bytes_accessed=1000, transcendentals=0),
        name="load_weights",
    )(index, *gate, *up, *down)


def expert_first_kernel(index_ref, x0, x1, pick_ref, gain_ref, gate_ref, up_ref, gate_up, squares, rows):
    parts, total = up_part(index_ref[3], pick_ref, ((x0,), (x1,)), gain_ref, gate_ref, up_ref, rows)
    for i, part in enumerate(parts):
        gate_up[:, i * 256:(i + 1) * 256] = part
    squares[...] = total


def expert_first(index, x0, x1, pick, gain, gate, up):
    return pl.pallas_call(
        expert_first_kernel,
        in_specs=[SMEM] + [VMEM] * 6,
        out_specs=[VMEM] * 2,
        scratch_shapes=[pltpu.VMEM((192, 4 * SEG), BF16)],
        out_shape=[jax.ShapeDtypeStruct((192, 1024), F32), jax.ShapeDtypeStruct((192, 1), F32)],
        compiler_params=params(16),
        cost_estimate=pl.CostEstimate(flops=1000, bytes_accessed=1000, transcendentals=0),
        name="expert_first",
    )(index, x0, x1, pick, gain, gate, up)


def expert_last_kernel(index_ref, x0, x1, x2, pick_ref, gain_ref, gate_ref, up_ref, down_ref, before, squares_before,
                       r0, r3, r1, r2_left, r2_right, rows, hidden):
    parts, total = up_part(1 - index_ref[3], pick_ref, ((x0,), (x1, x2)), gain_ref, gate_ref, up_ref, rows)
    scale = lax.rsqrt((total + squares_before[...]) * (1.0 / D) + EPSILON)
    for core in range(2):
        gate = (parts[core] + before[:, core * 256:(core + 1) * 256]) * scale
        up = (parts[2 + core] + before[:, 512 + core * 256:512 + (core + 1) * 256]) * scale
        hidden[:, core * 256:(core + 1) * 256] = (gate / (1.0 + jnp.exp(-gate)) * up).astype(BF16)
    for q in range(4):
        cols = slice(q * 2 * SEG, (q + 1) * 2 * SEG)
        out = jnp.dot(hidden[:, :256], down_ref[0, :, cols], preferred_element_type=F32)
        out = out + jnp.dot(hidden[:, 256:], down_ref[1, :, cols], preferred_element_type=F32)
        out = out.astype(BF16)
        for i, ref in enumerate((r0, r3, r1)):
            ref[:, cols] = out[i * 48:(i + 1) * 48]
        near = slice(q % 2 * 2 * SEG, (q % 2 + 1) * 2 * SEG)
        (r2_left, r2_right)[q // 2][:, near] = out[144:]


def expert_last(index, x0, x1, x2, pick, gain, gate, up, down, before, squares_before):
    return pl.pallas_call(
        expert_last_kernel,
        in_specs=[SMEM] + [VMEM] * 10,
        out_specs=[VMEM] * 5,
        scratch_shapes=[pltpu.VMEM((192, 4 * SEG), BF16), pltpu.VMEM((192, 512), BF16)],
        out_shape=[jax.ShapeDtypeStruct((48, D), BF16)] * 3
        + [jax.ShapeDtypeStruct((48, D // 2), BF16)] * 2,
        compiler_params=params(16),
        cost_estimate=pl.CostEstimate(flops=1000, bytes_accessed=1000, transcendentals=0),
        name="expert_last",
    )(index, x0, x1, x2, pick, gain, gate, up, down, before, squares_before)


def spread_kernel(p0, p1, p3, out):
    total = p0[...].astype(F32)
    for ref in (p1, p3):
        total = total + ref[...].astype(F32)
    total = total.astype(BF16)
    stack = jnp.concatenate([total[:, q * SEG:(q + 1) * SEG] for q in range(8)], axis=0)
    row = lax.broadcasted_iota(jnp.int32, (384, 384), 0)
    col = lax.broadcasted_iota(jnp.int32, (384, 384), 1)
    move = (row == (col % 48) * 8 + col // 48).astype(BF16)
    out[...] = jnp.dot(move, stack, preferred_element_type=F32).astype(BF16)


def spread(parts):
    return pl.pallas_call(
        spread_kernel,
        out_shape=jax.ShapeDtypeStruct((384, SEG), BF16),
        compiler_params=params(24),
        cost_estimate=pl.CostEstimate(flops=1000, bytes_accessed=1000, transcendentals=0),
        name="spread",
    )(*parts)


def combine_kernel(index_ref, rows, weight, stream_own, stream_far, out, routed):
    total = jnp.dot(weight[0], rows[...], preferred_element_type=F32)
    for i in (1, 2):
        total = total + jnp.dot(weight[i], rows[...], preferred_element_type=F32)
    routed[...] = total
    pair = index_ref[3]
    for q in range(4):
        for side, stream in ((pair, stream_own), (1 - pair, stream_far)):
            seg = side * 4 + q
            picked = routed[pl.ds(pl.multiple_of(seg * 16, 16), 16), :]
            out[:, pl.ds(pl.multiple_of(seg * SEG, 128), SEG)] = (picked + stream[q].astype(F32)).astype(BF16)


def combine(index, rows, weight, stream_own, stream_far):
    return pl.pallas_call(
        combine_kernel,
        in_specs=[SMEM] + [VMEM] * 4,
        out_specs=VMEM,
        scratch_shapes=[pltpu.VMEM((128, SEG), F32)],
        out_shape=jax.ShapeDtypeStruct((16, D), BF16),
        compiler_params=params(12),
        cost_estimate=pl.CostEstimate(flops=1000, bytes_accessed=1000, transcendentals=0),
        name="combine",
    )(index, rows, weight, stream_own, stream_far)


def per_device(residual, queries, latent, key_rope, doc_ids, kv_weight, out_weight, norm_gain,
               expert_ids, expert_gates, w_gate, w_up, w_down):
    c = lax.axis_index("ctx")
    e = lax.axis_index("exp")
    y, k, x, z = c >> 1, c & 1, e >> 2, e & 3
    pair = y >> 1
    index = jnp.stack([x, z, c & 3, pair, y, k]).astype(jnp.int32)

    far_start = (1 - pair) * (4 * SEG)

    lat = jnp.concatenate(
        [latent, key_rope, jnp.zeros((BLK, LAT_WIDTH - LATENT - ROPE), BF16)], axis=1
    )
    lat = jnp.concatenate([lat] + [swap_ctx(lat, 2 * m) for m in (1, 2, 3)], axis=0)
    out_top, out_low = out_weight[:HALF], out_weight[HALF:]
    lat, out_top, out_low, out_weight, doc_ids, w_gate, w_up, w_down, index = lax.optimization_barrier(
        (lat, out_top, out_low, out_weight, doc_ids, w_gate[0], w_up[0], w_down[0], index)
    )
    next_top = swap_ctx(out_top, 2)
    gate, up, down = ((v, swap_ctx(v, 1)) for v in (w_gate, w_up, w_down))
    near = lax.all_to_all(
        jnp.broadcast_to(lat[None], (16,) + lat.shape), "exp", split_axis=0, concat_axis=0, tiled=True
    ).reshape(16 * lat.shape[0], LAT_WIDTH)
    near, next_top, out_weight, doc_ids, gate, up, down = lax.optimization_barrier(
        (near, next_top, out_weight, doc_ids, gate, up, down)
    )
    far = swap_ctx(near, 1)
    bias = make_mask(index, doc_ids.reshape(1, KEYS))
    next_low = swap_ctx(out_low, 2)
    out_core = swap_ctx(out_weight, 1)
    near, far, bias = lax.optimization_barrier((near, far, bias))

    heads_0 = attention(0, queries, near, far, kv_weight, bias)
    near, far, heads_0, out_core = lax.optimization_barrier((near, far, heads_0, out_core))
    far_heads_0 = swap_ctx(heads_0, 6)
    both_top = swap_ctx(next_top, 1)
    heads_1 = attention(1, queries, near, far, kv_weight, bias)
    far_heads_1 = swap_ctx(heads_1, 6)
    both_top, next_low, far_heads_0, residual, expert_ids, _ = lax.optimization_barrier(
        (both_top, next_low, far_heads_0, residual, expert_ids, heads_1)
    )
    both_low = swap_ctx(next_low, 1)

    ids = jnp.concatenate([expert_ids.astype(BF16), jnp.zeros((BLK, 120), BF16)], axis=1)
    part = lax.dynamic_slice_in_dim(residual, far_start, 4 * SEG, 1)
    letter = swap_ctx(jnp.concatenate([part, ids], axis=1), 6)

    kept = load_out((out_weight, out_core, next_top, next_low, both_top, both_low))
    far_heads_0, far_heads_1, kept = lax.optimization_barrier((far_heads_0, far_heads_1, kept))
    heads = (heads_0, heads_1, far_heads_0, far_heads_1)
    left, right = project((2,), 2, index, heads, kept)
    from_1, from_3 = swap_plane(left, 1, True), swap_plane(right, 3, True)
    kept, _ = lax.optimization_barrier((kept, left))
    p0, p1, p3 = project((0, 1, 3), 4, index, heads, kept)
    p3, p1 = add_half(True, p3, from_1), add_half(False, p1, from_3)
    letter, _ = lax.optimization_barrier((letter, p1))
    place, weight = routing(expert_ids.T, letter, expert_gates.T)
    pieces = [p0, swap_plane(p1, 1, True), swap_plane(p3, 3, True)]
    pieces, place, weight = lax.optimization_barrier((pieces, place, weight))
    sums = first_sum(index, pieces)
    sums = [sums[0]] + [swap_plane(sums[m], m, False) for m in (1, 2, 3)]
    gain = norm_gain.reshape(1, D)
    stream_own, stream_far, send = make_stream(index, sums, residual, letter, gain, place)

    got = lax.all_to_all(send.reshape(16, 24, SEG), "exp", split_axis=0, concat_axis=0, tiled=True)
    got, stream_far, gate, up, down = lax.optimization_barrier(
        (got.reshape(384, SEG), stream_far, gate, up, down)
    )
    got_1, got_3 = swap_ctx(got, 2), swap_ctx(got, 6)
    loaded = load_weights(index, gate, up, down)
    got_1, _ = lax.optimization_barrier((got_1, loaded[0]))
    got_3, stream_far, _ = lax.optimization_barrier((got_3, stream_far, loaded[0]))
    got_2_top, got_2_low = swap_ctx(got_1[:192], 6), swap_ctx(got_3[192:], 2)
    stream_far = swap_ctx(stream_far, 6)
    gate_near, up_near, gate_far, up_far, down = loaded
    gate_up, squares = expert_first(index, got, got_1, pick_rows((0, 1)), gain, gate_near, up_near)
    r0, r3, r1, r2_left, r2_right = expert_last(
        index, got_3, got_2_top, got_2_low, pick_rows((1, 0)), gain, gate_far, up_far, down, gate_up, squares
    )
    r3, r1 = add_half(True, r3, swap_ctx(r2_left, 2)), add_half(False, r1, swap_ctx(r2_right, 6))
    back = spread([r0, swap_ctx(r1, 2), swap_ctx(r3, 6)])
    back, stream_far = lax.optimization_barrier((back, stream_far))
    rows = lax.all_to_all(back.reshape(16, 24, SEG), "exp", split_axis=0, concat_axis=0, tiled=True)
    return combine(index, rows.reshape(384, SEG), weight, stream_own, stream_far)


def solution(mesh):
    placed = (
        P(("ctx", "exp"), None),
        P("ctx", "exp"),
        P(("ctx", "exp"), None),
        P(("ctx", "exp"), None),
        P(),
        P(None, "exp"),
        P("exp", "ctx"),
        P(),
        P(("ctx", "exp"), None),
        P(("ctx", "exp"), None),
        P("exp", None, "ctx"),
        P("exp", None, "ctx"),
        P("exp", "ctx", None),
    )
    return jax.shard_map(
        per_device, mesh=mesh, in_specs=placed, out_specs=P(("ctx", "exp"), None), check_vma=False
    )
```

```python
import functools

import jax
import jax.numpy as jnp
import numpy as np
from jax import lax
from jax.experimental import pallas as pl
from jax.experimental.pallas import tpu as pltpu
from jax.sharding import PartitionSpec as P

NOPE = 128
ROPE = 64
VDIM = 128
LATENT = 512
CAP = 3
D = 7168
EPSILON = 1e-06
HEADS_HERE = 8
ROWS = 256
KEYS = 2048
BLK = 16
SEG = 896
NEG_FILL = -1e30
F32 = jnp.float32
BF16 = jnp.bfloat16
MIB = 1024 * 1024
SMEM = pl.BlockSpec(memory_space=pltpu.SMEM)
VMEM = pl.BlockSpec(memory_space=pltpu.VMEM)


def params(mib):
    return pltpu.CompilerParams(vmem_limit_bytes=mib * MIB)


def whole(shape):
    zeros = (0,) * len(shape)
    return pl.BlockSpec(shape, lambda *_: zeros)


def swap_ctx(value, bits):
    return lax.ppermute(value, "ctx", [(i, i ^ bits) for i in range(8)])


def swap_exp(value, bits):
    return lax.ppermute(value, "exp", [(i, i ^ bits) for i in range(16)])


def swap_plane(value, m, first):
    pairs = []
    for i in range(128):
        along_x = (i // 16 % 2 == 0) == first
        pairs.append((i, i ^ (4 * m if along_x else m)))
    return lax.ppermute(value, ("ctx", "exp"), pairs)


KEY_STEP = 512
LAT_WIDTH = LATENT + 128


def mask_kernel(index_ref, docs_ref, bias):
    y, k = index_ref[4], index_ref[5]
    spot = lax.broadcasted_iota(jnp.int32, (1, KEYS), 1)
    my, e, mk = (spot >> 4) & 3, (spot >> 6) & 15, spot >> 10
    kpos = (((my ^ y) * 2 + (mk ^ k)) * 16 + e) * 16 + (spot & 15)
    first = (y * 2 + k) * ROWS
    row = lax.broadcasted_iota(jnp.int32, (ROWS, ROWS), 0)
    col = lax.broadcasted_iota(jnp.int32, (ROWS, ROWS), 1)
    own = docs_ref[:, pl.ds(pl.multiple_of(first, ROWS), ROWS)]
    own = jnp.sum(jnp.where(row == col, own, 0), axis=1, keepdims=True)
    qlo = jnp.sum((docs_ref[...] < own).astype(jnp.int32), axis=1, keepdims=True)
    qpos = first + lax.broadcasted_iota(jnp.int32, (ROWS, 1), 0)
    allowed = (kpos <= qpos) & (kpos >= qlo)
    bias[...] = jnp.where(allowed, 0.0, NEG_FILL)


def make_mask(index, docs):
    return pl.pallas_call(
        mask_kernel,
        in_specs=[SMEM, VMEM],
        out_specs=VMEM,
        out_shape=jax.ShapeDtypeStruct((ROWS, KEYS), F32),
        compiler_params=params(8),
        cost_estimate=pl.CostEstimate(flops=1000, bytes_accessed=1000, transcendentals=0),
        name="make_mask",
    )(index, docs)


def attention_kernel(q_ref, near_ref, far_ref, w_ref, bias, out_ref, keys, values, scores):
    half = KEYS // 2

    @pl.when(pl.program_id(0) == 0)
    def _():
        for head in range(2):
            keys[head, :half, NOPE:] = near_ref[:, LATENT:LATENT + ROPE]
            keys[head, half:, NOPE:] = far_ref[:, LATENT:LATENT + ROPE]

    log2e = 1.4426950408889634
    factor = (NOPE + ROPE) ** (-0.5) * log2e
    steps = range(KEYS // KEY_STEP)
    for head in range(2):
        cols = slice(head * (NOPE + VDIM), (head + 1) * (NOPE + VDIM))
        for step in steps:
            rows = slice(step * KEY_STEP, (step + 1) * KEY_STEP)
            if step * KEY_STEP < half:
                lat = near_ref[rows, :LATENT]
            else:
                lat = far_ref[step * KEY_STEP - half:(step + 1) * KEY_STEP - half, :LATENT]
            pair = jnp.dot(lat, w_ref[:, cols], preferred_element_type=F32).astype(BF16)
            keys[head, rows, :NOPE] = pair[:, :NOPE]
            values[head, rows, :] = pair[:, NOPE:]
    for head in range(2):
        query = q_ref[:, head * (NOPE + ROPE):(head + 1) * (NOPE + ROPE)]
        peak = None
        for step in steps:
            rows = slice(step * KEY_STEP, (step + 1) * KEY_STEP)
            part = lax.dot_general(query, keys[head, rows, :], (((1,), (1,)), ((), ())),
                                   preferred_element_type=F32)
            part = part * factor + bias[:, rows]
            scores[head, :, rows] = part
            top = jnp.max(part, axis=1, keepdims=True)
            peak = top if peak is None else jnp.maximum(peak, top)
        total = jnp.zeros((ROWS, 1), F32)
        out = jnp.zeros((ROWS, VDIM), F32)
        for step in steps:
            rows = slice(step * KEY_STEP, (step + 1) * KEY_STEP)
            weight = jnp.exp2(scores[head, :, rows] - peak)
            total = total + jnp.sum(weight, axis=1, keepdims=True)
            out = out + jnp.dot(weight.astype(BF16), values[head, rows, :], preferred_element_type=F32)
        out_ref[:, head * VDIM:(head + 1) * VDIM] = (out / total).astype(BF16)


def attention(part, query, near, far, weight, bias):
    pairs = HEADS_HERE // 4
    first = part * pairs
    return pl.pallas_call(
        attention_kernel,
        grid=(pairs,),
        in_specs=[
            pl.BlockSpec((ROWS, 2 * (NOPE + ROPE)), lambda h: (0, first + h)),
            VMEM,
            VMEM,
            pl.BlockSpec((LATENT, 2 * (NOPE + VDIM)), lambda h: (0, first + h)),
            VMEM,
        ],
        out_specs=pl.BlockSpec((ROWS, 2 * VDIM), lambda h: (0, h)),
        scratch_shapes=[
            pltpu.VMEM((2, KEYS, NOPE + ROPE), BF16),
            pltpu.VMEM((2, KEYS, VDIM), BF16),
            pltpu.VMEM((2, ROWS, KEYS), F32),
        ],
        out_shape=jax.ShapeDtypeStruct((ROWS, pairs * 2 * VDIM), BF16),
        compiler_params=params(24),
        cost_estimate=pl.CostEstimate(flops=1000, bytes_accessed=1000, transcendentals=0),
        name="attention",
    )(query, near, far, weight, bias)


HALF = HEADS_HERE * VDIM // 2


def load_out_kernel(w0, w1, w2, w3, w4, w5, kept, sems):
    top, low = pl.ds(0, HALF), pl.ds(HALF, HALF)
    targets = (kept.at[0], kept.at[1], kept.at[2, top], kept.at[2, low], kept.at[3, top], kept.at[3, low])
    copies = [
        pltpu.make_async_copy(w, target, sems.at[i])
        for i, (w, target) in enumerate(zip((w0, w1, w2, w3, w4, w5), targets))
    ]
    for copy in copies:
        copy.start()
    for copy in copies:
        copy.wait()


def load_out(weights):
    return pl.pallas_call(
        load_out_kernel,
        in_specs=[pl.BlockSpec(memory_space=pl.ANY)] * 6,
        out_specs=VMEM,
        scratch_shapes=[pltpu.SemaphoreType.DMA((6,))],
        out_shape=jax.ShapeDtypeStruct((4, 2 * HALF, SEG), BF16),
        compiler_params=params(8),
        cost_estimate=pl.CostEstimate(flops=1000, bytes_accessed=1000, transcendentals=0),
        name="load_out",
    )(*weights)


def project_kernel(steps, widths, index_ref, h0, h1, h2, h3, kept, *refs):
    outs, left = refs[:-1], refs[-1]
    x, z, k = index_ref[0], index_ref[1], index_ref[5]
    heads = (h0, h1, h2, h3)
    for i, m in enumerate(steps):
        for n in range(4):
            first = (1 - k) * ((x ^ m) * 64 + n * 16) + k * (n * 64 + (z ^ m) * 16)
            first = pl.multiple_of(first, 16)
            for block in range(2):
                start = i * 128 + block * 64 + n * 16
                for half in range(2):
                    cols = slice(half * HALF, (half + 1) * HALF)
                    left[start:start + 16, cols] = heads[block * 2 + half][pl.ds(first, 16), :]
    count = 4 // widths
    for seg in range(4):
        part = jnp.dot(left[...], kept[seg], preferred_element_type=F32).astype(BF16)
        for i in range(len(steps)):
            out = outs[i * count + seg // widths]
            cols = slice(seg % widths * SEG, (seg % widths + 1) * SEG)
            out[:, cols] = part[i * 128:(i + 1) * 128, :]


def project(steps, widths, index, heads, kept):
    piece = jax.ShapeDtypeStruct((128, widths * SEG), BF16)
    count = len(steps) * (4 // widths)
    return pl.pallas_call(
        functools.partial(project_kernel, steps, widths),
        in_specs=[SMEM] + [VMEM] * 5,
        out_specs=[VMEM] * count,
        scratch_shapes=[pltpu.VMEM((128 * len(steps), 2 * HALF), BF16)],
        out_shape=[piece] * count,
        compiler_params=params(16),
        cost_estimate=pl.CostEstimate(flops=1000, bytes_accessed=1000, transcendentals=0),
        name="project",
    )(index, *heads, kept)


def add_half_kernel(on_left, piece, part, out):
    half = piece.shape[1] // 2
    with_part, without = slice(0, half), slice(half, 2 * half)
    if not on_left:
        with_part, without = without, with_part
    out[:, without] = piece[:, without]
    out[:, with_part] = (piece[:, with_part].astype(F32) + part[...].astype(F32)).astype(BF16)


def add_half(on_left, piece, part):
    return pl.pallas_call(
        functools.partial(add_half_kernel, on_left),
        in_specs=[VMEM] * 2,
        out_specs=VMEM,
        out_shape=jax.ShapeDtypeStruct(piece.shape, BF16),
        compiler_params=params(8),
        cost_estimate=pl.CostEstimate(flops=1000, bytes_accessed=1000, transcendentals=0),
        name="add_half",
    )(piece, part)


def first_sum_kernel(index_ref, i0, i1, i3, *outs):
    k = index_ref[5]
    spot = (1 - k) * index_ref[1] + k * index_ref[0]
    for m, out in enumerate(outs):
        for block in range(2):
            rows = pl.ds(pl.multiple_of(block * 64 + (spot ^ m) * 16, 16), 16)
            total = i0[rows, :].astype(F32)
            for ref in (i1, i3):
                total = total + ref[rows, :].astype(F32)
            out[block * 16:(block + 1) * 16, :] = total.astype(BF16)


def first_sum(index, pieces):
    out = jax.ShapeDtypeStruct((32, 4 * SEG), BF16)
    return pl.pallas_call(
        first_sum_kernel,
        in_specs=[SMEM] + [VMEM] * 3,
        out_specs=[VMEM] * 4,
        out_shape=[out] * 4,
        compiler_params=params(12),
        cost_estimate=pl.CostEstimate(flops=1000, bytes_accessed=1000, transcendentals=0),
        name="first_sum",
    )(index, *pieces)


def stream_kernel(index_ref, *refs):
    sums, (res, far_res, gain, place, stream_own, stream_far, send, stack) = refs[:4], refs[4:]
    spot, base = index_ref[2], index_ref[3] * 4
    for i in range(4):
        seg = spot ^ i
        cols = slice(i * SEG, (i + 1) * SEG)
        wide = pl.ds(pl.multiple_of((base + seg) * SEG, 128), SEG)
        near = pl.ds(pl.multiple_of(seg * SEG, 128), SEG)
        for block, start, stream in ((0, res[:, wide], stream_own), (1, far_res[:, near], stream_far)):
            total = start.astype(F32)
            for ref in sums:
                total = total + ref[block * 16:(block + 1) * 16, cols].astype(F32)
            stream[seg] = total.astype(stream.dtype)
            first = pl.multiple_of(seg * 32 + block * 16, 16)
            stack[pl.ds(first, 16), :] = (total * gain[:, wide]).astype(BF16)
    send[...] = jnp.dot(place[...], stack[...], preferred_element_type=F32).astype(BF16)


def make_stream(index, sums, res, far_res, gain, place):
    return pl.pallas_call(
        stream_kernel,
        in_specs=[SMEM] + [VMEM] * 8,
        out_specs=[VMEM] * 3,
        scratch_shapes=[pltpu.VMEM((128, SEG), BF16)],
        out_shape=[
            jax.ShapeDtypeStruct((4, 16, SEG), F32),
            jax.ShapeDtypeStruct((4, 16, SEG), BF16),
            jax.ShapeDtypeStruct((384, SEG), BF16),
        ],
        compiler_params=params(12),
        cost_estimate=pl.CostEstimate(flops=1000, bytes_accessed=1000, transcendentals=0),
        name="make_stream",
    )(index, *sums, res, far_res, gain, place)


def one_hot(values, count):
    return (np.asarray(values)[:, None] == np.arange(count)[None, :]).astype(np.float32)


def routing_tables():
    row, col = np.arange(384), np.arange(128)
    to_expert = one_hot(row // 24, 16)
    to_token = one_hot(col % 16, 16).T
    segment = (row // 6 % 4)[:, None] == (col // 32)[None, :]
    block = (row // 3 % 2)[:, None] == (col // 16 % 2)[None, :]
    kept = np.stack([segment & block & (col // 16 % 2 == b)[None, :] for b in range(2)])
    slot = (row % 3).astype(np.float32)[:, None]
    return_kept = (col // 16)[:, None] == (row % 8)[None, :]
    return_slot = (row // 8 % 3).astype(np.float32)[None, :]
    return [
        jnp.asarray(to_expert, BF16), jnp.asarray(to_token, BF16), jnp.asarray(kept, F32),
        jnp.asarray(slot, F32), jnp.asarray(return_kept, F32), jnp.asarray(return_slot, F32),
    ]


def routing_kernel(ids_ref, far_ref, gates_ref, to_expert, to_token, kept, slot, return_kept, return_slot,
                   place, weight):
    expert = lax.broadcasted_iota(jnp.int32, (16, 16), 0)
    token = lax.broadcasted_iota(jnp.int32, (16, 16), 1)
    earlier = (expert < token).astype(BF16)

    def spots(ids):
        named = jnp.zeros((16, 16), F32)
        for j in range(8):
            named = jnp.maximum(named, (ids[j:j + 1, :] == expert).astype(F32))
        rank = jnp.dot(named.astype(BF16), earlier, preferred_element_type=F32)
        return jnp.where(named > 0.0, rank, -1.0).astype(BF16)

    same = (expert == token).astype(BF16)
    far_ids = lax.dot_general(
        far_ref[:, 4 * SEG:4 * SEG + 128], same, (((0,), (0,)), ((), ())), preferred_element_type=F32
    )
    by_block = [spots(ids_ref[...]), spots(far_ids[:8].astype(jnp.int32))]
    total = jnp.zeros((384, 128), F32)
    for block in range(2):
        wide = jnp.dot(to_expert[...], by_block[block], preferred_element_type=F32)
        wide = jnp.dot(wide.astype(BF16), to_token[...], preferred_element_type=F32)
        total = total + jnp.where(wide == slot[...], kept[block], 0.0)
    place[...] = total.astype(BF16)

    def spread_out(value):
        tall = lax.dot_general(to_token[...], value, (((0,), (1,)), ((), ())), preferred_element_type=F32)
        return lax.dot_general(tall.astype(BF16), to_expert[...], (((1,), (1,)), ((), ())),
                               preferred_element_type=F32)

    live = jnp.where(spread_out(by_block[0]) == return_slot[...], return_kept[...], 0.0)
    route = jnp.zeros((16, 16), F32)
    for j in range(8):
        route = route + jnp.where(ids_ref[j:j + 1, :] == expert, gates_ref[j:j + 1, :], 0.0)
    for i in range(3):
        part = route.astype(BF16)
        weight[i] = (spread_out(part) * live).astype(BF16)
        route = route - part.astype(F32)


def routing(ids, letter, gates):
    tables = routing_tables()
    return pl.pallas_call(
        routing_kernel,
        in_specs=[VMEM] * 9,
        out_specs=[VMEM] * 2,
        out_shape=[jax.ShapeDtypeStruct((384, 128), BF16), jax.ShapeDtypeStruct((3, 128, 384), BF16)],
        compiler_params=params(8),
        cost_estimate=pl.CostEstimate(flops=1000, bytes_accessed=1000, transcendentals=0),
        name="routing",
    )(ids, letter, gates, *tables)


def pick_rows(order):
    matrix = np.zeros((4, 96, 384), np.float32)
    for q in range(4):
        for block in range(2):
            for e in range(16):
                for s in range(CAP):
                    matrix[q, block * 48 + e * 3 + s, e * 24 + q * 6 + order[block] * 3 + s] = 1.0
    return jnp.asarray(matrix.reshape(384, 384), BF16)


def up_part(base, pick_ref, inputs, gain_ref, gate_ref, up_ref, rows):
    squares = jnp.zeros((192, 1), F32)
    for i, refs in enumerate(inputs):
        if len(refs) == 1:
            moved = jnp.dot(pick_ref[...], refs[0][...], preferred_element_type=F32)
        else:
            moved = jnp.dot(pick_ref[:, :192], refs[0][...], preferred_element_type=F32)
            moved = moved + jnp.dot(pick_ref[:, 192:], refs[1][...], preferred_element_type=F32)
        for q in range(4):
            part = moved[q * 96:(q + 1) * 96]
            rows[i * 96:(i + 1) * 96, q * SEG:(q + 1) * SEG] = part.astype(BF16)
    for q in range(4):
        part = rows[:, q * SEG:(q + 1) * SEG].astype(F32)
        gain = gain_ref[:, pl.ds(pl.multiple_of((base * 4 + q) * SEG, 128), SEG)]
        squares = squares + jnp.sum(part * part * (1.0 / (gain * gain)), axis=1, keepdims=True)
    parts = [
        jnp.dot(rows[...], ref[core], preferred_element_type=F32)
        for ref in (gate_ref, up_ref) for core in range(2)
    ]
    return parts, squares


def load_kernel(index_ref, g0, g1, u0, u1, d0, d1, gate_near, up_near, gate_far, up_far, down, sems):
    base = index_ref[3]
    depth = 4 * SEG
    copies = []
    for outs, half in (((gate_near, up_near), base), ((gate_far, up_far), 1 - base)):
        rows = pl.ds(pl.multiple_of(half * depth, depth), depth)
        for out, refs in zip(outs, ((g0, g1), (u0, u1))):
            for core in range(2):
                copies.append((refs[core].at[rows], out.at[core]))
    copies += [(d0, down.at[0]), (d1, down.at[1])]
    copies = [pltpu.make_async_copy(a, b, sems.at[i]) for i, (a, b) in enumerate(copies)]
    for copy in copies:
        copy.start()
    for copy in copies:
        copy.wait()


def load_weights(index, gate, up, down):
    half = jax.ShapeDtypeStruct((2, 4 * SEG, 256), BF16)
    return pl.pallas_call(
        load_kernel,
        in_specs=[SMEM] + [pl.BlockSpec(memory_space=pl.ANY)] * 6,
        out_specs=[VMEM] * 5,
        scratch_shapes=[pltpu.SemaphoreType.DMA((10,))],
        out_shape=[half] * 4 + [jax.ShapeDtypeStruct((2, 256, D), BF16)],
        compiler_params=params(30),
        cost_estimate=pl.CostEstimate(flops=1000, bytes_accessed=1000, transcendentals=0),
        name="load_weights",
    )(index, *gate, *up, *down)


def expert_first_kernel(index_ref, x0, x1, pick_ref, gain_ref, gate_ref, up_ref, gate_up, squares, rows):
    parts, total = up_part(index_ref[3], pick_ref, ((x0,), (x1,)), gain_ref, gate_ref, up_ref, rows)
    for i, part in enumerate(parts):
        gate_up[:, i * 256:(i + 1) * 256] = part
    squares[...] = total


def expert_first(index, x0, x1, pick, gain, gate, up):
    return pl.pallas_call(
        expert_first_kernel,
        in_specs=[SMEM] + [VMEM] * 6,
        out_specs=[VMEM] * 2,
        scratch_shapes=[pltpu.VMEM((192, 4 * SEG), BF16)],
        out_shape=[jax.ShapeDtypeStruct((192, 1024), F32), jax.ShapeDtypeStruct((192, 1), F32)],
        compiler_params=params(16),
        cost_estimate=pl.CostEstimate(flops=1000, bytes_accessed=1000, transcendentals=0),
        name="expert_first",
    )(index, x0, x1, pick, gain, gate, up)


def expert_last_kernel(index_ref, x0, x1, x2, pick_ref, gain_ref, gate_ref, up_ref, down_ref, before, squares_before,
                       r0, r3, r1, r2_left, r2_right, rows, hidden):
    parts, total = up_part(1 - index_ref[3], pick_ref, ((x0,), (x1, x2)), gain_ref, gate_ref, up_ref, rows)
    scale = lax.rsqrt((total + squares_before[...]) * (1.0 / D) + EPSILON)
    for core in range(2):
        gate = (parts[core] + before[:, core * 256:(core + 1) * 256]) * scale
        up = (parts[2 + core] + before[:, 512 + core * 256:512 + (core + 1) * 256]) * scale
        hidden[:, core * 256:(core + 1) * 256] = (gate / (1.0 + jnp.exp(-gate)) * up).astype(BF16)
    for q in range(4):
        cols = slice(q * 2 * SEG, (q + 1) * 2 * SEG)
        out = jnp.dot(hidden[:, :256], down_ref[0, :, cols], preferred_element_type=F32)
        out = out + jnp.dot(hidden[:, 256:], down_ref[1, :, cols], preferred_element_type=F32)
        out = out.astype(BF16)
        for i, ref in enumerate((r0, r3, r1)):
            ref[:, cols] = out[i * 48:(i + 1) * 48]
        near = slice(q % 2 * 2 * SEG, (q % 2 + 1) * 2 * SEG)
        (r2_left, r2_right)[q // 2][:, near] = out[144:]


def expert_last(index, x0, x1, x2, pick, gain, gate, up, down, before, squares_before):
    return pl.pallas_call(
        expert_last_kernel,
        in_specs=[SMEM] + [VMEM] * 10,
        out_specs=[VMEM] * 5,
        scratch_shapes=[pltpu.VMEM((192, 4 * SEG), BF16), pltpu.VMEM((192, 512), BF16)],
        out_shape=[jax.ShapeDtypeStruct((48, D), BF16)] * 3
        + [jax.ShapeDtypeStruct((48, D // 2), BF16)] * 2,
        compiler_params=params(16),
        cost_estimate=pl.CostEstimate(flops=1000, bytes_accessed=1000, transcendentals=0),
        name="expert_last",
    )(index, x0, x1, x2, pick, gain, gate, up, down, before, squares_before)


def spread_kernel(p0, p1, p3, out):
    total = p0[...].astype(F32)
    for ref in (p1, p3):
        total = total + ref[...].astype(F32)
    total = total.astype(BF16)
    stack = jnp.concatenate([total[:, q * SEG:(q + 1) * SEG] for q in range(8)], axis=0)
    row = lax.broadcasted_iota(jnp.int32, (384, 384), 0)
    col = lax.broadcasted_iota(jnp.int32, (384, 384), 1)
    move = (row == (col % 48) * 8 + col // 48).astype(BF16)
    out[...] = jnp.dot(move, stack, preferred_element_type=F32).astype(BF16)


def spread(parts):
    return pl.pallas_call(
        spread_kernel,
        out_shape=jax.ShapeDtypeStruct((384, SEG), BF16),
        compiler_params=params(24),
        cost_estimate=pl.CostEstimate(flops=1000, bytes_accessed=1000, transcendentals=0),
        name="spread",
    )(*parts)


def combine_kernel(index_ref, rows, weight, stream_own, stream_far, out, routed):
    total = jnp.dot(weight[0], rows[...], preferred_element_type=F32)
    for i in (1, 2):
        total = total + jnp.dot(weight[i], rows[...], preferred_element_type=F32)
    routed[...] = total
    pair = index_ref[3]
    for q in range(4):
        for side, stream in ((pair, stream_own), (1 - pair, stream_far)):
            seg = side * 4 + q
            picked = routed[pl.ds(pl.multiple_of(seg * 16, 16), 16), :]
            out[:, pl.ds(pl.multiple_of(seg * SEG, 128), SEG)] = (picked + stream[q].astype(F32)).astype(BF16)


def combine(index, rows, weight, stream_own, stream_far):
    return pl.pallas_call(
        combine_kernel,
        in_specs=[SMEM] + [VMEM] * 4,
        out_specs=VMEM,
        scratch_shapes=[pltpu.VMEM((128, SEG), F32)],
        out_shape=jax.ShapeDtypeStruct((16, D), BF16),
        compiler_params=params(12),
        cost_estimate=pl.CostEstimate(flops=1000, bytes_accessed=1000, transcendentals=0),
        name="combine",
    )(index, rows, weight, stream_own, stream_far)


def per_device(residual, queries, latent, key_rope, doc_ids, kv_weight, out_weight, norm_gain,
               expert_ids, expert_gates, w_gate, w_up, w_down):
    c = lax.axis_index("ctx")
    e = lax.axis_index("exp")
    y, k, x, z = c >> 1, c & 1, e >> 2, e & 3
    pair = y >> 1
    index = jnp.stack([x, z, c & 3, pair, y, k]).astype(jnp.int32)

    far_start = (1 - pair) * (4 * SEG)

    lat = jnp.concatenate(
        [latent, key_rope, jnp.zeros((BLK, LAT_WIDTH - LATENT - ROPE), BF16)], axis=1
    )
    lat = jnp.concatenate([lat] + [swap_ctx(lat, 2 * m) for m in (1, 2, 3)], axis=0)
    out_top, out_low = out_weight[:HALF], out_weight[HALF:]
    lat, out_top, out_low, out_weight, doc_ids, w_gate, w_up, w_down, index = lax.optimization_barrier(
        (lat, out_top, out_low, out_weight, doc_ids, w_gate[0], w_up[0], w_down[0], index)
    )
    next_top = swap_ctx(out_top, 2)
    gate, up = ((v, swap_ctx(v, 1)) for v in (w_gate, w_up))
    near = lax.all_to_all(
        jnp.broadcast_to(lat[None], (16,) + lat.shape), "exp", split_axis=0, concat_axis=0, tiled=True
    ).reshape(16 * lat.shape[0], LAT_WIDTH)
    near, next_top, out_weight, doc_ids, gate, up = lax.optimization_barrier(
        (near, next_top, out_weight, doc_ids, gate, up)
    )
    far = swap_ctx(near, 1)
    bias = make_mask(index, doc_ids.reshape(1, KEYS))
    next_low = swap_ctx(out_low, 2)
    out_core = swap_ctx(out_weight, 1)
    near, far, bias, w_down = lax.optimization_barrier((near, far, bias, w_down))
    down = (w_down, swap_ctx(w_down, 1))

    heads_0 = attention(0, queries, near, far, kv_weight, bias)
    near, far, heads_0, out_core = lax.optimization_barrier((near, far, heads_0, out_core))
    far_heads_0 = swap_ctx(heads_0, 6)
    both_top = swap_ctx(next_top, 1)
    heads_1 = attention(1, queries, near, far, kv_weight, bias)
    far_heads_1 = swap_ctx(heads_1, 6)
    both_top, next_low, far_heads_0, residual, expert_ids, down, _ = lax.optimization_barrier(
        (both_top, next_low, far_heads_0, residual, expert_ids, down, heads_1)
    )
    both_low = swap_ctx(next_low, 1)

    ids = jnp.concatenate([expert_ids.astype(BF16), jnp.zeros((BLK, 120), BF16)], axis=1)
    part = lax.dynamic_slice_in_dim(residual, far_start, 4 * SEG, 1)
    letter = swap_ctx(jnp.concatenate([part, ids], axis=1), 6)

    kept = load_out((out_weight, out_core, next_top, next_low, both_top, both_low))
    far_heads_0, far_heads_1, kept = lax.optimization_barrier((far_heads_0, far_heads_1, kept))
    heads = (heads_0, heads_1, far_heads_0, far_heads_1)
    left, right = project((2,), 2, index, heads, kept)
    from_1, from_3 = swap_plane(left, 1, True), swap_plane(right, 3, True)
    kept, _ = lax.optimization_barrier((kept, left))
    p0, p1, p3 = project((0, 1, 3), 4, index, heads, kept)
    p3, p1 = add_half(True, p3, from_1), add_half(False, p1, from_3)
    letter, _ = lax.optimization_barrier((letter, p1))
    place, weight = routing(expert_ids.T, letter, expert_gates.T)
    pieces = [p0, swap_plane(p1, 1, True), swap_plane(p3, 3, True)]
    pieces, place, weight = lax.optimization_barrier((pieces, place, weight))
    sums = first_sum(index, pieces)
    sums = [sums[0]] + [swap_plane(sums[m], m, False) for m in (1, 2, 3)]
    gain = norm_gain.reshape(1, D)
    stream_own, stream_far, send = make_stream(index, sums, residual, letter, gain, place)

    got = lax.all_to_all(send.reshape(16, 24, SEG), "exp", split_axis=0, concat_axis=0, tiled=True)
    got, stream_far, gate, up, down = lax.optimization_barrier(
        (got.reshape(384, SEG), stream_far, gate, up, down)
    )
    got_1, got_3 = swap_ctx(got, 2), swap_ctx(got, 6)
    loaded = load_weights(index, gate, up, down)
    got_1, _ = lax.optimization_barrier((got_1, loaded[0]))
    got_3, stream_far, _ = lax.optimization_barrier((got_3, stream_far, loaded[0]))
    got_2_top, got_2_low = swap_ctx(got_1[:192], 6), swap_ctx(got_3[192:], 2)
    stream_far = swap_ctx(stream_far, 6)
    gate_near, up_near, gate_far, up_far, down = loaded
    gate_up, squares = expert_first(index, got, got_1, pick_rows((0, 1)), gain, gate_near, up_near)
    r0, r3, r1, r2_left, r2_right = expert_last(
        index, got_3, got_2_top, got_2_low, pick_rows((1, 0)), gain, gate_far, up_far, down, gate_up, squares
    )
    r3, r1 = add_half(True, r3, swap_ctx(r2_left, 2)), add_half(False, r1, swap_ctx(r2_right, 6))
    back = spread([r0, swap_ctx(r1, 2), swap_ctx(r3, 6)])
    back, stream_far = lax.optimization_barrier((back, stream_far))
    rows = lax.all_to_all(back.reshape(16, 24, SEG), "exp", split_axis=0, concat_axis=0, tiled=True)
    return combine(index, rows.reshape(384, SEG), weight, stream_own, stream_far)


def solution(mesh):
    placed = (
        P(("ctx", "exp"), None),
        P("ctx", "exp"),
        P(("ctx", "exp"), None),
        P(("ctx", "exp"), None),
        P(),
        P(None, "exp"),
        P("exp", "ctx"),
        P(),
        P(("ctx", "exp"), None),
        P(("ctx", "exp"), None),
        P("exp", None, "ctx"),
        P("exp", None, "ctx"),
        P("exp", "ctx", None),
    )
    return jax.shard_map(
        per_device, mesh=mesh, in_specs=placed, out_specs=P(("ctx", "exp"), None), check_vma=False
    )
```
